128 devices in a mesh: ctx: 16 (over z_lo, y, core), fsdp: 8 (over x, z_hi).
Axes of the slice: x: 4, y: 4, z: 4 (z_hi: 2, z_lo: 2; z = z_hi * 2 + z_lo), core: 2. Of those that a mesh axis runs over, the one named last changes fastest.
Arguments:
- tokens_in: bfloat16 [8, 16, 2, 64, 1024], P('fsdp', 'ctx'), may hold values from -6 to 6
- positions: int32 [8, 2048], P('fsdp'), may hold values from 0 to 6141, as said below
- block_pairs: int32 [16, 2], replicated, may hold values from 0 to 31, as said below
- first_gain: float32 [1024], replicated, may hold values from 0.5 to 1.5
- first_bias: float32 [1024], replicated, may hold values from -1.25 to 1.25
- second_gain: float32 [1024], replicated, may hold values from 0.5 to 1.5
- second_bias: float32 [1024], replicated, may hold values from -1.25 to 1.25
- triple_weight: bfloat16 [1024, 3072], P('fsdp'), may hold values from -0.1875 to 0.1875
- triple_bias: float32 [3072], replicated, may hold values from -1.25 to 1.25
- output_weight: bfloat16 [1024, 1024], P(None, 'fsdp'), may hold values from -0.75 to 0.75
- output_bias: float32 [1024], replicated, may hold values from -1.25 to 1.25
- expand_weight: bfloat16 [1024, 4096], P('fsdp'), may hold values from -0.1875 to 0.1875
- expand_bias: float32 [4096], replicated, may hold values from -1.25 to 1.25
- shrink_weight: bfloat16 [4096, 1024], P(None, 'fsdp'), may hold values from -0.09375 to 0.09375
- shrink_bias: float32 [1024], replicated, may hold values from -1.25 to 1.25
- cotangent: bfloat16 [8, 16, 2, 64, 1024], P('fsdp', 'ctx'), may hold values from -6 to 6
Outputs:
- activations: bfloat16 [8, 16, 2, 64, 1024], P('fsdp', 'ctx')
- grad_tokens: float32 [8, 16, 2, 64, 1024], P('fsdp', 'ctx')
- grad_first_gain: float32 [1024], P(('ctx', 'fsdp'))
- grad_first_bias: float32 [1024], P(('ctx', 'fsdp'))
- grad_second_gain: float32 [1024], P(('ctx', 'fsdp'))
- grad_second_bias: float32 [1024], P(('ctx', 'fsdp'))
- grad_triple_weight: float32 [1024, 3072], P(('ctx', 'fsdp'))
- grad_triple_bias: float32 [2048], P(('ctx', 'fsdp'))
- grad_value_bias: float32 [1024], P(('ctx', 'fsdp'))
- grad_output_weight: float32 [1024, 1024], P(('ctx', 'fsdp'))
- grad_output_bias: float32 [1024], P(('ctx', 'fsdp'))
- grad_expand_weight: float32 [1024, 4096], P(('ctx', 'fsdp'))
- grad_expand_bias: float32 [4096], P(('ctx', 'fsdp'))
- grad_shrink_weight: float32 [4096, 1024], P(('ctx', 'fsdp'))
- grad_shrink_bias: float32 [1024], P(('ctx', 'fsdp'))
The draws below stay inside these ranges and needn't reach their ends.
Inputs may be any that keep to these rules, and one draw needn't show every extreme that they name: `block_pairs`: row c holds a block p below 16 and its mirror 2 * 16 - 1 - p; every block of a sequence is named once. In each sequence's token order positions begin at 0 and rise by 1 to 3 from one token to the next, except that the last token of every sequence stands at 6141.
All inputs are finite; a program needn't handle non-finite values.
Results may differ from the reference program's by a relative error of at most 0.011.
Values may be sent and summed in bfloat16 or wider, within the bound.
A program may use at most 256 MiB of HBM per device.

```python
import math
import jax
import jax.numpy as jnp
from jax import lax

D = 1024
FF = 4096
HEADS = 16
BLK = 64
SEQ = 2048
SEQS = 8
N_CTX = 16


def draw_block_pairs(key, part):
    key = jax.random.fold_in(key, 11)
    lower = jax.random.permutation(key, N_CTX).astype(jnp.int32)
    return jnp.stack([lower, 2 * N_CTX - 1 - lower], axis=1).astype(jnp.int32)


def draw_positions(key, part):
    key = jax.random.fold_in(key, 12)
    strides = jax.random.randint(key, (SEQS, SEQ), 1, 4, dtype=jnp.int32)
    index = jnp.arange(SEQ, dtype=jnp.int32)[None, :]
    rising = jnp.cumsum(jnp.where(index == 0, 0, strides), axis=1).astype(jnp.int32)
    return jnp.where(index == SEQ - 1, 3 * SEQ - 3, rising).astype(jnp.int32)


def shard_levels(own_key, dims, split, least, largest):
    def one(position, blocks):
        draws = jax.random.uniform(jax.random.fold_in(jax.random.fold_in(own_key, 6), position), (blocks,), jnp.float32, least / len(split), largest / len(split))
        return jnp.repeat(jnp.exp(draws), dims[position] // blocks).reshape((-1,) + (1,) * (len(dims) - position - 1))

    level = one(*split[0])
    for cut in split[1:]:
        level = level * one(*cut)
    return level


def bell_draw(rng, dims, spread, bound, pieces=(), kind=jnp.bfloat16):
    factor_of = shard_levels(rng, dims, pieces, -0.22, 0.18) if pieces else 1.0
    values = jax.random.normal(rng, dims, jnp.float32) * spread * factor_of
    return jnp.minimum(jnp.maximum(values, -bound), bound).astype(kind)


def setup_inputs(seed: int = 0) -> dict:
    arg_keys = jax.random.split(jax.random.key(seed), 17)
    return {
        "tokens_in": bell_draw(arg_keys[0], (SEQS, N_CTX, 2, BLK, D), 1.0, 6.0, ((0, 8), (1, 16))),
        "positions": draw_positions(jax.random.fold_in(arg_keys[16], 71), 0),
        "block_pairs": draw_block_pairs(jax.random.fold_in(arg_keys[16], 71), 0),
        "first_gain": jnp.clip(1.0 + 0.1 * jax.random.normal(arg_keys[3], (D,), jnp.float32), 0.5, 1.5),
        "first_bias": bell_draw(arg_keys[4], (D,), 0.2, 1.25, (), jnp.float32),
        "second_gain": jnp.clip(1.0 + 0.1 * jax.random.normal(arg_keys[5], (D,), jnp.float32), 0.5, 1.5),
        "second_bias": bell_draw(arg_keys[6], (D,), 0.2, 1.25, (), jnp.float32),
        "triple_weight": bell_draw(arg_keys[7], (D, 3 * D), D ** -0.5, 0.1875, ((0, 8),)),
        "triple_bias": bell_draw(arg_keys[8], (3 * D,), 0.2, 1.25, (), jnp.float32),
        "output_weight": bell_draw(arg_keys[9], (D, D), (D // 16) ** -0.5, 0.75, ((1, 8),)),
        "output_bias": bell_draw(arg_keys[10], (D,), 0.2, 1.25, (), jnp.float32),
        "expand_weight": bell_draw(arg_keys[11], (D, FF), D ** -0.5, 0.1875, ((0, 8),)),
        "expand_bias": bell_draw(arg_keys[12], (FF,), 0.2, 1.25, (), jnp.float32),
        "shrink_weight": bell_draw(arg_keys[13], (FF, D), FF ** -0.5, 0.09375, ((1, 8),)),
        "shrink_bias": bell_draw(arg_keys[14], (D,), 0.2, 1.25, (), jnp.float32),
        "cotangent": bell_draw(arg_keys[15], (SEQS, N_CTX, 2, BLK, D), 1.0, 6.0, ((0, 8), (1, 16))),
    }


@jax.custom_vjp
def low(v):
    return lax.optimization_barrier(v.astype(jnp.bfloat16)).astype(jnp.float32)

@jax.custom_vjp
def low_back(v):
    return v

def low_keep(v):
    return (low(v), None)

def low_pass(kept, grad):
    return (grad,)

def back_keep(v):
    return (v, None)

def back_low(kept, grad):
    return (low(grad),)
low.defvjp(low_keep, low_pass)
low_back.defvjp(back_keep, back_low)
eps_norm = 1e-05
rotary_base = 10000.0
highest = lax.Precision.HIGHEST

def rotate(values, angles, rot_width):
    half = rot_width // 2
    first = values[..., :half]
    second = values[..., half:rot_width]
    cosine = jnp.cos(angles)
    sine = jnp.sin(angles)
    return jnp.concatenate([first * cosine - second * sine, second * cosine + first * sine, values[..., rot_width:]], axis=-1)

def frequency(rot_width):
    return 1.0 / rotary_base ** (jnp.arange(0, rot_width, 2, dtype=jnp.float32) / rot_width)

def block_forward(seq_x, seq_pos, params):
    first_gain, first_bias, second_gain, second_bias, triple_weight, triple_bias, output_weight, output_bias, expand_weight, expand_bias, shrink_weight, shrink_bias = params
    length = seq_x.shape[0]
    width = seq_x.shape[1]
    head_dim = width // HEADS
    rot_width = head_dim // 4
    scale = 1.0 / math.sqrt(head_dim)
    row_mean = lax.optimization_barrier(jnp.mean(seq_x, axis=1, keepdims=True))
    centred = seq_x - row_mean
    inv_std = lax.rsqrt(lax.optimization_barrier(jnp.mean(centred * centred, axis=1, keepdims=True)) + eps_norm)
    x_hat = centred * inv_std
    first_low = low(x_hat * first_gain + first_bias)
    second_low = low(x_hat * second_gain + second_bias)
    triple = low_back(jnp.dot(first_low, triple_weight, precision=highest) + triple_bias)
    expand = low_back(jnp.dot(second_low, expand_weight, precision=highest) + expand_bias)
    hidden_low = low(jax.nn.gelu(expand, approximate=False))
    parts = triple.reshape(length, 3, HEADS, head_dim)
    angles = (seq_pos.astype(jnp.float32)[:, None] * frequency(rot_width))[:, None, :]
    query_low = low(rotate(parts[:, 0], angles, rot_width))
    key_low = low(rotate(parts[:, 1], angles, rot_width))
    value_low = low(parts[:, 2])
    token_index = jnp.arange(length, dtype=jnp.int32)
    rows_blk = math.gcd(512, length)
    starts = jnp.arange(0, length, rows_blk, dtype=jnp.int32)

    @jax.checkpoint
    def attend_rows(start):
        query_blk = lax.dynamic_slice_in_dim(query_low, start, rows_blk, 0)
        raw = jnp.einsum('qhd,khd->hqk', query_blk, key_low, precision=highest)
        scores = low_back(raw * scale)
        query_index = start + jnp.arange(rows_blk, dtype=jnp.int32)
        allowed = token_index[None, :] <= query_index[:, None]
        scores = jnp.where(allowed[None], scores, -jnp.inf)
        probs = jax.nn.softmax(scores, axis=2)
        return jnp.einsum('hqk,khd->qhd', low(probs), value_low, precision=highest)
    mixed = lax.map(attend_rows, starts).reshape(length, width)
    attn_low = low(low_back(mixed))
    branch = jnp.dot(attn_low, output_weight, precision=highest) + output_bias + jnp.dot(hidden_low, shrink_weight, precision=highest) + shrink_bias
    return seq_x + branch

def reference(tokens_in, positions, block_pairs, first_gain, first_bias, second_gain, second_bias, triple_weight, triple_bias, output_weight, output_bias, expand_weight, expand_bias, shrink_weight, shrink_bias, cotangent):
    seqs = tokens_in.shape[0]
    width = tokens_in.shape[-1]
    length = positions.shape[1]
    order = (block_pairs[:, :, None] * BLK + jnp.arange(BLK, dtype=jnp.int32)[None, None, :]).reshape(length).astype(jnp.int32)

    def undeal(arr):
        flat = arr.reshape(seqs, length, width).astype(jnp.float32)
        return jnp.zeros((seqs, length, width), jnp.float32).at[:, order].set(flat)
    x_all = undeal(tokens_in)
    dy_all = undeal(cotangent)
    params = tuple((p.astype(jnp.float32) for p in (first_gain, first_bias, second_gain, second_bias, triple_weight, triple_bias, output_weight, output_bias, expand_weight, expand_bias, shrink_weight, shrink_bias)))

    def one_sequence(carry, inputs):
        seq_x, seq_pos, seq_dy = inputs
        outputs, pullback = jax.vjp(lambda xin, prm: block_forward(xin, seq_pos, prm), seq_x, params)
        grad_x, grad_params = pullback(seq_dy)
        carry = jax.tree.map(lambda left, right: left + right, carry, grad_params)
        return (carry, (outputs, grad_x))
    zeros = jax.tree.map(jnp.zeros_like, params)
    sums, (outs, grads) = lax.scan(one_sequence, zeros, (x_all, positions, dy_all))
    activations = outs[:, order].reshape(tokens_in.shape).astype(jnp.bfloat16)
    grad_tokens = grads[:, order].reshape(tokens_in.shape).astype(jnp.float32)
    sums = tuple((s.astype(jnp.float32) for s in sums))
    return (activations, grad_tokens, sums[0], sums[1], sums[2], sums[3], sums[4], sums[5][:2 * width], sums[5][2 * width:], sums[6], sums[7], sums[8], sums[9], sums[10], sums[11])
```

```python
import math

import jax
import jax.numpy as jnp
from jax import lax
from jax.experimental import pallas as pl
from jax.experimental.pallas import tpu as pltpu
from jax.sharding import PartitionSpec as P

MESH = pl.DeviceIdType.MESH
BF, F32 = jnp.bfloat16, jnp.float32
EPS = 1e-05
BASE = 10000.0
MIB = 1 << 20
SCALE = 0.125

ZL, KC, ZH = (1, 0, 0, 0, 0), (0, 0, 1, 0, 0), (0, 0, 0, 0, 1)
YS = {i: (0, i, 0, 0, 0) for i in (1, 2, 3)}
XS = {i: (0, 0, 0, i, 0) for i in (1, 2, 3)}
ZYS = {i: (1, i, 0, 0, 0) for i in (1, 2, 3)}
NEAR_FIRST = (1, 3, 2)


def coords():
    c, f = lax.axis_index("ctx"), lax.axis_index("fsdp")
    return lax.div(c, 8), lax.rem(lax.div(c, 2), 4), lax.rem(c, 2), lax.div(f, 2), lax.rem(f, 2)


def device_at(me, off):
    a, b, k, x, h = (lax.rem(p + o, n) for p, o, n in zip(me, off, (2, 4, 2, 4, 2)))
    return ((a * 4 + b) * 2 + k, x * 2 + h)


def barrier(me, offs):
    sem = pltpu.get_barrier_semaphore()
    for off in offs:
        pl.semaphore_signal(sem, inc=1, device_id=device_at(me, off), device_id_type=MESH)
    pl.semaphore_wait(sem, len(offs))


class Sender:
    def __init__(self, me, send_sems, recv_sems):
        self.me, self.send_sems, self.recv_sems, self.copies = me, send_sems, recv_sems, []

    def __call__(self, src, dst, off):
        i = len(self.copies)
        copy = pltpu.make_async_remote_copy(
            src_ref=src,
            dst_ref=dst,
            send_sem=self.send_sems.at[i],
            recv_sem=self.recv_sems.at[i],
            device_id=device_at(self.me, off),
            device_id_type=MESH,
        )
        copy.start()
        self.copies.append(copy)
        return copy

    def finish(self):
        for copy in self.copies:
            copy.wait_send()


def nt(left, right):
    return lax.dot_general(left, right, (((1,), (1,)), ((), ())), preferred_element_type=F32)


def tn(left, right):
    return lax.dot_general(left, right, (((0,), (0,)), ((), ())), preferred_element_type=F32)


def nn(left, right):
    return jnp.dot(left, right, preferred_element_type=F32)


ANY = pl.BlockSpec(memory_space=pl.ANY)
VM = pl.BlockSpec(memory_space=pltpu.VMEM)


GATHER_COPIES = 2 * (1 + 3 + 3 + 0) + 2 * (1 + 3 + 3 + 8)


def gather_kernel(x, g, wa, wb, xo, go, wao, wbo, ss, rs, ls):
    me = coords()
    a, b, k, xx, h = me
    t, f = a * 4 + b, xx * 2 + h
    barrier(me, [ZL, *YS.values(), *XS.values(), ZH, KC])
    send = Sender(me, ss, rs)

    def wa_at(ff):
        return wao.at[pl.ds(pl.multiple_of(ff * 128 + k * 64, 64), 64)]

    def wb_at(ff):
        return wbo.at[
            pl.ds(pl.multiple_of(k * 320, 64), 320), pl.ds(pl.multiple_of(ff * 128, 128), 128)
        ]

    own_wa = wa.at[pl.ds(pl.multiple_of(k * 64, 64), 64)]
    own_wb = wb.at[pl.ds(pl.multiple_of(k * 320, 64), 320)]
    gz = send(g, go.at[t], ZL)
    wz = (send(own_wa, wa_at(f), ZH), send(own_wb, wb_at(f), ZH))
    gy = [send(g, go.at[t], YS[i]) for i in NEAR_FIRST]
    wx = [
        (send(own_wa, wa_at(f), XS[i]), send(own_wb, wb_at(f), XS[i])) for i in NEAR_FIRST
    ]
    xy = [send(x, xo.at[t], YS[i]) for i in NEAR_FIRST]
    rest = list(gy)
    rest.append(send(x, xo.at[t], ZL))
    rest += [send(own_wa, wa_at(f), KC), send(own_wb, wb_at(f), KC)]
    local = [
        pltpu.make_async_copy(src, dst, ls.at[i])
        for i, (src, dst) in enumerate(
            ((x, xo.at[t]), (g, go.at[t]), (own_wa, wa_at(f)), (own_wb, wb_at(f)))
        )
    ]
    for copy in local:
        copy.start()
    tz = (1 - a) * 4 + b
    gz.wait_recv()
    rest += [send(go.at[tz], go.at[tz], YS[i]) for i in NEAR_FIRST]
    fz = xx * 2 + (1 - h)
    for copy in wz:
        copy.wait_recv()
    wxz = [
        (send(wa_at(fz), wa_at(fz), XS[i]), send(wb_at(fz), wb_at(fz), XS[i]))
        for i in NEAR_FIRST
    ]
    rest += [send(wa_at(fz), wa_at(fz), KC), send(wb_at(fz), wb_at(fz), KC)]
    for j, i in enumerate(NEAR_FIRST):
        xy[j].wait_recv()
        ts = a * 4 + lax.rem(b + 4 - i, 4)
        rest.append(send(xo.at[ts], xo.at[ts], ZL))
        for copy in wx[j]:
            copy.wait_recv()
        fs = lax.rem(xx + 4 - i, 4) * 2 + h
        rest += [send(wa_at(fs), wa_at(fs), KC), send(wb_at(fs), wb_at(fs), KC)]
    for j, i in enumerate(NEAR_FIRST):
        for copy in wxz[j]:
            copy.wait_recv()
        fs = lax.rem(xx + 4 - i, 4) * 2 + (1 - h)
        rest += [send(wa_at(fs), wa_at(fs), KC), send(wb_at(fs), wb_at(fs), KC)]
    for copy in rest:
        copy.wait_recv()
    send.finish()
    for copy in local:
        copy.wait()


def gather(x, g, wa, wb):
    return pl.pallas_call(
        gather_kernel,
        out_shape=(
            jax.ShapeDtypeStruct((8, 128, 1024), BF),
            jax.ShapeDtypeStruct((8, 128, 1024), BF),
            jax.ShapeDtypeStruct((1024, 896), BF),
            jax.ShapeDtypeStruct((640, 1024), BF),
        ),
        in_specs=[ANY] * 4,
        out_specs=(ANY,) * 4,
        scratch_shapes=[
            pltpu.SemaphoreType.DMA((GATHER_COPIES,)),
            pltpu.SemaphoreType.DMA((GATHER_COPIES,)),
            pltpu.SemaphoreType.DMA((4,)),
        ],
        compiler_params=pltpu.CompilerParams(collective_id=0, has_side_effects=True),
        name="gather",
    )(x, g, wa, wb)


def normalised(x):
    mean = jnp.mean(x, axis=1, keepdims=True)
    centred = x - mean
    inv = lax.rsqrt(jnp.mean(centred * centred, axis=1, keepdims=True) + EPS)
    return centred * inv, inv


def lanes(shape):
    return lax.broadcasted_iota(jnp.int32, shape, 1)


def left_half(shape):
    return lanes(shape) < 64


def roll(v, shift):
    return pltpu.roll(v, shift, 1)


def tokens_kernel(
    x, g, wa, wb, tb, eb, g1, b1, g2, b2, cs, first, second, pack, hidden, dexp, ge, gs
):
    step = pl.program_id(0)
    n = 256
    x_hat, _ = normalised(x[...].reshape(n, 1024).astype(F32))
    first_low = (x_hat * g1[...] + b1[...]).astype(BF)
    second_low = (x_hat * g2[...] + b2[...]).astype(BF)
    first[...] = first_low
    second[...] = second_low
    grad = g[...].reshape(n, 1024)
    cos, sin = cs[0:8, :], cs[8:16, :]
    one, zero = jnp.ones((48, n), F32), jnp.zeros((48, n), F32)
    tc = jnp.concatenate([cos, cos, one, cos, cos, one], axis=0).T
    ts = jnp.concatenate([-sin, sin, zero, -sin, sin, zero], axis=0).T
    early = (lanes((n, 128)) & 63) < 8

    def turn(v):
        return v * tc + jnp.where(early, roll(v, 120), roll(v, 8)) * ts

    triple = nn(first_low, wa[:, 0:384]) + tb[...]
    query, key, value = turn(triple[:, 0:128]), turn(triple[:, 128:256]), triple[:, 256:384]
    dmix = nt(grad, wb[0:128, :])
    low = left_half((n, 128))
    pack[0, :, 0:128] = jnp.where(low, query, roll(key, 64)).astype(BF)
    pack[0, :, 128:256] = jnp.where(low, value, roll(dmix, 64)).astype(BF)
    pack[1, :, 0:128] = jnp.where(low, roll(query, 64), key).astype(BF)
    pack[1, :, 128:256] = jnp.where(low, roll(value, 64), dmix).astype(BF)
    u = nn(second_low, wa[:, 384:896]) + eb[...]
    cdf = 0.5 * (1.0 + lax.erf(u * math.sqrt(0.5)))
    pdf = jnp.exp(-0.5 * u * u) * (1.0 / math.sqrt(2.0 * math.pi))
    hidden_low = (u * cdf).astype(BF)
    hidden[...] = hidden_low
    dexp_low = (nt(grad, wb[128:640, :]) * (cdf + u * pdf)).astype(BF)
    dexp[...] = dexp_low

    @pl.when(step == 0)
    def _():
        ge[...] = jnp.zeros_like(ge)
        gs[...] = jnp.zeros_like(gs)

    ge[...] += tn(second_low, dexp_low)
    gs[...] += tn(hidden_low, grad)


def tokens_part(x, g, wa, wb, tb, eb, g1, b1, g2, b2, cs):
    def whole(*shape):
        return pl.BlockSpec(shape, lambda i: (0,) * len(shape))

    return pl.pallas_call(
        tokens_kernel,
        grid=(4,),
        out_shape=(
            jax.ShapeDtypeStruct((1024, 1024), BF),
            jax.ShapeDtypeStruct((1024, 1024), BF),
            jax.ShapeDtypeStruct((2, 1024, 256), BF),
            jax.ShapeDtypeStruct((1024, 512), BF),
            jax.ShapeDtypeStruct((1024, 512), BF),
            jax.ShapeDtypeStruct((1024, 512), F32),
            jax.ShapeDtypeStruct((512, 1024), F32),
        ),
        in_specs=[
            pl.BlockSpec((2, 128, 1024), lambda i: (i, 0, 0)),
            pl.BlockSpec((2, 128, 1024), lambda i: (i, 0, 0)),
            whole(1024, 896),
            whole(640, 1024),
            whole(1, 384),
            whole(1, 512),
            whole(1, 1024),
            whole(1, 1024),
            whole(1, 1024),
            whole(1, 1024),
            pl.BlockSpec((16, 256), lambda i: (0, i)),
        ],
        out_specs=(
            pl.BlockSpec((256, 1024), lambda i: (i, 0)),
            pl.BlockSpec((256, 1024), lambda i: (i, 0)),
            pl.BlockSpec((2, 256, 256), lambda i: (0, i, 0)),
            pl.BlockSpec((256, 512), lambda i: (i, 0)),
            pl.BlockSpec((256, 512), lambda i: (i, 0)),
            whole(1024, 512),
            whole(512, 1024),
        ),
        compiler_params=pltpu.CompilerParams(
            dimension_semantics=("arbitrary",), vmem_limit_bytes=56 * MIB
        ),
        name="tokens_part",
    )(x, g, wa, wb, tb, eb, g1, b1, g2, b2, cs)


def swap(src, name, ident):
    def kernel(src, dst, ss, rs, ls):
        me = coords()
        k = me[2]
        keep = pltpu.make_async_copy(src.at[k], dst.at[k], ls.at[0])
        keep.start()
        barrier(me, [KC])
        send = Sender(me, ss, rs)
        away = send(src.at[1 - k], dst.at[k], KC)
        away.wait_recv()
        send.finish()
        keep.wait()

    return pl.pallas_call(
        kernel,
        out_shape=jax.ShapeDtypeStruct(src.shape, src.dtype),
        in_specs=[ANY],
        out_specs=ANY,
        scratch_shapes=[pltpu.SemaphoreType.DMA((1,))] * 3,
        compiler_params=pltpu.CompilerParams(collective_id=ident, has_side_effects=True),
        name=name,
    )(src)


TILE = 256


def attention_kernel(
    order, pack, cs, out, t0, t1, t0r, t1r, qz, dz, t0t, t1t, sc, acc, left, right
):
    def place(n, _):
        at = pl.ds(pl.multiple_of(order[n] * 64, 64), 64)
        v0, v1 = pack[n, :, 0:128].astype(F32), pack[n, :, 128:256].astype(F32)
        low = left_half((64, 128))
        v0 = jnp.where(low, v0 * SCALE, v0)
        t0[at, :] = v0.astype(BF)
        t1[at, :] = v1.astype(BF)
        t0r[at, :] = roll(v0, 64).astype(BF)
        t1r[at, :] = roll(v1, 64).astype(BF)
        qz[at, :] = jnp.where(low, v0, 0.0).astype(BF)
        dz[at, :] = jnp.where(low, 0.0, v1).astype(BF)
        return 0

    lax.fori_loop(0, 32, place, 0)
    acc[...] = jnp.zeros_like(acc)
    for i in range(8):
        rows = pl.ds(i * TILE, TILE)
        t0t[:, rows] = t0[rows, :].astype(F32).T.astype(BF)
        t1t[:, rows] = t1[rows, :].astype(F32).T.astype(BF)

    key_row = lax.broadcasted_iota(jnp.int32, (TILE, TILE), 0)
    query_col = lax.broadcasted_iota(jnp.int32, (TILE, TILE), 1)
    seen = key_row <= query_col
    low = left_half((TILE, 128))

    def folded(v, op):
        parts = [v[j * 8 : j * 8 + 8] for j in range(TILE // 8)]
        while len(parts) > 1:
            parts = [op(parts[j], parts[j + 1]) for j in range(0, len(parts), 2)]
        return parts[0]

    for i in range(8):
        cols = pl.ds(i * TILE, TILE)
        q_i, d_i = qz[cols, :], dz[cols, :]

        def scores(j, peak):
            rows = pl.ds(pl.multiple_of(j * TILE, TILE), TILE)
            s = nt(t0r[rows, :], q_i)
            sc[rows, :] = s
            return jnp.maximum(peak, folded(s, jnp.maximum))

        s = jnp.where(seen, nt(t0r[cols, :], q_i), -jnp.inf)
        sc[cols, :] = s
        peak = lax.fori_loop(0, i, scores, folded(s, jnp.maximum))
        peak = jnp.max(peak, axis=0, keepdims=True)

        def weigh(j, carry):
            total, mix = carry
            rows = pl.ds(pl.multiple_of(j * TILE, TILE), TILE)
            e = jnp.exp(sc[rows, :] - peak)
            sc[rows, :] = e
            return total + folded(e, jnp.add), mix + nn(t1t[:, rows], e.astype(BF))

        total, mix = lax.fori_loop(
            0, i + 1, weigh, (jnp.zeros((8, TILE), F32), jnp.zeros((128, TILE), F32))
        )
        inv = 1.0 / jnp.sum(total, axis=0, keepdims=True)
        mix = mix[0:64] * inv
        inner = jnp.sum(mix * t1t[64:128, cols].astype(F32), axis=0, keepdims=True)

        def back(j, dq):
            rows = pl.ds(pl.multiple_of(j * TILE, TILE), TILE)
            p = sc[rows, :] * inv
            ds = (p * (nt(t1r[rows, :], d_i) - inner)).astype(BF)
            acc[rows, :] += jnp.where(low, nn(ds, t0[cols, :]), nn(p.astype(BF), t1[cols, :]))
            return dq + nn(t0t[:, rows], ds)

        dq = lax.fori_loop(0, i + 1, back, jnp.zeros((128, TILE), F32))[64:128] * SCALE
        cos, sin = cs[0:8, cols], cs[8:16, cols]
        f1, f2 = dq[0:8], dq[8:16]
        both = jnp.concatenate(
            [mix, f1 * cos + f2 * sin, f2 * cos - f1 * sin, dq[16:64]], axis=0
        )
        left[cols, :] = both.T.astype(BF)

    for i in range(8):
        cols = pl.ds(i * TILE, TILE)
        dk = acc[cols, :].T
        cos, sin = cs[0:8, cols], cs[8:16, cols]
        f1, f2 = dk[0:8], dk[8:16]
        both = jnp.concatenate([f1 * cos + f2 * sin, f2 * cos - f1 * sin, dk[16:128]], axis=0)
        right[cols, :] = both.T.astype(BF)

    def give(n, _):
        at = pl.ds(pl.multiple_of(order[n] * 64, 64), 64)
        out[n, :, 0:128] = left[at, :]
        out[n, :, 128:256] = right[at, :]
        return 0

    lax.fori_loop(0, 32, give, 0)


def attention(order, pack, cs):
    return pl.pallas_call(
        attention_kernel,
        out_shape=jax.ShapeDtypeStruct((32, 64, 256), BF),
        in_specs=[pl.BlockSpec(memory_space=pltpu.SMEM), VM, VM],
        out_specs=VM,
        scratch_shapes=[pltpu.VMEM((2048, 128), BF)] * 6
        + [pltpu.VMEM((128, 2048), BF)] * 2
        + [
            pltpu.VMEM((2048, TILE), F32),
            pltpu.VMEM((2048, 128), F32),
            pltpu.VMEM((2048, 128), BF),
            pltpu.VMEM((2048, 128), BF),
        ],
        compiler_params=pltpu.CompilerParams(vmem_limit_bytes=56 * MIB),
        name="attention",
    )(order, pack, cs)


def partials_kernel(
    x, g, e, hidden, dexp, first, wa, wb, g1, g2, ge, gs, act, dhat, grads, sums, gt, go
):
    step = pl.program_id(0)
    n = 256

    @pl.when(step == 0)
    def _():
        gt[...] = jnp.zeros_like(gt)
        go[...] = jnp.zeros_like(go)
        sums[...] = jnp.zeros_like(sums)

    low = left_half((n, 128))
    p0, p1 = e[0, :, 0:128].astype(F32), e[1, :, 0:128].astype(F32)
    r0, r1 = e[0, :, 128:256].astype(F32), e[1, :, 128:256].astype(F32)
    attn = jnp.where(low, p0, roll(p1, 64)).astype(BF)
    dtr = jnp.concatenate(
        [
            jnp.where(low, roll(p0, 64), p1),
            jnp.where(low, r0, roll(r1, 64)),
            jnp.where(low, roll(r0, 64), r1),
        ],
        axis=1,
    )
    dtr_low = dtr.astype(BF)
    grad = g[...].reshape(n, 1024)
    out = nn(attn, wb[0:128, :]) + nn(hidden[...], wb[128:640, :])
    act[...] = out.astype(BF).reshape(2, 128, 1024)
    x_hat, _ = normalised(x[...].reshape(n, 1024).astype(F32))
    d_first = nt(dtr_low, wa[:, 0:384])
    d_second = nt(dexp[...], wa[:, 384:896])
    both = d_first * g1[...] + d_second * g2[...]
    dhat[...] = both.astype(BF).reshape(2, 128, 1024)

    def down(v):
        return jnp.sum(v, axis=0, keepdims=True)

    sums[0:1, :] += down(d_first * x_hat)
    sums[1:2, :] += down(d_first)
    sums[2:3, :] += down(d_second * x_hat)
    sums[3:4, :] += down(d_second)
    sums[4:5, :] += down(grad.astype(F32))
    sums[5:6, 0:384] += down(dtr)
    sums[5:6, 384:896] += down(dexp[...].astype(F32))
    gt[...] += tn(first[...], dtr_low)
    go[...] += tn(attn, grad)

    @pl.when(step == 3)
    def _():
        for kk in range(2):
            for ff in range(8):
                at = [(tt * 2 + kk) * 64 + ff * 8 for tt in range(8)]
                own = kk * 8 + ff
                grads[kk, ff, 0:64, 0:384] = jnp.concatenate(
                    [gt[r : r + 8, :] for r in at], axis=0
                ).astype(BF)
                grads[kk, ff, 0:64, 384:896] = jnp.concatenate(
                    [ge[r : r + 8, :] for r in at], axis=0
                ).astype(BF)
                grads[kk, ff, 0:64, 896:1024] = jnp.concatenate(
                    [go[own * 8 : own * 8 + 8, j * 128 : j * 128 + 128] for j in range(8)], axis=0
                ).astype(BF)
                grads[kk, ff, 64:96, :] = gs[own * 32 : own * 32 + 32, :].astype(BF)


def partials(x, g, e, hidden, dexp, first, wa, wb, g1, g2, ge, gs):
    def whole(*shape):
        return pl.BlockSpec(shape, lambda i: (0,) * len(shape))

    tok = pl.BlockSpec((2, 128, 1024), lambda i: (i, 0, 0))
    return pl.pallas_call(
        partials_kernel,
        grid=(4,),
        out_shape=(
            jax.ShapeDtypeStruct((8, 128, 1024), BF),
            jax.ShapeDtypeStruct((8, 128, 1024), BF),
            jax.ShapeDtypeStruct((2, 8, 96, 1024), BF),
            jax.ShapeDtypeStruct((8, 1024), F32),
        ),
        in_specs=[
            tok,
            tok,
            pl.BlockSpec((2, 256, 256), lambda i: (0, i, 0)),
            pl.BlockSpec((256, 512), lambda i: (i, 0)),
            pl.BlockSpec((256, 512), lambda i: (i, 0)),
            pl.BlockSpec((256, 1024), lambda i: (i, 0)),
            whole(1024, 896),
            whole(640, 1024),
            whole(1, 1024),
            whole(1, 1024),
            whole(1024, 512),
            whole(512, 1024),
        ],
        out_specs=(tok, tok, whole(2, 8, 96, 1024), whole(8, 1024)),
        scratch_shapes=[pltpu.VMEM((1024, 384), F32), pltpu.VMEM((128, 1024), F32)],
        compiler_params=pltpu.CompilerParams(
            dimension_semantics=("arbitrary",), vmem_limit_bytes=56 * MIB
        ),
        name="partials",
    )(x, g, e, hidden, dexp, first, wa, wb, g1, g2, ge, gs)


SUM_COPIES = 2 + 1 + 3 + 6 + 3 + 2 + 1 + 14


def sums_kernel(
    act, dhat, grads, small, x, g, bias,
    act_o, tok_o, gtw_o, gew_o, gow_o, gsw_o, small_o,
    rb, rm, ra, rd, u, um, ru, rum, ta, rta, v, vm, rv, rvm, w, rw, fin, finm, rg, rgm,
    ss, rs,
):
    me = coords()
    a, b, k, xx, h = me
    t = a * 4 + b
    barrier(me, [ZL, *YS.values(), *ZYS.values(), *XS.values(), ZH, KC])
    send = Sender(me, ss, rs)
    to_core = (send(grads.at[1 - k], rb, KC), send(small.at[1 - k], rm, KC))
    act_z = send(act.at[1 - a], ra, ZL)
    dhat_y = [
        send(dhat.at[:, lax.rem(b + i, 4)], rd.at[j], YS[i]) for j, i in enumerate(NEAR_FIRST)
    ]
    for copy in to_core:
        copy.wait_recv()

    def pair(ff, _):
        u[ff] = (grads[k, ff].astype(F32) + rb[ff].astype(F32)).astype(BF)
        um[ff] = small[k, ff] + rm[ff]
        return 0

    lax.fori_loop(0, 8, pair, 0)
    to_x = []
    for j, i in enumerate(NEAR_FIRST):
        there = pl.ds(lax.rem(xx + i, 4) * 2, 2)
        to_x += [send(u.at[there], ru.at[j], XS[i]), send(um.at[there], rum.at[j], XS[i])]
    act_z.wait_recv()

    def pair_act(bb, _):
        ta[bb] = (act[a, bb].astype(F32) + ra[bb].astype(F32)).astype(BF)
        return 0

    lax.fori_loop(0, 4, pair_act, 0)
    act_y = [send(ta.at[lax.rem(b + i, 4)], rta.at[j], YS[i]) for j, i in enumerate(NEAR_FIRST)]
    for copy in to_x:
        copy.wait_recv()
    for hh in range(2):
        total, total_m = u[xx * 2 + hh].astype(F32), um[xx * 2 + hh]
        for j in range(3):
            total += ru[j, hh].astype(F32)
            total_m += rum[j, hh]
        v[hh] = total.astype(BF)
        vm[hh] = total_m
    to_zh = (send(v.at[1 - h], rv, ZH), send(vm.at[1 - h], rvm, ZH))
    for copy in dhat_y:
        copy.wait_recv()
    for aa in range(2):
        total = dhat[aa, b].astype(F32)
        for j in range(3):
            total += rd[j, aa].astype(F32)
        w[aa] = total.astype(BF)
    dhat_z = send(w.at[1 - a], rw, ZL)
    for copy in to_zh:
        copy.wait_recv()
    total = v[h].astype(F32) + rv[...].astype(F32)
    gsw_o[...] = total[64:96, :]
    for j in range(8):
        gow_o[:, j * 128 : j * 128 + 128] = total[j * 8 : j * 8 + 8, 896:1024]
        fin[j] = total[j * 8 : j * 8 + 8, 0:896]
    finm[...] = vm[h] + rvm[...]
    peers = [(ZL, 1, 0)] + [(YS[i], 0, i) for i in NEAR_FIRST] + [(ZYS[i], 1, i) for i in NEAR_FIRST]
    owners = []
    for off, da, db in peers:
        there = lax.rem(a + da, 2) * 4 + lax.rem(b + db, 4)
        owners += [send(fin.at[there], rg.at[t], off), send(finm, rgm.at[t], off)]
    rg[t] = fin[t]
    rgm[t] = finm[...]
    for copy in act_y:
        copy.wait_recv()
    total = x[...].astype(F32) + bias[...] + ta[b].astype(F32)
    for j in range(3):
        total += rta[j].astype(F32)
    act_o[...] = total.astype(BF)
    dhat_z.wait_recv()
    d_hat = w[a].astype(F32) + rw[...].astype(F32)
    x_hat, inv = normalised(x[...].astype(F32))
    tok_o[...] = g[...].astype(F32) + inv * (
        d_hat
        - jnp.mean(d_hat, axis=1, keepdims=True)
        - x_hat * jnp.mean(d_hat * x_hat, axis=1, keepdims=True)
    )
    for copy in owners:
        copy.wait_recv()
    for s in range(8):
        for o in range(3):
            at = o * 1024 + s * 128
            gtw_o[:, at : at + 128] = rg[s, :, o * 128 : o * 128 + 128]
        gew_o[:, s * 512 : s * 512 + 512] = rg[s, :, 384:896]
    total = rgm[0]
    for s in range(1, 8):
        total += rgm[s]
    small_o[...] = total
    send.finish()


def sums(act, dhat, grads, small, x, g, bias):
    shapes = [
        ((8, 96, 1024), BF),
        ((8, 8, 128), F32),
        ((4, 128, 1024), BF),
        ((3, 2, 128, 1024), BF),
        ((8, 96, 1024), BF),
        ((8, 8, 128), F32),
        ((3, 2, 96, 1024), BF),
        ((3, 2, 8, 128), F32),
        ((4, 128, 1024), BF),
        ((3, 128, 1024), BF),
        ((2, 96, 1024), BF),
        ((2, 8, 128), F32),
        ((96, 1024), BF),
        ((8, 128), F32),
        ((2, 128, 1024), BF),
        ((128, 1024), BF),
        ((8, 8, 896), F32),
        ((8, 128), F32),
        ((8, 8, 896), F32),
        ((8, 8, 128), F32),
    ]
    return pl.pallas_call(
        sums_kernel,
        out_shape=(
            jax.ShapeDtypeStruct((128, 1024), BF),
            jax.ShapeDtypeStruct((128, 1024), F32),
            jax.ShapeDtypeStruct((8, 3072), F32),
            jax.ShapeDtypeStruct((8, 4096), F32),
            jax.ShapeDtypeStruct((8, 1024), F32),
            jax.ShapeDtypeStruct((32, 1024), F32),
            jax.ShapeDtypeStruct((8, 128), F32),
        ),
        in_specs=[VM] * 7,
        out_specs=(VM,) * 7,
        scratch_shapes=[pltpu.VMEM(shape, kind) for shape, kind in shapes]
        + [pltpu.SemaphoreType.DMA((SUM_COPIES,))] * 2,
        compiler_params=pltpu.CompilerParams(
            collective_id=3, has_side_effects=True, vmem_limit_bytes=56 * MIB
        ),
        name="sums",
    )(act, dhat, grads, small, x, g, bias)


def shards(
    tokens_in,
    positions,
    block_pairs,
    first_gain,
    first_bias,
    second_gain,
    second_bias,
    triple_weight,
    triple_bias,
    output_weight,
    output_bias,
    expand_weight,
    expand_bias,
    shrink_weight,
    shrink_bias,
    cotangent,
):
    c = lax.axis_index("ctx")
    t, k = c // 2, c % 2
    x, g = tokens_in.reshape(128, 1024), cotangent.reshape(128, 1024)

    def cut(v, at, size, dim):
        return lax.dynamic_slice_in_dim(v, at, size, dim)

    wa = jnp.concatenate(
        [cut(triple_weight, o * 1024 + t * 128, 128, 1) for o in range(3)]
        + [cut(expand_weight, t * 512, 512, 1)],
        axis=1,
    )
    wb = jnp.concatenate(
        [cut(output_weight, t * 128, 128, 0), cut(shrink_weight, t * 512, 512, 0)], axis=0
    )
    tb = cut(triple_bias.reshape(3, 1024), t * 128, 128, 1).reshape(1, 384)
    eb = cut(expand_bias, t * 512, 512, 0).reshape(1, 512)
    order = block_pairs.reshape(8, 2, 2).transpose(1, 0, 2)
    rates = 1.0 / BASE ** (jnp.arange(0, 16, 2, dtype=F32) / 16)

    def turns(pos):
        angles = rates[:, None] * pos.astype(F32)[None, :]
        return jnp.concatenate([jnp.cos(angles), jnp.sin(angles)], axis=0)

    own_blocks = lax.dynamic_index_in_dim(order, k, 0, keepdims=False).reshape(16)
    cs_own = turns(jnp.take(positions.reshape(32, 64), own_blocks, axis=0).reshape(1024))
    cs_all = turns(positions.reshape(2048))
    g1, b1 = first_gain.reshape(1, 1024), first_bias.reshape(1, 1024)
    g2, b2 = second_gain.reshape(1, 1024), second_bias.reshape(1, 1024)

    xs, gs, was, wbs = gather(x, g, wa, wb)
    first, second, pack, hidden, dexp, grad_e, grad_s = tokens_part(
        xs, gs, was, wbs, tb, eb, g1, b1, g2, b2, cs_own
    )
    del second
    pack = swap(pack, "swap_in", 1)
    mixed = attention(order.reshape(32), pack.reshape(32, 64, 256), cs_all)
    mixed = swap(mixed.reshape(2, 1024, 256), "swap_out", 2)
    act, dhat, grads, sm = partials(
        xs, gs, mixed, hidden, dexp, first, was, wbs, g1, g2, grad_e, grad_s
    )

    here = (jnp.arange(8) == t).astype(F32)[:, None]

    def by_owner(v, n):
        return v.reshape(8, 2, 8, n).transpose(1, 2, 0, 3)

    def spread(v):
        return (here * v[None, :]).reshape(-1)

    dq, dk, dv, de = sm[5, 0:128], sm[5, 128:256], sm[5, 256:384], sm[5, 384:896]
    pieces = [by_owner(sm[i], 8) for i in range(4)]
    pieces.append(by_owner(jnp.concatenate([spread(dq), spread(dk)]), 16))
    pieces.append(by_owner(spread(dv), 8))
    pieces.append(by_owner(spread(de), 32))
    pieces.append(by_owner(sm[4] * jnp.repeat(here[:, 0], 128), 8))
    small = jnp.pad(jnp.concatenate(pieces, axis=3), ((0, 0),) * 3 + ((0, 32),))

    bias = (output_bias + shrink_bias).reshape(1, 1024)
    act, tok, gtw, gew, gow, gsw, small = sums(
        act.reshape(2, 4, 128, 1024), dhat.reshape(2, 4, 128, 1024), grads, small, x, g, bias
    )
    own = lax.dynamic_index_in_dim(small, t, 0, keepdims=False)
    return (
        act.reshape(tokens_in.shape),
        tok.reshape(tokens_in.shape),
        own[0:8],
        own[8:16],
        own[16:24],
        own[24:32],
        gtw,
        own[32:48],
        own[48:56],
        gow,
        own[88:96],
        gew,
        own[56:88],
        gsw,
        own[88:96],
    )


def solution(mesh):
    return jax.shard_map(
        shards,
        mesh=mesh,
        in_specs=(
            P("fsdp", "ctx", None, None, None),
            P("fsdp", None),
            P(),
            P(),
            P(),
            P(),
            P(),
            P("fsdp", None),
            P(),
            P(None, "fsdp"),
            P(),
            P("fsdp", None),
            P(),
            P(None, "fsdp"),
            P(),
            P("fsdp", "ctx", None, None, None),
        ),
        out_specs=(
            P("fsdp", "ctx", None, None, None),
            P("fsdp", "ctx", None, None, None),
            P(("ctx", "fsdp")),
            P(("ctx", "fsdp")),
            P(("ctx", "fsdp")),
            P(("ctx", "fsdp")),
            P(("ctx", "fsdp"), None),
            P(("ctx", "fsdp")),
            P(("ctx", "fsdp")),
            P(("ctx", "fsdp"), None),
            P(("ctx", "fsdp")),
            P(("ctx", "fsdp"), None),
            P(("ctx", "fsdp")),
            P(("ctx", "fsdp"), None),
            P(("ctx", "fsdp")),
        ),
        check_vma=False,
    )
```

```python
import math

import jax
import jax.numpy as jnp
from jax import lax
from jax.experimental import pallas as pl
from jax.experimental.pallas import tpu as pltpu
from jax.sharding import PartitionSpec as P

MESH = pl.DeviceIdType.MESH
BF, F32 = jnp.bfloat16, jnp.float32
EPS = 1e-05
BASE = 10000.0
MIB = 1 << 20
SCALE = 0.125

ZL, KC, ZH = (1, 0, 0, 0, 0), (0, 0, 1, 0, 0), (0, 0, 0, 0, 1)
YS = {i: (0, i, 0, 0, 0) for i in (1, 2, 3)}
XS = {i: (0, 0, 0, i, 0) for i in (1, 2, 3)}
NEAR_FIRST = (1, 3, 2)
OFFS = ((0, 0), (0, 1), (0, 3), (0, 2), (1, 0), (1, 1), (1, 3), (1, 2))
SLOT = {off: n for n, off in enumerate(OFFS)}


def origin(da, i):
    return SLOT[(da, (4 - i) % 4)]


def chips(n):
    return (*OFFS[n], 0, 0, 0)


def coords():
    c, f = lax.axis_index("ctx"), lax.axis_index("fsdp")
    return lax.div(c, 8), lax.rem(lax.div(c, 2), 4), lax.rem(c, 2), lax.div(f, 2), lax.rem(f, 2)


def device_at(me, off):
    a, b, k, x, h = (lax.rem(p + o, n) for p, o, n in zip(me, off, (2, 4, 2, 4, 2)))
    return ((a * 4 + b) * 2 + k, x * 2 + h)


def barrier(me, offs):
    sem = pltpu.get_barrier_semaphore()
    for off in offs:
        pl.semaphore_signal(sem, inc=1, device_id=device_at(me, off), device_id_type=MESH)
    pl.semaphore_wait(sem, len(offs))


class Sender:
    def __init__(self, me, send_sems, recv_sems):
        self.me, self.send_sems, self.recv_sems, self.copies = me, send_sems, recv_sems, []

    def __call__(self, src, dst, off):
        i = len(self.copies)
        copy = pltpu.make_async_remote_copy(
            src_ref=src,
            dst_ref=dst,
            send_sem=self.send_sems.at[i],
            recv_sem=self.recv_sems.at[i],
            device_id=device_at(self.me, off),
            device_id_type=MESH,
        )
        copy.start()
        self.copies.append(copy)
        return copy

    def finish(self):
        for copy in self.copies:
            copy.wait_send()


def nt(left, right):
    return lax.dot_general(left, right, (((1,), (1,)), ((), ())), preferred_element_type=F32)


def tn(left, right):
    return lax.dot_general(left, right, (((0,), (0,)), ((), ())), preferred_element_type=F32)


def nn(left, right):
    return jnp.dot(left, right, preferred_element_type=F32)


ANY = pl.BlockSpec(memory_space=pl.ANY)
VM = pl.BlockSpec(memory_space=pltpu.VMEM)


GATHER_COPIES = 2 * 7 + 2 * 15 + 8
KEEP = 4 + 6 * 8 + 2


def gather_kernel(
    x, g, wa, wb, tb, eb, g1, b1, g2, b2, cs,
    pack_o, x_o, g_o, first_o, p1_o, p2_o, waq_o, wbo_o, grads_o, sums_o,
    xs, gs, was, wbs, first, second, hidden, dexp, p1, p2, mine, theirs, ge, gsh,
    ss, rs, ls,
):
    me = coords()
    a, b, k, xx, h = me
    f = xx * 2 + h
    barrier(me, [ZL, *YS.values(), *XS.values(), ZH, KC])
    send = Sender(me, ss, rs)
    local = []

    def keep(src, dst):
        copy = pltpu.make_async_copy(src, dst, ls.at[len(local)])
        copy.start()
        local.append(copy)
        return copy

    def wa_at(ff):
        return was.at[pl.ds(pl.multiple_of(ff * 128 + k * 64, 64), 64)]

    def wb_at(ff):
        return wbs.at[
            pl.ds(pl.multiple_of(k * 320, 64), 320), pl.ds(pl.multiple_of(ff * 128, 128), 128)
        ]

    own_wa = wa.at[pl.ds(pl.multiple_of(k * 64, 64), 64)]
    own_wb = wb.at[pl.ds(pl.multiple_of(k * 320, 64), 320)]
    wz = (send(own_wa, wa_at(f), ZH), send(own_wb, wb_at(f), ZH))
    gz = send(g, gs.at[SLOT[(1, 0)]], ZL)
    wx = [(send(own_wa, wa_at(f), XS[i]), send(own_wb, wb_at(f), XS[i])) for i in NEAR_FIRST]
    gy = {i: send(g, gs.at[origin(0, i)], YS[i]) for i in NEAR_FIRST}
    xy = {i: send(x, xs.at[origin(0, i)], YS[i]) for i in NEAR_FIRST}
    xz = send(x, xs.at[SLOT[(1, 0)]], ZL)
    weights = [send(own_wa, wa_at(f), KC), send(own_wb, wb_at(f), KC)]
    own = [keep(x, xs.at[0]), keep(g, gs.at[0]), keep(own_wa, wa_at(f)), keep(own_wb, wb_at(f))]
    fz = xx * 2 + (1 - h)
    for copy in wz:
        copy.wait_recv()
    wxz = [
        (send(wa_at(fz), wa_at(fz), XS[i]), send(wb_at(fz), wb_at(fz), XS[i]))
        for i in NEAR_FIRST
    ]
    weights += [send(wa_at(fz), wa_at(fz), KC), send(wb_at(fz), wb_at(fz), KC)]
    gz.wait_recv()
    gzy = {i: send(gs.at[4], gs.at[origin(1, i)], YS[i]) for i in NEAR_FIRST}
    for j, i in enumerate(NEAR_FIRST):
        for copy in wx[j]:
            copy.wait_recv()
        fs = lax.rem(xx + 4 - i, 4) * 2 + h
        weights += [send(wa_at(fs), wa_at(fs), KC), send(wb_at(fs), wb_at(fs), KC)]
    xyz = {}
    for i in NEAR_FIRST:
        xy[i].wait_recv()
        n = origin(0, i)
        xyz[i] = send(xs.at[n], xs.at[origin(1, i)], ZL)
    for j, i in enumerate(NEAR_FIRST):
        for copy in wxz[j]:
            copy.wait_recv()
        fs = lax.rem(xx + 4 - i, 4) * 2 + (1 - h)
        weights += [send(wa_at(fs), wa_at(fs), KC), send(wb_at(fs), wb_at(fs), KC)]
    for copy in own:
        copy.wait()
    for copy in weights:
        copy.wait_recv()
    keep(was.at[:, 0:384], waq_o)
    keep(wbs.at[0:128], wbo_o)
    sums_o[...] = jnp.zeros_like(sums_o)
    low = left_half((128, 128))
    early = (lanes((128, 128)) & 63) < 8
    packs = []

    def down(v):
        return jnp.sum(v, axis=0, keepdims=True)

    def block(n):
        rows = slice(n * 128, n * 128 + 128)
        x_hat, _ = normalised(xs[n].astype(F32))
        first_low = (x_hat * g1[...] + b1[...]).astype(BF)
        second_low = (x_hat * g2[...] + b2[...]).astype(BF)
        first[n] = first_low
        second[rows, :] = second_low
        grad = gs[n]
        cos, sin = cs[0:8, rows], cs[8:16, rows]
        one, zero = jnp.ones((48, 128), F32), jnp.zeros((48, 128), F32)
        tc = jnp.concatenate([cos, cos, one, cos, cos, one], axis=0).T
        ts = jnp.concatenate([-sin, sin, zero, -sin, sin, zero], axis=0).T

        def turn(v):
            return v * tc + jnp.where(early, roll(v, 120), roll(v, 8)) * ts

        triple = nn(first_low, was[:, 0:384]) + tb[...]
        query, key, value = turn(triple[:, 0:128]), turn(triple[:, 128:256]), triple[:, 256:384]
        dmix = nt(grad, wbs[0:128, :])
        pairs = (
            (jnp.where(low, query, roll(key, 64)), jnp.where(low, roll(query, 64), key)),
            (jnp.where(low, value, roll(dmix, 64)), jnp.where(low, roll(value, 64), dmix)),
        )
        for j, (head0, head1) in enumerate(pairs):
            at = slice(j * 128, j * 128 + 128)
            mine[n, :, at] = jnp.where(k == 0, head0, head1).astype(BF)
            theirs[n, :, at] = jnp.where(k == 0, head1, head0).astype(BF)
        keep(mine.at[n], pack_o.at[k, n])
        packs.append(send(theirs.at[n], pack_o.at[k, n], KC))
        u = nn(second_low, was[:, 384:896]) + eb[...]
        cdf = 0.5 * (1.0 + lax.erf(u * math.sqrt(0.5)))
        pdf = jnp.exp(-0.5 * u * u) * (1.0 / math.sqrt(2.0 * math.pi))
        hidden_low = (u * cdf).astype(BF)
        hidden[rows, :] = hidden_low
        dexp_low = (nt(grad, wbs[128:640, :]) * (cdf + u * pdf)).astype(BF)
        dexp[rows, :] = dexp_low
        p1[n] = nn(hidden_low, wbs[128:640, :]).astype(BF)
        d_second = nt(dexp_low, was[:, 384:896])
        p2[n] = (d_second * g2[...]).astype(BF)
        sums_o[2:3, :] += down(d_second * x_hat)
        sums_o[3:4, :] += down(d_second)
        sums_o[4:5, :] += down(grad.astype(F32))
        sums_o[5:6, 384:896] += down(dexp_low.astype(F32))
        for src, dst in ((xs, x_o), (gs, g_o), (first, first_o), (p1, p1_o), (p2, p2_o)):
            keep(src.at[n], dst.at[n])

    for n, (da, db) in enumerate(OFFS):
        i = (4 - db) % 4
        if (da, db) == (1, 0):
            xz.wait_recv()
        elif da:
            gzy[i].wait_recv()
            xyz[i].wait_recv()
        elif db:
            gy[i].wait_recv()
        block(n)
    ge[...] = tn(second[...], dexp[...])
    gsh[...] = tn(hidden[...], gs[...].reshape(1024, 1024))
    for kk in range(2):
        for ff in range(8):
            at = [(tt * 2 + kk) * 64 + ff * 8 for tt in range(8)]
            own_rows = slice((kk * 8 + ff) * 32, (kk * 8 + ff) * 32 + 32)
            grads_o[kk, ff, 0:64, :] = jnp.concatenate(
                [ge[r : r + 8, :] for r in at], axis=0
            ).astype(BF)
            grads_o[kk, ff, 64:96, :] = gsh[own_rows, 0:512].astype(BF)
            grads_o[kk, ff, 96:128, :] = gsh[own_rows, 512:1024].astype(BF)
    for copy in packs:
        copy.wait_recv()
    send.finish()
    for copy in local[4:]:
        copy.wait()


def gather(x, g, wa, wb, tb, eb, g1, b1, g2, b2, cs):
    tok = jax.ShapeDtypeStruct((8, 128, 1024), BF)
    big = pltpu.VMEM((8, 128, 1024), BF)
    return pl.pallas_call(
        gather_kernel,
        out_shape=(
            jax.ShapeDtypeStruct((2, 8, 128, 256), BF),
            tok,
            tok,
            tok,
            tok,
            tok,
            jax.ShapeDtypeStruct((1024, 384), BF),
            jax.ShapeDtypeStruct((128, 1024), BF),
            jax.ShapeDtypeStruct((2, 8, 128, 512), BF),
            jax.ShapeDtypeStruct((8, 1024), F32),
        ),
        in_specs=[ANY] * 4 + [VM] * 7,
        out_specs=(ANY,) * 8 + (VM,) * 2,
        scratch_shapes=[
            big,
            big,
            pltpu.VMEM((1024, 896), BF),
            pltpu.VMEM((640, 1024), BF),
            big,
            pltpu.VMEM((1024, 1024), BF),
            pltpu.VMEM((1024, 512), BF),
            pltpu.VMEM((1024, 512), BF),
            big,
            big,
            pltpu.VMEM((8, 128, 256), BF),
            pltpu.VMEM((8, 128, 256), BF),
            pltpu.VMEM((1024, 512), F32),
            pltpu.VMEM((512, 1024), F32),
            pltpu.SemaphoreType.DMA((GATHER_COPIES,)),
            pltpu.SemaphoreType.DMA((GATHER_COPIES,)),
            pltpu.SemaphoreType.DMA((KEEP,)),
        ],
        compiler_params=pltpu.CompilerParams(
            collective_id=0, has_side_effects=True, vmem_limit_bytes=56 * MIB
        ),
        name="gather",
    )(x, g, wa, wb, tb, eb, g1, b1, g2, b2, cs)


def normalised(x):
    mean = jnp.mean(x, axis=1, keepdims=True)
    centred = x - mean
    inv = lax.rsqrt(jnp.mean(centred * centred, axis=1, keepdims=True) + EPS)
    return centred * inv, inv


def lanes(shape):
    return lax.broadcasted_iota(jnp.int32, shape, 1)


def left_half(shape):
    return lanes(shape) < 64


def roll(v, shift):
    return pltpu.roll(v, shift, 1)


TILE = 256


def attention_kernel(
    order, pack, cs, out, t0, t1, t0r, t1r, qz, dz, t0t, t1t, sc, acc, left, right
):
    def place(n, _):
        at = pl.ds(pl.multiple_of(order[n] * 64, 64), 64)
        v0, v1 = pack[n, :, 0:128].astype(F32), pack[n, :, 128:256].astype(F32)
        low = left_half((64, 128))
        v0 = jnp.where(low, v0 * SCALE, v0)
        t0[at, :] = v0.astype(BF)
        t1[at, :] = v1.astype(BF)
        t0r[at, :] = roll(v0, 64).astype(BF)
        t1r[at, :] = roll(v1, 64).astype(BF)
        qz[at, :] = jnp.where(low, v0, 0.0).astype(BF)
        dz[at, :] = jnp.where(low, 0.0, v1).astype(BF)
        return 0

    lax.fori_loop(0, 32, place, 0)
    acc[...] = jnp.zeros_like(acc)
    for i in range(8):
        rows = pl.ds(i * TILE, TILE)
        t0t[:, rows] = t0[rows, :].astype(F32).T.astype(BF)
        t1t[:, rows] = t1[rows, :].astype(F32).T.astype(BF)

    key_row = lax.broadcasted_iota(jnp.int32, (TILE, TILE), 0)
    query_col = lax.broadcasted_iota(jnp.int32, (TILE, TILE), 1)
    seen = key_row <= query_col
    low = left_half((TILE, 128))

    def folded(v, op):
        parts = [v[j * 8 : j * 8 + 8] for j in range(TILE // 8)]
        while len(parts) > 1:
            parts = [op(parts[j], parts[j + 1]) for j in range(0, len(parts), 2)]
        return parts[0]

    for i in range(8):
        cols = pl.ds(i * TILE, TILE)
        q_i, d_i = qz[cols, :], dz[cols, :]

        def scores(j, peak):
            rows = pl.ds(j * TILE, TILE)
            s = nt(t0r[rows, :], q_i)
            sc[rows, :] = s
            return jnp.maximum(peak, folded(s, jnp.maximum))

        s = jnp.where(seen, nt(t0r[cols, :], q_i), -jnp.inf)
        sc[cols, :] = s
        peak = folded(s, jnp.maximum)
        for j in range(i):
            peak = scores(j, peak)
        peak = jnp.max(peak, axis=0, keepdims=True)

        def weigh(j, carry):
            total, mix = carry
            rows = pl.ds(j * TILE, TILE)
            e = jnp.exp(sc[rows, :] - peak)
            sc[rows, :] = e
            return total + folded(e, jnp.add), mix + nn(t1t[:, rows], e.astype(BF))

        carry = (jnp.zeros((8, TILE), F32), jnp.zeros((128, TILE), F32))
        for j in range(i + 1):
            carry = weigh(j, carry)
        total, mix = carry
        inv = 1.0 / jnp.sum(total, axis=0, keepdims=True)
        mix = mix[0:64] * inv
        inner = jnp.sum(mix * t1t[64:128, cols].astype(F32), axis=0, keepdims=True)

        def back(j, dq):
            rows = pl.ds(j * TILE, TILE)
            p = sc[rows, :] * inv
            ds = (p * (nt(t1r[rows, :], d_i) - inner)).astype(BF)
            acc[rows, :] += jnp.where(low, nn(ds, t0[cols, :]), nn(p.astype(BF), t1[cols, :]))
            return dq + nn(t0t[:, rows], ds)

        dq = jnp.zeros((128, TILE), F32)
        for j in range(i + 1):
            dq = back(j, dq)
        dq = dq[64:128] * SCALE
        cos, sin = cs[0:8, cols], cs[8:16, cols]
        f1, f2 = dq[0:8], dq[8:16]
        both = jnp.concatenate(
            [mix, f1 * cos + f2 * sin, f2 * cos - f1 * sin, dq[16:64]], axis=0
        )
        left[cols, :] = both.T.astype(BF)

    for i in range(8):
        cols = pl.ds(i * TILE, TILE)
        dk = acc[cols, :].T
        cos, sin = cs[0:8, cols], cs[8:16, cols]
        f1, f2 = dk[0:8], dk[8:16]
        both = jnp.concatenate([f1 * cos + f2 * sin, f2 * cos - f1 * sin, dk[16:128]], axis=0)
        right[cols, :] = both.T.astype(BF)

    def give(n, _):
        at = pl.ds(pl.multiple_of(order[n] * 64, 64), 64)
        out[n, :, 0:128] = left[at, :]
        out[n, :, 128:256] = right[at, :]
        return 0

    lax.fori_loop(0, 32, give, 0)


def attention(order, pack, cs):
    return pl.pallas_call(
        attention_kernel,
        out_shape=jax.ShapeDtypeStruct((32, 64, 256), BF),
        in_specs=[pl.BlockSpec(memory_space=pltpu.SMEM), VM, VM],
        out_specs=VM,
        scratch_shapes=[pltpu.VMEM((2048, 128), BF)] * 6
        + [pltpu.VMEM((128, 2048), BF)] * 2
        + [
            pltpu.VMEM((2048, TILE), F32),
            pltpu.VMEM((2048, 128), F32),
            pltpu.VMEM((2048, 128), BF),
            pltpu.VMEM((2048, 128), BF),
        ],
        compiler_params=pltpu.CompilerParams(vmem_limit_bytes=56 * MIB),
        name="attention",
    )(order, pack, cs)


SUM_COPIES = 4 + 1 + 4 + 6 + 3 + 3 + 1 + 7 + 1 + 3 + 1 + 7 + 1 + 3 + 1 + 7 + 1
AFTER = (4, 5, 6, 7, 1, 2, 3, 0)


def finish_kernel(
    mixed, xi, gi, firsti, p1i, p2i, waq, wbo, gradsi, sums_a, g1, bias,
    act_o, tok_o, gtw_o, gew_o, gow_o, gsw_o, small_o,
    em, eo, xs, gs, first, p1, p2, act, dhat, attn, dtr, ra, rd, ta, rta, w, rw,
    gm, rgm, um, rum, vm, rvm, finm, rfm,
    gt, go, ga, rga, ua, rua, va, rva, fina, rfa,
    sm, rsm, sk, rsx, sz, rsz, st, rst,
    ss, rs, ls,
):
    me = coords()
    a, b, k, xx, h = me
    t = a * 4 + b
    local = []

    def load(src, dst):
        copy = pltpu.make_async_copy(src, dst, ls.at[len(local)])
        copy.start()
        local.append(copy)

    load(mixed.at[k], em)
    for src, dst in ((p1i, p1), (p2i, p2), (xi, xs), (gi, gs), (firsti, first)):
        load(src, dst)
    load(gradsi.at[k], gm)
    barrier(me, [*(chips(n) for n in range(1, 8)), *XS.values(), ZH, KC])
    send = Sender(me, ss, rs)
    e_sent = {
        n: send(mixed.at[1 - k, pl.ds(n, 2)], eo.at[pl.ds(n, 2)], KC) for n in (4, 6, 0, 2)
    }
    gm_core = send(gradsi.at[1 - k], rgm, KC)
    low = left_half((128, 128))
    sm[...] = sums_a[...]
    for copy in local:
        copy.wait()
    act_z, dhat_y = {}, {}

    def down(v):
        return jnp.sum(v, axis=0, keepdims=True)

    def block(n):
        rows = slice(n * 128, n * 128 + 128)
        tiles = []
        for at in (slice(0, 128), slice(128, 256)):
            own, other = em[n, :, at].astype(F32), eo[n, :, at].astype(F32)
            tiles.append((jnp.where(k == 0, own, other), jnp.where(k == 0, other, own)))
        (p_0, p_1), (r_0, r_1) = tiles
        attn_low = jnp.where(low, p_0, roll(p_1, 64)).astype(BF)
        turned = jnp.concatenate(
            [
                jnp.where(low, roll(p_0, 64), p_1),
                jnp.where(low, r_0, roll(r_1, 64)),
                jnp.where(low, roll(r_0, 64), r_1),
            ],
            axis=1,
        )
        turned_low = turned.astype(BF)
        attn[rows, :] = attn_low
        dtr[rows, :] = turned_low
        act[n] = (p1[n].astype(F32) + nn(attn_low, wbo[...])).astype(BF)
        da, db = OFFS[n]
        if da:
            act_z[n - 4] = send(act.at[n], ra.at[n - 4], ZL)
        d_first = nt(turned_low, waq[...])
        dhat[n] = (p2[n].astype(F32) + d_first * g1[...]).astype(BF)
        if db:
            dhat_y[n] = send(dhat.at[n], rd.at[da, NEAR_FIRST.index(db)], YS[db])
        x_hat, _ = normalised(xs[n].astype(F32))
        sm[0:1, :] += down(d_first * x_hat)
        sm[1:2, :] += down(d_first)
        sm[5:6, 0:384] += down(turned)

    def to_x(src, dst):
        sent = []
        for j, i in enumerate(NEAR_FIRST):
            there = pl.ds(lax.rem(xx + i, 4) * 2, 2)
            sent.append(send(src.at[there], dst.at[j], XS[i]))
        return sent

    def core_sum(own, got, dst):
        def one(ff, _):
            dst[ff] = (own[ff].astype(F32) + got[ff].astype(F32)).astype(BF)
            return 0

        lax.fori_loop(0, 8, one, 0)

    def x_sum(own, got, dst):
        for hh in range(2):
            total = own[xx * 2 + hh].astype(F32)
            for j in range(3):
                total += got[j, hh].astype(F32)
            dst[hh] = total.astype(BF)

    def to_owners(fin, got):
        sent = []
        for n in range(1, 8):
            da, db = OFFS[n]
            there = lax.rem(a + da, 2) * 4 + lax.rem(b + db, 4)
            sent.append(send(fin.at[there], got.at[origin(da, db)], chips(n)))
        got[0] = fin[t]
        return sent

    def wait(copies):
        for copy in copies:
            copy.wait_recv()

    for n in AFTER:
        if n in (4, 6, 1, 2):
            e_sent[n & 6].wait_recv()
        block(n)
        if n == 5:
            gm_core.wait_recv()
            core_sum(gm, rgm, um)
            gm_x = to_x(um, rum)
    sm_core = send(sm, rsm, KC)
    gt[...] = tn(first[...].reshape(1024, 1024), dtr[...])
    go[...] = tn(attn[...], gs[...].reshape(1024, 1024))
    for kk in range(2):
        for ff in range(8):
            at = [(tt * 2 + kk) * 64 + ff * 8 for tt in range(8)]
            r = (kk * 8 + ff) * 8
            ga[kk, ff, :, 0:384] = jnp.concatenate([gt[q : q + 8, :] for q in at], axis=0).astype(BF)
            ga[kk, ff, :, 384:512] = jnp.concatenate(
                [go[r : r + 8, j * 128 : j * 128 + 128] for j in range(8)], axis=0
            ).astype(BF)
    ga_core = send(ga.at[1 - k], rga, KC)
    act_y = []
    for m in (1, 2, 3):
        act_z[m].wait_recv()
        ta[m] = (act[m].astype(F32) + ra[m].astype(F32)).astype(BF)
        db = OFFS[m][1]
        act_y.append(send(ta.at[m], rta.at[NEAR_FIRST.index(db)], YS[db]))
    ga_core.wait_recv()
    core_sum(ga.at[k], rga, ua)
    ga_x = to_x(ua, rua)
    sm_core.wait_recv()
    sk[...] = sm[...] + rsm[...]
    sm_x = [send(sk, rsx.at[j], XS[i]) for j, i in enumerate(NEAR_FIRST)]
    wait(gm_x)
    x_sum(um, rum, vm)
    gm_zh = send(vm.at[1 - h], rvm, ZH)
    for n in (5, 6, 7):
        dhat_y[n].wait_recv()
    total = dhat[4].astype(F32)
    for j in range(3):
        total += rd[1, j].astype(F32)
    w[...] = total.astype(BF)
    dhat_z = send(w, rw, ZL)
    wait(ga_x)
    x_sum(ua, rua, va)
    ga_zh = send(va.at[1 - h], rva, ZH)
    wait(sm_x)
    sz[...] = sk[...] + rsx[0] + rsx[1] + rsx[2]
    sm_zh = send(sz, rsz, ZH)
    gm_zh.wait_recv()
    total = vm[h].astype(F32) + rvm[...].astype(F32)
    for j in range(8):
        finm[j] = total[j * 8 : j * 8 + 8, :]
    gsw_o[:, 0:512] = total[64:96, :]
    gsw_o[:, 512:1024] = total[96:128, :]
    gm_own = to_owners(finm, rfm)
    ga_zh.wait_recv()
    total = va[h].astype(F32) + rva[...].astype(F32)
    for j in range(8):
        fina[j] = total[j * 8 : j * 8 + 8, 0:384]
        gow_o[:, j * 128 : j * 128 + 128] = total[j * 8 : j * 8 + 8, 384:512]
    ga_own = to_owners(fina, rfa)
    sm_zh.wait_recv()
    total = sz[...] + rsz[...]
    for j in range(8):
        st[j, 0:4, :] = total[0:4, j * 128 : j * 128 + 128]
        st[j, 4:5, :] = total[5:6, 0:128]
        st[j, 5:6, :] = total[5:6, 128:256]
        st[j, 6:7, :] = total[4:5, j * 128 : j * 128 + 128]
        st[j, 7:8, :] = total[5:6, 256:384]
    small_o[8:12, :] = jnp.concatenate(
        [total[5:6, 384 + j * 128 : 512 + j * 128] for j in range(4)], axis=0
    )
    small_o[12:16, :] = jnp.zeros((4, 128), F32)
    st_own = to_owners(st, rst)
    act_z[0].wait_recv()
    wait(act_y)
    total = xs[0].astype(F32) + bias[...] + act[0].astype(F32) + ra[0].astype(F32)
    for j in range(3):
        total += rta[j].astype(F32)
    act_o[...] = total.astype(BF)
    for n in (1, 2, 3):
        dhat_y[n].wait_recv()
    total = dhat[0].astype(F32)
    for j in range(3):
        total += rd[0, j].astype(F32)
    x_hat, inv = normalised(xs[0].astype(F32))
    dhat_z.wait_recv()
    d_hat = total + rw[...].astype(F32)
    tok_o[...] = gs[0].astype(F32) + inv * (
        d_hat
        - jnp.mean(d_hat, axis=1, keepdims=True)
        - x_hat * jnp.mean(d_hat * x_hat, axis=1, keepdims=True)
    )
    wait(gm_own)
    wait(ga_own)
    wait(st_own)
    for n, (da, db) in enumerate(OFFS):
        ts = lax.rem(a + da, 2) * 4 + lax.rem(b + db, 4)
        for o in range(3):
            at = pl.ds(pl.multiple_of(o * 1024 + ts * 128, 128), 128)
            gtw_o[:, at] = rfa[n, :, o * 128 : o * 128 + 128]
        gew_o[:, pl.ds(pl.multiple_of(ts * 512, 512), 512)] = rfm[n]
    total = rst[0]
    for n in range(1, 8):
        total += rst[n]
    small_o[0:4, :] = total[0:4, :]
    source = lax.rem(2 * t + k, 8)
    bias_rows = jnp.zeros((2, 128), F32)
    for n, (da, db) in enumerate(OFFS):
        ts = lax.rem(a + da, 2) * 4 + lax.rem(b + db, 4)
        bias_rows = jnp.where(ts == source, rst[n, 4:6, :], bias_rows)
    small_o[4:5, :] = jnp.where(a == 0, bias_rows[0:1], bias_rows[1:2])
    small_o[5:6, :] = st[t, 6:7, :]
    small_o[6:7, :] = st[t, 7:8, :]
    small_o[7:8, :] = jnp.zeros((1, 128), F32)
    send.finish()


def finish(mixed, xs, gs, first, p1, p2, waq, wbo, grads, sums_a, g1, bias):
    tok = ((8, 128, 1024), BF)
    shapes = [
        ((8, 128, 256), BF),
        ((8, 128, 256), BF),
        tok,
        tok,
        tok,
        tok,
        tok,
        tok,
        tok,
        ((1024, 128), BF),
        ((1024, 384), BF),
        ((4, 128, 1024), BF),
        ((2, 3, 128, 1024), BF),
        ((4, 128, 1024), BF),
        ((3, 128, 1024), BF),
        ((128, 1024), BF),
        ((128, 1024), BF),
        ((8, 128, 512), BF),
        ((8, 128, 512), BF),
        ((8, 128, 512), BF),
        ((3, 2, 128, 512), BF),
        ((2, 128, 512), BF),
        ((128, 512), BF),
        ((8, 8, 512), F32),
        ((8, 8, 512), F32),
        ((1024, 384), F32),
        ((128, 1024), F32),
        ((2, 8, 64, 512), BF),
        ((8, 64, 512), BF),
        ((8, 64, 512), BF),
        ((3, 2, 64, 512), BF),
        ((2, 64, 512), BF),
        ((64, 512), BF),
        ((8, 8, 384), F32),
        ((8, 8, 384), F32),
        ((8, 1024), F32),
        ((8, 1024), F32),
        ((8, 1024), F32),
        ((3, 8, 1024), F32),
        ((8, 1024), F32),
        ((8, 1024), F32),
        ((8, 8, 128), F32),
        ((8, 8, 128), F32),
    ]
    return pl.pallas_call(
        finish_kernel,
        out_shape=(
            jax.ShapeDtypeStruct((128, 1024), BF),
            jax.ShapeDtypeStruct((128, 1024), F32),
            jax.ShapeDtypeStruct((8, 3072), F32),
            jax.ShapeDtypeStruct((8, 4096), F32),
            jax.ShapeDtypeStruct((8, 1024), F32),
            jax.ShapeDtypeStruct((32, 1024), F32),
            jax.ShapeDtypeStruct((16, 128), F32),
        ),
        in_specs=[ANY] * 6 + [VM] * 2 + [ANY] + [VM] * 3,
        out_specs=(VM,) * 7,
        scratch_shapes=[pltpu.VMEM(shape, kind) for shape, kind in shapes]
        + [
            pltpu.SemaphoreType.DMA((SUM_COPIES,)),
            pltpu.SemaphoreType.DMA((SUM_COPIES,)),
            pltpu.SemaphoreType.DMA((7,)),
        ],
        compiler_params=pltpu.CompilerParams(
            collective_id=1, has_side_effects=True, vmem_limit_bytes=56 * MIB
        ),
        name="finish",
    )(mixed, xs, gs, first, p1, p2, waq, wbo, grads, sums_a, g1, bias)


def shards(
    tokens_in,
    positions,
    block_pairs,
    first_gain,
    first_bias,
    second_gain,
    second_bias,
    triple_weight,
    triple_bias,
    output_weight,
    output_bias,
    expand_weight,
    expand_bias,
    shrink_weight,
    shrink_bias,
    cotangent,
):
    c = lax.axis_index("ctx")
    t, k = c // 2, c % 2
    x, g = tokens_in.reshape(128, 1024), cotangent.reshape(128, 1024)

    def cut(v, at, size, dim):
        return lax.dynamic_slice_in_dim(v, at, size, dim)

    wa = jnp.concatenate(
        [cut(triple_weight, o * 1024 + t * 128, 128, 1) for o in range(3)]
        + [cut(expand_weight, t * 512, 512, 1)],
        axis=1,
    )
    wb = jnp.concatenate(
        [cut(output_weight, t * 128, 128, 0), cut(shrink_weight, t * 512, 512, 0)], axis=0
    )
    tb = cut(triple_bias.reshape(3, 1024), t * 128, 128, 1).reshape(1, 384)
    eb = cut(expand_bias, t * 512, 512, 0).reshape(1, 512)
    a, b = t // 4, t % 4
    chip = jnp.stack([((a + da) % 2) * 4 + (b + db) % 4 for da, db in OFFS])
    order = jnp.take(block_pairs.reshape(8, 2, 2), chip, axis=0).transpose(1, 0, 2)
    rates = 1.0 / BASE ** (jnp.arange(0, 16, 2, dtype=F32) / 16)

    def turns(pos):
        angles = rates[:, None] * pos.astype(F32)[None, :]
        return jnp.concatenate([jnp.cos(angles), jnp.sin(angles)], axis=0)

    own_blocks = lax.dynamic_index_in_dim(order, k, 0, keepdims=False).reshape(16)
    cs_own = turns(jnp.take(positions.reshape(32, 64), own_blocks, axis=0).reshape(1024))
    cs_all = turns(positions.reshape(2048))
    g1, b1 = first_gain.reshape(1, 1024), first_bias.reshape(1, 1024)
    g2, b2 = second_gain.reshape(1, 1024), second_bias.reshape(1, 1024)

    pack, xs, gs, first, p1, p2, waq, wbo, grads, sm = gather(
        x, g, wa, wb, tb, eb, g1, b1, g2, b2, cs_own
    )
    mixed = attention(order.reshape(32), pack.reshape(32, 64, 256), cs_all)
    bias = (output_bias + shrink_bias).reshape(1, 1024)
    act, tok, gtw, gew, gow, gsw, small = finish(
        mixed.reshape(2, 8, 128, 256), xs, gs, first, p1, p2, waq, wbo, grads, sm, g1, bias
    )
    f = lax.axis_index("fsdp")
    eight = cut(small, k * 64 + f * 8, 8, 1)
    sixteen = cut(small[4], f * 16, 16, 0)
    wide = cut(small[8:12].reshape(512), k * 256 + f * 32, 32, 0)
    return (
        act.reshape(tokens_in.shape),
        tok.reshape(tokens_in.shape),
        eight[0],
        eight[1],
        eight[2],
        eight[3],
        gtw,
        sixteen,
        eight[6],
        gow,
        eight[5],
        gew,
        wide,
        gsw,
        eight[5],
    )


def solution(mesh):
    return jax.shard_map(
        shards,
        mesh=mesh,
        in_specs=(
            P("fsdp", "ctx", None, None, None),
            P("fsdp", None),
            P(),
            P(),
            P(),
            P(),
            P(),
            P("fsdp", None),
            P(),
            P(None, "fsdp"),
            P(),
            P("fsdp", None),
            P(),
            P(None, "fsdp"),
            P(),
            P("fsdp", "ctx", None, None, None),
        ),
        out_specs=(
            P("fsdp", "ctx", None, None, None),
            P("fsdp", "ctx", None, None, None),
            P(("ctx", "fsdp")),
            P(("ctx", "fsdp")),
            P(("ctx", "fsdp")),
            P(("ctx", "fsdp")),
            P(("ctx", "fsdp"), None),
            P(("ctx", "fsdp")),
            P(("ctx", "fsdp")),
            P(("ctx", "fsdp"), None),
            P(("ctx", "fsdp")),
            P(("ctx", "fsdp"), None),
            P(("ctx", "fsdp")),
            P(("ctx", "fsdp"), None),
            P(("ctx", "fsdp")),
        ),
        check_vma=False,
    )
```

```python
import math

import jax
import jax.numpy as jnp
import numpy as np
from jax import lax
from jax.experimental import pallas as pl
from jax.experimental.pallas import tpu as pltpu
from jax.sharding import PartitionSpec as P

MESH = pl.DeviceIdType.MESH
BF, F32 = jnp.bfloat16, jnp.float32
EPS = 1e-05
BASE = 10000.0
MIB = 1 << 20
SCALE = 0.125
TILE = 256
RATES = 1.0 / BASE ** (np.arange(0, 16, 2, dtype=np.float32) / 16)

ZL, KC, ZH = (1, 0, 0, 0, 0), (0, 0, 1, 0, 0), (0, 0, 0, 0, 1)
YS = {i: (0, i, 0, 0, 0) for i in (1, 2, 3)}
XS = {i: (0, 0, 0, i, 0) for i in (1, 2, 3)}
NEAR_FIRST = (1, 3, 2)
OFFS = ((0, 0), (0, 1), (0, 3), (0, 2), (1, 0), (1, 1), (1, 3), (1, 2))
SLOT = {off: n for n, off in enumerate(OFFS)}


def origin(da, i):
    return SLOT[(da, (4 - i) % 4)]


def chips(n):
    return (*OFFS[n], 0, 0, 0)


def coords():
    c, f = lax.axis_index("ctx"), lax.axis_index("fsdp")
    return lax.div(c, 8), lax.rem(lax.div(c, 2), 4), lax.rem(c, 2), lax.div(f, 2), lax.rem(f, 2)


def device_at(me, off):
    a, b, k, x, h = (lax.rem(p + o, n) for p, o, n in zip(me, off, (2, 4, 2, 4, 2)))
    return ((a * 4 + b) * 2 + k, x * 2 + h)


def barrier(me, offs):
    sem = pltpu.get_barrier_semaphore()
    for off in offs:
        pl.semaphore_signal(sem, inc=1, device_id=device_at(me, off), device_id_type=MESH)
    pl.semaphore_wait(sem, len(offs))


class Sender:
    def __init__(self, me, send_sems, recv_sems):
        self.me, self.send_sems, self.recv_sems, self.copies = me, send_sems, recv_sems, []

    def __call__(self, src, dst, off):
        i = len(self.copies)
        copy = pltpu.make_async_remote_copy(
            src_ref=src,
            dst_ref=dst,
            send_sem=self.send_sems.at[i],
            recv_sem=self.recv_sems.at[i],
            device_id=device_at(self.me, off),
            device_id_type=MESH,
        )
        copy.start()
        self.copies.append(copy)
        return copy

    def finish(self):
        for copy in self.copies:
            copy.wait_send()


def nt(left, right):
    return lax.dot_general(left, right, (((1,), (1,)), ((), ())), preferred_element_type=F32)


def tn(left, right):
    return lax.dot_general(left, right, (((0,), (0,)), ((), ())), preferred_element_type=F32)


def nn(left, right):
    return jnp.dot(left, right, preferred_element_type=F32)


def down(v):
    return jnp.sum(v, axis=0, keepdims=True)


def lanes(shape):
    return lax.broadcasted_iota(jnp.int32, shape, 1)


def roll(v, shift):
    return pltpu.roll(v, shift, 1)


ANY = pl.BlockSpec(memory_space=pl.ANY)
VM = pl.BlockSpec(memory_space=pltpu.VMEM)


COPIES = 45 + 22 + 16 + 10 + 5 + 21 + 28
LOADS = 8
TOK = (8, 128, 1024)
SCRATCH = (
    ("xs", TOK, BF),
    ("gs", TOK, BF),
    ("first", TOK, BF),
    ("second", (1024, 1024), BF),
    ("mus", (1024, 1), F32),
    ("invs", (1024, 1), F32),
    ("was", (1024, 896), BF),
    ("wos", (128, 1024), BF),
    ("wss", (512, 1024), BF),
    ("slope", (1024, 512), F32),
    ("hidden", (1024, 512), BF),
    ("dexp", (1024, 512), BF),
    ("cst", (16, 2048), F32),
    ("cs3", (32, 16, 128), F32),
    ("pk", (32, 64, 256), BF),
    ("th", (16, 64, 256), BF),
    ("pd", (32, 64, 128), BF),
    ("td", (16, 64, 128), BF),
    ("kq", (2048, 128), BF),
    ("qz", (2048, 128), BF),
    ("vz", (2048, 128), BF),
    ("vt", (64, 2048), BF),
    ("kt", (64, 2048), BF),
    ("dt", (64, 2048), BF),
    ("sc", (2048, TILE), F32),
    ("es", (36, TILE, TILE), BF),
    ("acc", (2048, 128), F32),
    ("mixs", (64, 2048), F32),
    ("rsum", (8, TILE), F32),
    ("ot", (32, 64, 128), BF),
    ("o_own", (16, 64, 128), BF),
    ("o_away", (16, 64, 128), BF),
    ("o_got", (16, 64, 128), BF),
    ("dd", (32, 64, 256), BF),
    ("d_own", (16, 64, 256), BF),
    ("d_away", (16, 64, 256), BF),
    ("d_got", (16, 64, 256), BF),
    ("attn", (1024, 128), BF),
    ("dtr", (1024, 384), BF),
    ("act", TOK, BF),
    ("act_rz", (4, 64, 1024), BF),
    ("act_ry", (2, 3, 64, 1024), BF),
    ("act_t", (4, 64, 1024), BF),
    ("act_rt", (3, 64, 1024), BF),
    ("act_w", (64, 1024), BF),
    ("act_rw", (64, 1024), BF),
    ("dhat", TOK, BF),
    ("dhat_rz", (4, 64, 1024), BF),
    ("dhat_ry", (2, 3, 64, 1024), BF),
    ("dhat_t", (4, 64, 1024), BF),
    ("dhat_rt", (3, 64, 1024), BF),
    ("dhat_w", (64, 1024), BF),
    ("dhat_rw", (64, 1024), BF),
    ("gsh", (512, 1024), F32),
    ("gm", (2, 8, 128, 512), BF),
    ("gm_r", (8, 128, 512), BF),
    ("gm_u", (8, 128, 512), BF),
    ("gm_ru", (3, 2, 128, 512), BF),
    ("gm_v", (2, 128, 512), BF),
    ("gm_rv", (128, 512), BF),
    ("gm_f", (8, 8, 512), F32),
    ("gm_rf", (8, 8, 512), F32),
    ("go", (128, 1024), F32),
    ("ga", (2, 8, 64, 512), BF),
    ("ga_r", (8, 64, 512), BF),
    ("ga_u", (8, 64, 512), BF),
    ("ga_ru", (3, 2, 64, 512), BF),
    ("ga_v", (2, 64, 512), BF),
    ("ga_rv", (64, 512), BF),
    ("ga_f", (8, 8, 384), F32),
    ("ga_rf", (8, 8, 384), F32),
    ("sm", (8, 1024), F32),
    ("sm_r", (8, 1024), F32),
    ("sm_u", (8, 1024), F32),
    ("sm_ru", (3, 8, 1024), F32),
    ("sm_v", (8, 1024), F32),
    ("sm_rv", (8, 1024), F32),
    ("sm_f", (8, 8, 128), F32),
    ("sm_rf", (8, 8, 128), F32),
)
ZR, YR = slice(0, 64), slice(64, 128)


class Refs:
    pass


class RowSum:
    def __init__(self, send, src, rz, ry, t, rt, w, rw):
        self.send, self.src = send, src
        self.rz, self.ry, self.t, self.rt, self.w, self.rw = rz, ry, t, rt, w, rw
        self.z, self.y, self.on = {}, {}, []

    def start(self, n):
        da, db = OFFS[n]
        if da:
            self.z[n - 4] = self.send(self.src.at[n, ZR], self.rz.at[n - 4], ZL)
        if db:
            j = NEAR_FIRST.index(db)
            self.y[n] = self.send(self.src.at[n, YR], self.ry.at[da, j], YS[db])

    def middle(self):
        for m in (1, 2, 3):
            self.z[m].wait_recv()
            self.t[m] = (self.src[m, ZR].astype(F32) + self.rz[m].astype(F32)).astype(BF)
            db = OFFS[m][1]
            j = NEAR_FIRST.index(db)
            self.on.append(self.send(self.t.at[m], self.rt.at[j], YS[db]))
        for n in (5, 6, 7):
            self.y[n].wait_recv()
        total = self.src[4, YR].astype(F32)
        for j in range(3):
            total += self.ry[1, j].astype(F32)
        self.w[...] = total.astype(BF)
        self.on.append(self.send(self.w, self.rw, ZL))

    def end(self):
        self.z[0].wait_recv()
        for n in (1, 2, 3):
            self.y[n].wait_recv()
        for copy in self.on:
            copy.wait_recv()
        upper = self.src[0, ZR].astype(F32) + self.rz[0].astype(F32)
        lower = self.src[0, YR].astype(F32) + self.rw[...].astype(F32)
        for j in range(3):
            upper += self.rt[j].astype(F32)
            lower += self.ry[0, j].astype(F32)
        return jnp.concatenate([upper, lower], axis=0)


class WeightSum:
    def __init__(self, send, me, kind, r, u, ru, v, rv, f, rf):
        self.send, self.me, self.kind = send, me, kind
        self.r, self.u, self.ru, self.v, self.rv, self.f, self.rf = r, u, ru, v, rv, f, rf

    def core(self, src):
        self.src = src
        self.sent = [self.send(src.at[1 - self.me[2]], self.r, KC)]

    def wait(self):
        for copy in self.sent:
            copy.wait_recv()

    def along_x(self):
        k, x = self.me[2], self.me[3]
        self.wait()

        def one(f, _):
            self.u[f] = (self.src[k, f].astype(F32) + self.r[f].astype(F32)).astype(self.kind)
            return 0

        lax.fori_loop(0, 8, one, 0)
        self.sent = []
        for j, i in enumerate(NEAR_FIRST):
            there = pl.ds(lax.rem(x + i, 4) * 2, 2)
            self.sent.append(self.send(self.u.at[there], self.ru.at[j], XS[i]))

    def along_z(self):
        x, h = self.me[3], self.me[4]
        self.wait()
        for hh in range(2):
            total = self.u[x * 2 + hh].astype(F32)
            for j in range(3):
                total += self.ru[j, hh].astype(F32)
            self.v[hh] = total.astype(self.kind)
        self.sent = [self.send(self.v.at[1 - h], self.rv, ZH)]

    def total(self):
        self.wait()
        return self.v[self.me[4]].astype(F32) + self.rv[...].astype(F32)

    def to_owners(self):
        a, b = self.me[0], self.me[1]
        self.sent = []
        for n in range(1, 8):
            da, db = OFFS[n]
            there = lax.rem(a + da, 2) * 4 + lax.rem(b + db, 4)
            self.sent.append(self.send(self.f.at[there], self.rf.at[origin(da, db)], chips(n)))
        self.rf[0] = self.f[a * 4 + b]


def block_kernel(
    pairs, pos, x, g, tw, ow, ew, sw, tb, eb, g1, b1, g2, b2, bias,
    act_o, tok_o, gtw_o, gew_o, gow_o, gsw_o, small_o, *scratch,
):
    s = Refs()
    for (name, _, _), ref in zip(SCRATCH, scratch):
        setattr(s, name, ref)
    ss, rs, ls, inv_slot = scratch[len(SCRATCH) :]
    me = coords()
    a, b, k, xx, h = me
    t, f = a * 4 + b, xx * 2 + h
    local = []

    def load(src, dst):
        copy = pltpu.make_async_copy(src, dst, ls.at[len(local)])
        copy.start()
        local.append(copy)

    def cols_at(ff):
        return pl.ds(pl.multiple_of(ff * 128, 128), 128)

    def pieces(ff):
        rows = pl.ds(pl.multiple_of(ff * 128 + k * 64, 64), 64)
        return (
            s.was.at[rows],
            s.wos.at[pl.ds(pl.multiple_of(k * 64, 64), 64), cols_at(ff)],
            s.wss.at[pl.ds(pl.multiple_of(k * 256, 256), 256), cols_at(ff)],
        )

    half = pl.ds(pl.multiple_of(k * 64, 64), 64)
    mine = pl.ds(pl.multiple_of(f * 128 + k * 64, 64), 64)
    for o in range(3):
        load(
            tw.at[half, pl.ds(pl.multiple_of(o * 1024 + t * 128, 128), 128)],
            s.was.at[mine, pl.ds(o * 128, 128)],
        )
    load(ew.at[half, pl.ds(pl.multiple_of(t * 512, 512), 512)], s.was.at[mine, pl.ds(384, 512)])
    load(ow.at[pl.ds(pl.multiple_of(t * 128 + k * 64, 64), 64)], pieces(f)[1])
    load(sw.at[pl.ds(pl.multiple_of(t * 512 + k * 256, 256), 256)], pieces(f)[2])
    load(x, s.xs.at[0])
    load(g, s.gs.at[0])
    barrier(me, [*(chips(n) for n in range(1, 8)), *XS.values(), ZH, KC])
    send = Sender(me, ss, rs)

    def send_pieces(ff, off):
        return [send(ref, ref, off) for ref in pieces(ff)]

    def wait(copies):
        for copy in copies:
            copy.wait_recv()

    def tokens_out(src, dst):
        z = [send(src.at[rows], dst.at[4, rows], ZL) for rows in (ZR, YR)]
        y = {i: send(src, dst.at[origin(0, i)], YS[i]) for i in NEAR_FIRST}
        return z, y

    def tokens_on_y(z, dst):
        z[0].wait_recv()
        return {i: send(dst.at[4, ZR], dst.at[origin(1, i), ZR], YS[i]) for i in NEAR_FIRST}

    def tokens_on_z(y, dst):
        on = {}
        for i in NEAR_FIRST:
            y[i].wait_recv()
            on[i] = send(dst.at[origin(0, i), YR], dst.at[origin(1, i), YR], ZL)
        return on

    for copy in local:
        copy.wait()
    wz = send_pieces(f, ZH)
    wx = {i: send_pieces(f, XS[i]) for i in NEAR_FIRST}
    x_z, x_y = tokens_out(x, s.xs)
    weights = send_pieces(f, KC)

    def chip_at(n):
        da, db = OFFS[n]
        return lax.rem(a + da, 2) * 4 + lax.rem(b + db, 4)

    def block_of(kk, n, j):
        return pairs[j, chip_at(n) * 2 + kk]

    held = [block_of(kk, n, j) for kk in range(2) for n in range(8) for j in range(2)]

    def find(j, _):
        at = jnp.int32(0)
        for q, block in enumerate(held):
            at = jnp.where(block == j, q, at)
        inv_slot[j] = at
        return 0

    lax.fori_loop(0, 32, find, 0)
    row = lax.broadcasted_iota(jnp.int32, (8, 1), 0)
    rates = jnp.zeros((8, 1), F32)
    for j in range(8):
        rates = jnp.where(row == j, float(RATES[j]), rates)
    angles = rates * pos[...].astype(F32)
    s.cst[0:8, :] = jnp.cos(angles)
    s.cst[8:16, :] = jnp.sin(angles)
    low16 = lanes((16, 128)) < 64
    for j in range(16):
        both = s.cst[:, j * 128 : j * 128 + 128]
        turned = roll(both, 64)
        s.cs3[2 * j] = jnp.where(low16, both, turned)
        s.cs3[2 * j + 1] = jnp.where(low16, turned, both)
    s.sm[...] = jnp.zeros_like(s.sm)

    def norm(n):
        rows = slice(n * 128, n * 128 + 128)
        v = s.xs[n].astype(F32)
        mean = jnp.mean(v, axis=1, keepdims=True)
        centred = v - mean
        inv = lax.rsqrt(jnp.mean(centred * centred, axis=1, keepdims=True) + EPS)
        s.mus[rows, :] = mean
        s.invs[rows, :] = inv
        x_hat = centred * inv
        s.first[n] = (x_hat * g1[...] + b1[...]).astype(BF)
        s.second[rows, :] = (x_hat * g2[...] + b2[...]).astype(BF)

    norm(0)
    fz = xx * 2 + (1 - h)
    wait(wz)
    wxz = {i: send_pieces(fz, XS[i]) for i in NEAR_FIRST}
    weights += send_pieces(fz, KC)
    x_yz = tokens_on_y(x_z, s.xs)
    x_zy = tokens_on_z(x_y, s.xs)
    g_z, g_y = tokens_out(g, s.gs)
    for n in (1, 2, 3):
        norm(n)
    for i in NEAR_FIRST:
        wait(wx[i])
        weights += send_pieces(lax.rem(xx + 4 - i, 4) * 2 + h, KC)
    x_z[1].wait_recv()
    norm(4)
    for i in NEAR_FIRST:
        wait(wxz[i])
        weights += send_pieces(lax.rem(xx + 4 - i, 4) * 2 + (1 - h), KC)
    for i, n in ((3, 5), (1, 6), (2, 7)):
        x_yz[i].wait_recv()
        x_zy[i].wait_recv()
        norm(n)
    g_yz = tokens_on_y(g_z, s.gs)
    wait(weights)

    low = lanes((256, 128)) < 64
    low128 = lanes((16, 128)) < 64
    early = (lanes((256, 128)) & 63) < 8
    bias_at = [tb[0:1, pl.ds(pl.multiple_of(o * 1024 + t * 128, 128), 128)] for o in range(3)]
    triple_bias = jnp.concatenate(bias_at, axis=1)
    expand_bias = eb[0:1, pl.ds(pl.multiple_of(t * 512, 512), 512)]

    def deal(tiles, own, away, to, m):
        quads = pl.ds(4 * m, 4)
        for j, (head0, head1) in enumerate(tiles):
            at = slice(j * 128, j * 128 + 128)
            keep = jnp.where(k == 0, head0, head1).astype(BF).reshape(4, 64, 128)
            give = jnp.where(k == 0, head1, head0).astype(BF).reshape(4, 64, 128)
            own[pl.ds(k * 16 + 4 * m, 4), :, at] = keep
            away[quads, :, at] = give
        return send(away.at[quads], to.at[pl.ds(k * 16 + 4 * m, 4)], KC)

    def attend_in(m):
        rows = slice(m * 256, m * 256 + 256)
        tables = []
        for n in (2 * m, 2 * m + 1):
            tables.append(
                jnp.where(low128, s.cs3[block_of(k, n, 0)], s.cs3[block_of(k, n, 1)])
            )
        cs = jnp.concatenate(tables, axis=1)
        cos, sin = cs[0:8], cs[8:16]
        one, zero = jnp.ones((48, 256), F32), jnp.zeros((48, 256), F32)
        tc = jnp.concatenate([cos, cos, one, cos, cos, one], axis=0).T
        ts = jnp.concatenate([-sin, sin, zero, -sin, sin, zero], axis=0).T

        def turn(v):
            return v * tc + jnp.where(early, roll(v, 120), roll(v, 8)) * ts

        left = s.first[2 * m : 2 * m + 2].reshape(256, 1024)
        triple = nn(left, s.was[:, 0:384]) + triple_bias
        query, key, value = turn(triple[:, 0:128]), turn(triple[:, 128:256]), triple[:, 256:384]
        zeros = jnp.zeros_like(value)
        return deal(
            (
                (jnp.where(low, query, roll(key, 64)), jnp.where(low, roll(query, 64), key)),
                (jnp.where(low, value, zeros), jnp.where(low, roll(value, 64), zeros)),
            ),
            s.pk,
            s.th,
            s.pk,
            m,
        )

    heads_in = [attend_in(m) for m in range(4)]
    g_zy = tokens_on_z(g_y, s.gs)

    for m in range(4):
        rows = slice(m * 256, m * 256 + 256)
        u = nn(s.second[rows, :], s.was[:, 384:896]) + expand_bias
        cdf = 0.5 * (1.0 + lax.erf(u * math.sqrt(0.5)))
        pdf = jnp.exp(-0.5 * u * u) * (1.0 / math.sqrt(2.0 * math.pi))
        s.hidden[rows, :] = (u * cdf).astype(BF)
        s.slope[rows, :] = cdf + u * pdf

    wait(heads_in)
    low64 = lanes((64, 128)) < 64

    def place(j, _):
        at = pl.ds(pl.multiple_of(j * 64, 64), 64)
        both = s.pk[inv_slot[j], :, 0:128].astype(F32)
        value = s.pk[inv_slot[j], :, 128:256].astype(F32)
        s.kq[at, :] = roll(both, 64).astype(BF)
        s.qz[at, :] = jnp.where(low64, both * SCALE, 0.0).astype(BF)
        s.vz[at, :] = roll(value, 64).astype(BF)
        return 0

    lax.fori_loop(0, 32, place, 0)
    for i in range(8):
        cols = slice(i * TILE, i * TILE + TILE)
        s.kt[:, cols] = s.kq[cols, :].astype(F32).T[0:64].astype(BF)
        s.vt[:, cols] = s.vz[cols, :].astype(F32).T[64:128].astype(BF)
    seen = lax.broadcasted_iota(jnp.int32, (TILE, TILE), 0) <= lanes((TILE, TILE))

    def folded(v, op):
        parts = [v[j * 8 : j * 8 + 8] for j in range(TILE // 8)]
        while len(parts) > 1:
            parts = [op(parts[j], parts[j + 1]) for j in range(0, len(parts), 2)]
        return parts[0]

    def tile(i, j):
        return i * (i + 1) // 2 + j

    def at_tile(i):
        return slice(i * TILE, i * TILE + TILE)

    for i in range(8):
        cols = at_tile(i)
        q_i = s.qz[cols, :]
        peak = None
        for j in range(i + 1):
            score = nt(s.kq[at_tile(j), :], q_i)
            if j == i:
                score = jnp.where(seen, score, -jnp.inf)
            s.sc[at_tile(j), :] = score
            high = folded(score, jnp.maximum)
            peak = high if peak is None else jnp.maximum(peak, high)
        peak = jnp.max(peak, axis=0, keepdims=True)
        total, mix = jnp.zeros((8, TILE), F32), jnp.zeros((64, TILE), F32)
        for j in range(i + 1):
            e = jnp.exp(s.sc[at_tile(j), :] - peak)
            total += folded(e, jnp.add)
            e_low = e.astype(BF)
            s.es[tile(i, j)] = e_low
            mix += nn(s.vt[:, at_tile(j)], e_low)
        inv = 1.0 / jnp.sum(total, axis=0, keepdims=True)
        mix *= inv
        s.rsum[i : i + 1, :] = inv
        s.mixs[:, cols] = mix
        out = jnp.concatenate([mix, jnp.zeros_like(mix)], axis=0).T
        s.ot[4 * i : 4 * i + 4] = out.astype(BF).reshape(4, 64, 128)
    for n in range(8):
        for j in range(2):
            s.o_own[2 * n + j] = s.ot[block_of(k, n, j)]
            s.o_away[2 * n + j] = s.ot[block_of(1 - k, n, j)]
    o_sent = send(s.o_away, s.o_got, KC)

    act = RowSum(send, s.act, s.act_rz, s.act_ry, s.act_t, s.act_rt, s.act_w, s.act_rw)
    o_sent.wait_recv()
    for m in (2, 3, 1, 0):
        rows = slice(m * 256, m * 256 + 256)
        own = s.o_own[4 * m : 4 * m + 4].reshape(256, 128).astype(F32)
        got = s.o_got[4 * m : 4 * m + 4].reshape(256, 128).astype(F32)
        head0, head1 = jnp.where(k == 0, own, got), jnp.where(k == 0, got, own)
        attn_low = jnp.where(low, head0, roll(head1, 64)).astype(BF)
        s.attn[rows, :] = attn_low
        out = nn(attn_low, s.wos[...]) + nn(s.hidden[rows, :], s.wss[...])
        s.act[2 * m : 2 * m + 2] = out.astype(BF).reshape(2, 128, 1024)
        act.start(2 * m)
        act.start(2 * m + 1)

    g_z[1].wait_recv()
    wait(g_yz.values())
    wait(g_zy.values())
    grads_in = []
    for m in range(4):
        dmix = nt(s.gs[2 * m : 2 * m + 2].reshape(256, 1024), s.wos[...])
        grads_in.append(deal(((dmix, roll(dmix, 64)),), s.pd, s.td, s.pd, m))

    def x_hat_of(m):
        rows = slice(m * 256, m * 256 + 256)
        v = s.xs[2 * m : 2 * m + 2].reshape(256, 1024).astype(F32)
        return (v - s.mus[rows, :]) * s.invs[rows, :]

    for m in range(4):
        rows = slice(m * 256, m * 256 + 256)
        grad = s.gs[2 * m : 2 * m + 2].reshape(256, 1024)
        dexp_low = (nt(grad, s.wss[...]) * s.slope[rows, :]).astype(BF)
        s.dexp[rows, :] = dexp_low
        d_second = nt(dexp_low, s.was[:, 384:896])
        s.dhat[2 * m : 2 * m + 2] = (d_second * g2[...]).astype(BF).reshape(2, 128, 1024)
        s.sm[2:3, :] += down(d_second * x_hat_of(m))
        s.sm[3:4, :] += down(d_second)
        s.sm[4:5, :] += down(grad.astype(F32))
        s.sm[5:6, 384:896] += down(dexp_low.astype(F32))

    gm = WeightSum(send, me, BF, s.gm_r, s.gm_u, s.gm_ru, s.gm_v, s.gm_rv, s.gm_f, s.gm_rf)
    ga = WeightSum(send, me, BF, s.ga_r, s.ga_u, s.ga_ru, s.ga_v, s.ga_rv, s.ga_f, s.ga_rf)
    s.slope[...] = tn(s.second[...], s.dexp[...])
    s.gsh[...] = tn(s.hidden[...], s.gs[...].reshape(1024, 1024))
    for kk in range(2):
        for ff in range(8):
            at = [(tt * 2 + kk) * 64 + ff * 8 for tt in range(8)]
            own = slice((kk * 8 + ff) * 32, (kk * 8 + ff) * 32 + 32)
            s.gm[kk, ff, 0:64, :] = jnp.concatenate(
                [s.slope[r : r + 8, :] for r in at], axis=0
            ).astype(BF)
            s.gm[kk, ff, 64:96, :] = s.gsh[own, 0:512].astype(BF)
            s.gm[kk, ff, 96:128, :] = s.gsh[own, 512:1024].astype(BF)
    gm.core(s.gm)

    wait(grads_in)

    def place_back(j, _):
        at = pl.ds(pl.multiple_of(j * 64, 64), 64)
        s.vz[at, :] = jnp.where(
            low64, s.pd[inv_slot[j]].astype(F32), s.vz[at, :].astype(F32)
        ).astype(BF)
        return 0

    lax.fori_loop(0, 32, place_back, 0)
    for i in range(8):
        cols = at_tile(i)
        s.dt[:, cols] = s.vz[cols, :].astype(F32).T[0:64].astype(BF)
    for i in range(8):
        cols = at_tile(i)
        scaled = (s.dt[:, cols].astype(F32) * s.rsum[i : i + 1, :]).astype(BF).astype(F32)
        inner = jnp.sum(s.mixs[:, cols] * scaled, axis=0, keepdims=True)
        d_i = jnp.concatenate([jnp.zeros_like(scaled), scaled], axis=0).T.astype(BF)
        right = jnp.concatenate([s.qz[cols, :], d_i], axis=0)
        dq = jnp.zeros((64, TILE), F32)
        for j in range(i + 1):
            rows = at_tile(j)
            e_low = s.es[tile(i, j)]
            ds = (e_low.astype(F32) * (nt(s.vz[rows, :], d_i) - inner)).astype(BF)
            both = nn(jnp.concatenate([ds, e_low], axis=1), right)
            s.acc[rows, :] = both if i == j else s.acc[rows, :] + both
            dq += nn(s.kt[:, rows], ds)
        s.mixs[:, cols] = dq * SCALE
        if i == 3:
            gm.along_x()
        if i == 6:
            act.middle()

    def turned_back(v, cols):
        cos, sin = s.cst[0:8, cols], s.cst[8:16, cols]
        f1, f2 = v[0:8], v[8:16]
        return [f1 * cos + f2 * sin, f2 * cos - f1 * sin, v[16:64]]

    for i in range(8):
        cols = at_tile(i)
        tail = s.acc[cols, :]
        both = turned_back(s.mixs[:, cols], cols) + turned_back(tail.T[0:64], cols)
        s.dd[4 * i : 4 * i + 4, :, 0:128] = (
            jnp.concatenate(both, axis=0).T.astype(BF).reshape(4, 64, 128)
        )
        s.dd[4 * i : 4 * i + 4, :, 128:256] = tail.astype(BF).reshape(4, 64, 128)
    for n in range(8):
        for j in range(2):
            s.d_own[2 * n + j] = s.dd[block_of(k, n, j)]
            s.d_away[2 * n + j] = s.dd[block_of(1 - k, n, j)]
    d_sent = send(s.d_away, s.d_got, KC)

    dhat = RowSum(
        send, s.dhat, s.dhat_rz, s.dhat_ry, s.dhat_t, s.dhat_rt, s.dhat_w, s.dhat_rw
    )
    d_sent.wait_recv()
    for m in (2, 3, 1, 0):
        rows = slice(m * 256, m * 256 + 256)
        quads = slice(4 * m, 4 * m + 4)
        tiles = []
        for at in (slice(0, 128), slice(128, 256)):
            own = s.d_own[quads, :, at].reshape(256, 128).astype(F32)
            got = s.d_got[quads, :, at].reshape(256, 128).astype(F32)
            tiles.append((jnp.where(k == 0, own, got), jnp.where(k == 0, got, own)))
        (p_0, p_1), (r_0, r_1) = tiles
        turned = jnp.concatenate(
            [
                jnp.where(low, p_0, roll(p_1, 64)),
                jnp.where(low, roll(p_0, 64), p_1),
                jnp.where(low, roll(r_0, 64), r_1),
            ],
            axis=1,
        )
        turned_low = turned.astype(BF)
        s.dtr[rows, :] = turned_low
        d_first = nt(turned_low, s.was[:, 0:384])
        before = s.dhat[2 * m : 2 * m + 2].reshape(256, 1024).astype(F32)
        s.dhat[2 * m : 2 * m + 2] = (
            (before + d_first * g1[...]).astype(BF).reshape(2, 128, 1024)
        )
        dhat.start(2 * m)
        dhat.start(2 * m + 1)
        s.sm[0:1, :] += down(d_first * x_hat_of(m))
        s.sm[1:2, :] += down(d_first)
        s.sm[5:6, 0:384] += down(turned)

    sm_core = send(s.sm, s.sm_r, KC)
    s.slope[:, 0:384] = tn(s.first[...].reshape(1024, 1024), s.dtr[...])
    s.go[...] = tn(s.attn[...], s.gs[...].reshape(1024, 1024))
    for kk in range(2):
        for ff in range(8):
            at = [(tt * 2 + kk) * 64 + ff * 8 for tt in range(8)]
            r = (kk * 8 + ff) * 8
            s.ga[kk, ff, :, 0:384] = jnp.concatenate(
                [s.slope[q : q + 8, 0:384] for q in at], axis=0
            ).astype(BF)
            s.ga[kk, ff, :, 384:512] = jnp.concatenate(
                [s.go[r : r + 8, j * 128 : j * 128 + 128] for j in range(8)], axis=0
            ).astype(BF)
    ga.core(s.ga)
    gm.along_z()
    sm_core.wait_recv()
    s.sm_u[...] = s.sm[...] + s.sm_r[...]
    sm_x = [send(s.sm_u, s.sm_ru.at[j], XS[i]) for j, i in enumerate(NEAR_FIRST)]
    ga.along_x()
    total = gm.total()
    for j in range(8):
        s.gm_f[j] = total[j * 8 : j * 8 + 8, :]
    gsw_o[:, 0:512] = total[64:96, :]
    gsw_o[:, 512:1024] = total[96:128, :]
    gm.to_owners()
    wait(sm_x)
    s.sm_v[...] = s.sm_u[...] + s.sm_ru[0] + s.sm_ru[1] + s.sm_ru[2]
    sm_zh = send(s.sm_v, s.sm_rv, ZH)
    act_o[...] = (s.xs[0].astype(F32) + bias[...] + act.end()).astype(BF)
    dhat.middle()
    ga.along_z()
    sm_zh.wait_recv()
    total = s.sm_v[...] + s.sm_rv[...]
    for j in range(8):
        s.sm_f[j, 0:4, :] = total[0:4, j * 128 : j * 128 + 128]
        s.sm_f[j, 4:5, :] = total[5:6, 0:128]
        s.sm_f[j, 5:6, :] = total[5:6, 128:256]
        s.sm_f[j, 6:7, :] = total[4:5, j * 128 : j * 128 + 128]
        s.sm_f[j, 7:8, :] = total[5:6, 256:384]
    small_o[8:12, :] = jnp.concatenate(
        [total[5:6, 384 + j * 128 : 512 + j * 128] for j in range(4)], axis=0
    )
    small_o[12:16, :] = jnp.zeros((4, 128), F32)
    sm = WeightSum(send, me, F32, None, None, None, None, None, s.sm_f, s.sm_rf)
    sm.to_owners()
    total = ga.total()
    for j in range(8):
        s.ga_f[j] = total[j * 8 : j * 8 + 8, 0:384]
        gow_o[:, j * 128 : j * 128 + 128] = total[j * 8 : j * 8 + 8, 384:512]
    ga.to_owners()
    d_hat = dhat.end()
    inv = s.invs[0:128, :]
    x_hat = (s.xs[0].astype(F32) - s.mus[0:128, :]) * inv
    tok_o[...] = s.gs[0].astype(F32) + inv * (
        d_hat
        - jnp.mean(d_hat, axis=1, keepdims=True)
        - x_hat * jnp.mean(d_hat * x_hat, axis=1, keepdims=True)
    )
    gm.wait()
    for n in range(8):
        gew_o[:, pl.ds(pl.multiple_of(chip_at(n) * 512, 512), 512)] = s.gm_rf[n]
    sm.wait()
    total = s.sm_rf[0]
    for n in range(1, 8):
        total += s.sm_rf[n]
    small_o[0:4, :] = total[0:4, :]
    source = lax.rem(2 * t + k, 8)
    bias_rows = jnp.zeros((2, 128), F32)
    for n in range(8):
        bias_rows = jnp.where(chip_at(n) == source, s.sm_rf[n, 4:6, :], bias_rows)
    small_o[4:5, :] = jnp.where(a == 0, bias_rows[0:1], bias_rows[1:2])
    small_o[5:6, :] = s.sm_f[t, 6:7, :]
    small_o[6:7, :] = s.sm_f[t, 7:8, :]
    small_o[7:8, :] = jnp.zeros((1, 128), F32)
    ga.wait()
    for n in range(8):
        for o in range(3):
            at = pl.ds(pl.multiple_of(o * 1024 + chip_at(n) * 128, 128), 128)
            gtw_o[:, at] = s.ga_rf[n, :, o * 128 : o * 128 + 128]
    send.finish()


def block(pairs, pos, x, g, tw, ow, ew, sw, tb, eb, g1, b1, g2, b2, bias):
    return pl.pallas_call(
        block_kernel,
        out_shape=(
            jax.ShapeDtypeStruct((128, 1024), BF),
            jax.ShapeDtypeStruct((128, 1024), F32),
            jax.ShapeDtypeStruct((8, 3072), F32),
            jax.ShapeDtypeStruct((8, 4096), F32),
            jax.ShapeDtypeStruct((8, 1024), F32),
            jax.ShapeDtypeStruct((32, 1024), F32),
            jax.ShapeDtypeStruct((16, 128), F32),
        ),
        in_specs=[pl.BlockSpec(memory_space=pltpu.SMEM), VM] + [ANY] * 6 + [VM] * 7,
        out_specs=(VM,) * 7,
        scratch_shapes=[pltpu.VMEM(shape, kind) for _, shape, kind in SCRATCH]
        + [
            pltpu.SemaphoreType.DMA((COPIES,)),
            pltpu.SemaphoreType.DMA((COPIES,)),
            pltpu.SemaphoreType.DMA((LOADS,)),
            pltpu.SMEM((32,), jnp.int32),
        ],
        compiler_params=pltpu.CompilerParams(
            collective_id=0, has_side_effects=True, vmem_limit_bytes=62 * MIB
        ),
        name="block",
    )(pairs, pos, x, g, tw, ow, ew, sw, tb, eb, g1, b1, g2, b2, bias)


def shards(
    tokens_in,
    positions,
    block_pairs,
    first_gain,
    first_bias,
    second_gain,
    second_bias,
    triple_weight,
    triple_bias,
    output_weight,
    output_bias,
    expand_weight,
    expand_bias,
    shrink_weight,
    shrink_bias,
    cotangent,
):
    c = lax.axis_index("ctx")
    k = c % 2
    x, g = tokens_in.reshape(128, 1024), cotangent.reshape(128, 1024)

    def cut(v, at, size, dim):
        return lax.dynamic_slice_in_dim(v, at, size, dim)

    def line(v):
        return v.reshape(1, -1)

    act, tok, gtw, gew, gow, gsw, small = block(
        block_pairs.T,
        positions,
        x,
        g,
        triple_weight,
        output_weight,
        expand_weight,
        shrink_weight,
        line(triple_bias),
        line(expand_bias),
        line(first_gain),
        line(first_bias),
        line(second_gain),
        line(second_bias),
        line(output_bias + shrink_bias),
    )
    f = lax.axis_index("fsdp")
    eight = cut(small, k * 64 + f * 8, 8, 1)
    sixteen = cut(small[4], f * 16, 16, 0)
    wide = cut(small[8:12].reshape(512), k * 256 + f * 32, 32, 0)
    return (
        act.reshape(tokens_in.shape),
        tok.reshape(tokens_in.shape),
        eight[0],
        eight[1],
        eight[2],
        eight[3],
        gtw,
        sixteen,
        eight[6],
        gow,
        eight[5],
        gew,
        wide,
        gsw,
        eight[5],
    )


def solution(mesh):
    return jax.shard_map(
        shards,
        mesh=mesh,
        in_specs=(
            P("fsdp", "ctx", None, None, None),
            P("fsdp", None),
            P(),
            P(),
            P(),
            P(),
            P(),
            P("fsdp", None),
            P(),
            P(None, "fsdp"),
            P(),
            P("fsdp", None),
            P(),
            P(None, "fsdp"),
            P(),
            P("fsdp", "ctx", None, None, None),
        ),
        out_specs=(
            P("fsdp", "ctx", None, None, None),
            P("fsdp", "ctx", None, None, None),
            P(("ctx", "fsdp")),
            P(("ctx", "fsdp")),
            P(("ctx", "fsdp")),
            P(("ctx", "fsdp")),
            P(("ctx", "fsdp"), None),
            P(("ctx", "fsdp")),
            P(("ctx", "fsdp")),
            P(("ctx", "fsdp"), None),
            P(("ctx", "fsdp")),
            P(("ctx", "fsdp"), None),
            P(("ctx", "fsdp")),
            P(("ctx", "fsdp"), None),
            P(("ctx", "fsdp")),
        ),
        check_vma=False,
    )
```

```python
import math

import jax
import jax.numpy as jnp
import numpy as np
from jax import lax
from jax.experimental import pallas as pl
from jax.experimental.pallas import tpu as pltpu
from jax.sharding import PartitionSpec as P

MESH = pl.DeviceIdType.MESH
BF, F32 = jnp.bfloat16, jnp.float32
EPS = 1e-05
BASE = 10000.0
MIB = 1 << 20
SCALE = 0.125
TILE = 256
RATES = 1.0 / BASE ** (np.arange(0, 16, 2, dtype=np.float32) / 16)

ZL, KC, ZH = (1, 0, 0, 0, 0), (0, 0, 1, 0, 0), (0, 0, 0, 0, 1)
YS = {i: (0, i, 0, 0, 0) for i in (1, 2, 3)}
XS = {i: (0, 0, 0, i, 0) for i in (1, 2, 3)}
NEAR_FIRST = (1, 3, 2)
OFFS = ((0, 0), (0, 1), (0, 3), (0, 2), (1, 0), (1, 1), (1, 3), (1, 2))
SLOT = {off: n for n, off in enumerate(OFFS)}


def origin(da, i):
    return SLOT[(da, (4 - i) % 4)]


def chips(n):
    return (*OFFS[n], 0, 0, 0)


def coords():
    c, f = lax.axis_index("ctx"), lax.axis_index("fsdp")
    return lax.div(c, 8), lax.rem(lax.div(c, 2), 4), lax.rem(c, 2), lax.div(f, 2), lax.rem(f, 2)


def device_at(me, off):
    a, b, k, x, h = (lax.rem(p + o, n) for p, o, n in zip(me, off, (2, 4, 2, 4, 2)))
    return ((a * 4 + b) * 2 + k, x * 2 + h)


def barrier(me, offs):
    sem = pltpu.get_barrier_semaphore()
    for off in offs:
        pl.semaphore_signal(sem, inc=1, device_id=device_at(me, off), device_id_type=MESH)
    pl.semaphore_wait(sem, len(offs))


class Sender:
    def __init__(self, me, send_sems, recv_sems):
        self.me, self.send_sems, self.recv_sems, self.copies = me, send_sems, recv_sems, []

    def __call__(self, src, dst, off):
        i = len(self.copies)
        copy = pltpu.make_async_remote_copy(
            src_ref=src,
            dst_ref=dst,
            send_sem=self.send_sems.at[i],
            recv_sem=self.recv_sems.at[i],
            device_id=device_at(self.me, off),
            device_id_type=MESH,
        )
        copy.start()
        self.copies.append(copy)
        return copy

    def finish(self):
        for copy in self.copies:
            copy.wait_send()


def nt(left, right):
    return lax.dot_general(left, right, (((1,), (1,)), ((), ())), preferred_element_type=F32)


def tn(left, right):
    return lax.dot_general(left, right, (((0,), (0,)), ((), ())), preferred_element_type=F32)


def nn(left, right):
    return jnp.dot(left, right, preferred_element_type=F32)


def down(v):
    return jnp.sum(v, axis=0, keepdims=True)


def lanes(shape):
    return lax.broadcasted_iota(jnp.int32, shape, 1)


def roll(v, shift):
    return pltpu.roll(v, shift, 1)


ANY = pl.BlockSpec(memory_space=pl.ANY)
VM = pl.BlockSpec(memory_space=pltpu.VMEM)


COPIES = 60 + 28 + 10 + 28 + 10 + 5 + 21
LOADS = 8
SPLIT = 32
TOK = (8, 128, 1024)
SCRATCH = (
    ("xs", TOK, BF),
    ("gs", TOK, BF),
    ("first", TOK, BF),
    ("second", (1024, 1024), BF),
    ("mus", (1024, 1), F32),
    ("invs", (1024, 1), F32),
    ("was", (1024, 896), BF),
    ("wos", (128, 1024), BF),
    ("wss", (512, 1024), BF),
    ("slope", (1024, 512), F32),
    ("hidden", (1024, 512), BF),
    ("dexp", (1024, 512), BF),
    ("cst", (16, 2048), F32),
    ("cs3", (32, 16, 128), F32),
    ("pk", (32, 64, 256), BF),
    ("th", (16, 64, 256), BF),
    ("pd", (32, 64, 128), BF),
    ("td", (16, 64, 128), BF),
    ("kv", (2048, 128), BF),
    ("qz", (2048, 128), BF),
    ("kvt", (128, 2048), BF),
    ("dt", (64, 2048), BF),
    ("sc", (2048, TILE), F32),
    ("es", (36, TILE, TILE), BF),
    ("acc", (2048, 128), F32),
    ("mixs", (64, 2048), F32),
    ("rsum", (8, TILE), F32),
    ("ot", (32, 64, 128), BF),
    ("o_own", (16, 64, 128), BF),
    ("o_away", (16, 64, 128), BF),
    ("o_got", (16, 64, 128), BF),
    ("dd", (32, 64, 256), BF),
    ("d_own", (16, 64, 256), BF),
    ("d_away", (16, 64, 256), BF),
    ("d_got", (16, 64, 256), BF),
    ("attn", (1024, 128), BF),
    ("dtr", (1024, 384), BF),
    ("act", TOK, BF),
    ("act_rz", (4, 64, 1024), BF),
    ("act_ry", (2, 3, 64, 1024), BF),
    ("act_t", (4, 64, 1024), BF),
    ("act_rt", (3, 64, 1024), BF),
    ("act_w", (64, 1024), BF),
    ("act_rw", (64, 1024), BF),
    ("dhat", TOK, BF),
    ("dhat_rz", (4, SPLIT, 1024), BF),
    ("dhat_ry", (2, 3, 128 - SPLIT, 1024), BF),
    ("dhat_t", (4, SPLIT, 1024), BF),
    ("dhat_rt", (3, SPLIT, 1024), BF),
    ("dhat_w", (128 - SPLIT, 1024), BF),
    ("dhat_rw", (128 - SPLIT, 1024), BF),
    ("gsh", (512, 1024), F32),
    ("gm", (2, 8, 128, 512), BF),
    ("gm_r", (8, 128, 512), BF),
    ("gm_u", (8, 128, 512), BF),
    ("gm_ru", (3, 2, 128, 512), BF),
    ("gm_v", (2, 128, 512), BF),
    ("gm_rv", (128, 512), BF),
    ("gm_f", (8, 8, 512), F32),
    ("gm_rf", (8, 8, 512), F32),
    ("go", (128, 1024), F32),
    ("ga", (2, 8, 64, 512), BF),
    ("ga_r", (8, 64, 512), BF),
    ("ga_u", (8, 64, 512), BF),
    ("ga_ru", (3, 2, 64, 512), BF),
    ("ga_v", (2, 64, 512), BF),
    ("ga_rv", (64, 512), BF),
    ("ga_f", (8, 8, 384), F32),
    ("ga_rf", (8, 8, 384), F32),
    ("sm", (8, 1024), F32),
    ("sm_r", (8, 1024), F32),
    ("sm_u", (8, 1024), F32),
    ("sm_ru", (3, 8, 1024), F32),
    ("sm_v", (8, 1024), F32),
    ("sm_rv", (8, 1024), F32),
    ("sm_f", (8, 8, 128), F32),
    ("sm_rf", (8, 8, 128), F32),
)
ZR, YR = slice(0, 64), slice(64, 128)


class Refs:
    pass


class RowSum:
    def __init__(self, send, src, rz, ry, t, rt, w, rw):
        self.send, self.src = send, src
        self.zr, self.yr = slice(0, rz.shape[1]), slice(rz.shape[1], 128)
        self.rz, self.ry, self.t, self.rt, self.w, self.rw = rz, ry, t, rt, w, rw
        self.z, self.y, self.on = {}, {}, []

    def start(self, n):
        da, db = OFFS[n]
        if da:
            self.z[n - 4] = self.send(self.src.at[n, self.zr], self.rz.at[n - 4], ZL)
        if db:
            j = NEAR_FIRST.index(db)
            self.y[n] = self.send(self.src.at[n, self.yr], self.ry.at[da, j], YS[db])

    def middle(self):
        for m in (1, 2, 3):
            self.z[m].wait_recv()
            self.t[m] = (self.src[m, self.zr].astype(F32) + self.rz[m].astype(F32)).astype(BF)
            db = OFFS[m][1]
            j = NEAR_FIRST.index(db)
            self.on.append(self.send(self.t.at[m], self.rt.at[j], YS[db]))
        for n in (5, 6, 7):
            self.y[n].wait_recv()
        total = self.src[4, self.yr].astype(F32)
        for j in range(3):
            total += self.ry[1, j].astype(F32)
        self.w[...] = total.astype(BF)
        self.on.append(self.send(self.w, self.rw, ZL))

    def end(self):
        self.z[0].wait_recv()
        for n in (1, 2, 3):
            self.y[n].wait_recv()
        for copy in self.on:
            copy.wait_recv()
        upper = self.src[0, self.zr].astype(F32) + self.rz[0].astype(F32)
        lower = self.src[0, self.yr].astype(F32) + self.rw[...].astype(F32)
        for j in range(3):
            upper += self.rt[j].astype(F32)
            lower += self.ry[0, j].astype(F32)
        return jnp.concatenate([upper, lower], axis=0)


class WeightSum:
    def __init__(self, send, me, kind, r, u, ru, v, rv, f, rf):
        self.send, self.me, self.kind = send, me, kind
        self.r, self.u, self.ru, self.v, self.rv, self.f, self.rf = r, u, ru, v, rv, f, rf

    def core(self, src):
        self.src = src
        self.sent = [self.send(src.at[1 - self.me[2]], self.r, KC)]

    def wait(self):
        for copy in self.sent:
            copy.wait_recv()

    def along_x(self):
        k, x = self.me[2], self.me[3]
        self.wait()

        def one(f, _):
            self.u[f] = (self.src[k, f].astype(F32) + self.r[f].astype(F32)).astype(self.kind)
            return 0

        lax.fori_loop(0, 8, one, 0)
        self.sent = []
        for j, i in enumerate(NEAR_FIRST):
            there = pl.ds(lax.rem(x + i, 4) * 2, 2)
            self.sent.append(self.send(self.u.at[there], self.ru.at[j], XS[i]))

    def along_z(self):
        x, h = self.me[3], self.me[4]
        self.wait()
        for hh in range(2):
            total = self.u[x * 2 + hh].astype(F32)
            for j in range(3):
                total += self.ru[j, hh].astype(F32)
            self.v[hh] = total.astype(self.kind)
        self.sent = [self.send(self.v.at[1 - h], self.rv, ZH)]

    def total(self):
        self.wait()
        return self.v[self.me[4]].astype(F32) + self.rv[...].astype(F32)

    def to_owners(self):
        a, b = self.me[0], self.me[1]
        self.sent = []
        for n in range(1, 8):
            da, db = OFFS[n]
            there = lax.rem(a + da, 2) * 4 + lax.rem(b + db, 4)
            self.sent.append(self.send(self.f.at[there], self.rf.at[origin(da, db)], chips(n)))
        self.rf[0] = self.f[a * 4 + b]


def block_kernel(
    pairs, pos, x, g, tw, ow, ew, sw, tb, eb, g1, b1, g2, b2, ob, sb,
    act_o, tok_o, gtw_o, gew_o, gow_o, gsw_o, small_o, *scratch,
):
    s = Refs()
    for (name, _, _), ref in zip(SCRATCH, scratch):
        setattr(s, name, ref)
    ss, rs, ls, inv_slot = scratch[len(SCRATCH) :]
    me = coords()
    a, b, k, xx, h = me
    t, f = a * 4 + b, xx * 2 + h
    local = []

    def load(src, dst):
        copy = pltpu.make_async_copy(src, dst, ls.at[len(local)])
        copy.start()
        local.append(copy)

    def cols_at(ff):
        return pl.ds(pl.multiple_of(ff * 128, 128), 128)

    def pieces(ff):
        rows = pl.ds(pl.multiple_of(ff * 128 + k * 64, 64), 64)
        return (
            s.was.at[rows, 0:384],
            s.was.at[rows, 384:896],
            s.wos.at[pl.ds(pl.multiple_of(k * 64, 64), 64), cols_at(ff)],
            s.wss.at[pl.ds(pl.multiple_of(k * 256, 256), 256), cols_at(ff)],
        )

    half = pl.ds(pl.multiple_of(k * 64, 64), 64)
    mine = pl.ds(pl.multiple_of(f * 128 + k * 64, 64), 64)
    for o in range(3):
        load(
            tw.at[half, pl.ds(pl.multiple_of(o * 1024 + t * 128, 128), 128)],
            s.was.at[mine, pl.ds(o * 128, 128)],
        )
    load(ew.at[half, pl.ds(pl.multiple_of(t * 512, 512), 512)], s.was.at[mine, pl.ds(384, 512)])
    load(ow.at[pl.ds(pl.multiple_of(t * 128 + k * 64, 64), 64)], pieces(f)[2])
    load(sw.at[pl.ds(pl.multiple_of(t * 512 + k * 256, 256), 256)], pieces(f)[3])
    load(x, s.xs.at[0])
    load(g, s.gs.at[0])
    barrier(me, [*(chips(n) for n in range(1, 8)), *XS.values(), ZH, KC])
    send = Sender(me, ss, rs)

    def send_pieces(ff, off):
        return [send(ref, ref, off) for ref in pieces(ff)]

    def wait(copies):
        for copy in copies:
            copy.wait_recv()

    def tokens_out(src, dst):
        z = [send(src.at[ZR], dst.at[4, ZR], ZL)]
        y = {i: [send(src.at[YR], dst.at[origin(0, i), YR], YS[i])] for i in NEAR_FIRST}
        z.append(send(src.at[YR], dst.at[4, YR], ZL))
        for i in NEAR_FIRST:
            y[i].append(send(src.at[ZR], dst.at[origin(0, i), ZR], YS[i]))
        return z, y

    def tokens_on_y(z, dst):
        z[0].wait_recv()
        return {i: send(dst.at[4, ZR], dst.at[origin(1, i), ZR], YS[i]) for i in NEAR_FIRST}

    def tokens_on_z(y, dst):
        on = {}
        for i in NEAR_FIRST:
            y[i][0].wait_recv()
            on[i] = send(dst.at[origin(0, i), YR], dst.at[origin(1, i), YR], ZL)
        return on

    for copy in local:
        copy.wait()
    ways = {0: ZH, **XS}
    w_own = {i: [send(pieces(f)[0], pieces(f)[0], ways[i])] for i in (0, *NEAR_FIRST)}
    x_z, x_y = tokens_out(x, s.xs)
    for i in (0, *NEAR_FIRST):
        w_own[i] += [send(ref, ref, ways[i]) for ref in pieces(f)[1:]]
    wz, wx = w_own[0], w_own
    weights = [send_pieces(f, KC)]

    def chip_at(n):
        da, db = OFFS[n]
        return lax.rem(a + da, 2) * 4 + lax.rem(b + db, 4)

    def block_of(kk, n, j):
        return pairs[j, chip_at(n) * 2 + kk]

    held = [block_of(kk, n, j) for kk in range(2) for n in range(8) for j in range(2)]

    def find(j, _):
        at = jnp.int32(0)
        for q, block in enumerate(held):
            at = jnp.where(block == j, q, at)
        inv_slot[j] = at
        return 0

    lax.fori_loop(0, 32, find, 0)
    row = lax.broadcasted_iota(jnp.int32, (8, 1), 0)
    rates = jnp.zeros((8, 1), F32)
    for j in range(8):
        rates = jnp.where(row == j, float(RATES[j]), rates)
    angles = rates * pos[...].astype(F32)
    s.cst[0:8, :] = jnp.cos(angles)
    s.cst[8:16, :] = jnp.sin(angles)
    low16 = lanes((16, 128)) < 64
    for j in range(16):
        both = s.cst[:, j * 128 : j * 128 + 128]
        turned = roll(both, 64)
        s.cs3[2 * j] = jnp.where(low16, both, turned)
        s.cs3[2 * j + 1] = jnp.where(low16, turned, both)
    s.sm[...] = jnp.zeros_like(s.sm)

    def norm(n):
        rows = slice(n * 128, n * 128 + 128)
        v = s.xs[n].astype(F32)
        mean = jnp.mean(v, axis=1, keepdims=True)
        centred = v - mean
        inv = lax.rsqrt(jnp.mean(centred * centred, axis=1, keepdims=True) + EPS)
        s.mus[rows, :] = mean
        s.invs[rows, :] = inv
        x_hat = centred * inv
        s.first[n] = (x_hat * g1[...] + b1[...]).astype(BF)
        s.second[rows, :] = (x_hat * g2[...] + b2[...]).astype(BF)

    norm(0)
    fz = xx * 2 + (1 - h)
    wz[0].wait_recv()
    wxz = {i: [send(pieces(fz)[0], pieces(fz)[0], XS[i])] for i in NEAR_FIRST}
    x_yz = tokens_on_y(x_z, s.xs)
    x_zy = tokens_on_z(x_y, s.xs)
    wait(wz[1:])
    for i in NEAR_FIRST:
        wxz[i] += [send(ref, ref, XS[i]) for ref in pieces(fz)[1:]]
    weights.append(send_pieces(fz, KC))
    g_z, g_y = tokens_out(g, s.gs)

    low = lanes((256, 128)) < 64
    low128 = lanes((16, 128)) < 64
    early = (lanes((256, 128)) & 63) < 8
    bias_at = [tb[0:1, pl.ds(pl.multiple_of(o * 1024 + t * 128, 128), 128)] for o in range(3)]
    triple_bias = jnp.concatenate(bias_at, axis=1)
    expand_bias = eb[0:1, pl.ds(pl.multiple_of(t * 512, 512), 512)]

    def deal(tiles, own, away, to, m):
        quads = pl.ds(4 * m, 4)
        for j, (head0, head1) in enumerate(tiles):
            at = slice(j * 128, j * 128 + 128)
            keep = jnp.where(k == 0, head0, head1).astype(BF).reshape(4, 64, 128)
            give = jnp.where(k == 0, head1, head0).astype(BF).reshape(4, 64, 128)
            own[pl.ds(k * 16 + 4 * m, 4), :, at] = keep
            away[quads, :, at] = give
        return send(away.at[quads], to.at[pl.ds(k * 16 + 4 * m, 4)], KC)

    def attend_in(m):
        rows = slice(m * 256, m * 256 + 256)
        tables = []
        for n in (2 * m, 2 * m + 1):
            tables.append(
                jnp.where(low128, s.cs3[block_of(k, n, 0)], s.cs3[block_of(k, n, 1)])
            )
        cs = jnp.concatenate(tables, axis=1)
        cos, sin = cs[0:8], cs[8:16]
        one, zero = jnp.ones((48, 256), F32), jnp.zeros((48, 256), F32)
        tc = jnp.concatenate([cos, cos, one, cos, cos, one], axis=0).T
        ts = jnp.concatenate([-sin, sin, zero, -sin, sin, zero], axis=0).T

        def turn(v):
            return v * tc + jnp.where(early, roll(v, 120), roll(v, 8)) * ts

        left = s.first[2 * m : 2 * m + 2].reshape(256, 1024)
        triple = nn(left, s.was[:, 0:384]) + triple_bias
        query, key, value = turn(triple[:, 0:128]), turn(triple[:, 128:256]), triple[:, 256:384]
        query *= SCALE
        zeros = jnp.zeros_like(value)
        return deal(
            (
                (jnp.where(low, key, roll(value, 64)), jnp.where(low, roll(key, 64), value)),
                (jnp.where(low, query, zeros), jnp.where(low, roll(query, 64), zeros)),
            ),
            s.pk,
            s.th,
            s.pk,
            m,
        )

    def forward_in(m):
        rows = slice(m * 256, m * 256 + 256)
        u = nn(s.second[rows, :], s.was[:, 384:896]) + expand_bias
        cdf = 0.5 * (1.0 + lax.erf(u * math.sqrt(0.5)))
        pdf = jnp.exp(-0.5 * u * u) * (1.0 / math.sqrt(2.0 * math.pi))
        s.hidden[rows, :] = (u * cdf).astype(BF)
        s.slope[rows, :] = cdf + u * pdf

    def weights_on(i, which, hh):
        wait(which[i])
        weights.append(send_pieces(lax.rem(xx + 4 - i, 4) * 2 + hh, KC))

    for i, n in ((3, 1), (1, 2), (2, 3)):
        x_y[i][1].wait_recv()
        norm(n)
    for i in NEAR_FIRST:
        weights_on(i, wx, h)
    x_z[1].wait_recv()
    norm(4)
    for i in NEAR_FIRST:
        weights_on(i, wxz, 1 - h)
    for copies in weights:
        copies[0].wait_recv()
    heads_in = [attend_in(0), attend_in(1)]
    for copies in weights:
        wait(copies[1:])
    forward_in(0)
    forward_in(1)
    g_yz = tokens_on_y(g_z, s.gs)
    for i, n in ((3, 5), (1, 6), (2, 7)):
        x_yz[i].wait_recv()
        x_zy[i].wait_recv()
        norm(n)
    heads_in += [attend_in(2), attend_in(3)]
    forward_in(2)
    forward_in(3)

    wait(heads_in)
    def place(j, _):
        at = pl.ds(pl.multiple_of(j * 64, 64), 64)
        s.kv[at, :] = s.pk[inv_slot[j], :, 0:128]
        s.qz[at, :] = s.pk[inv_slot[j], :, 128:256]
        return 0

    lax.fori_loop(0, 32, place, 0, unroll=4)
    for i in range(8):
        cols = slice(i * TILE, i * TILE + TILE)
        s.kvt[:, cols] = s.kv[cols, :].astype(F32).T.astype(BF)
    seen = lax.broadcasted_iota(jnp.int32, (TILE, TILE), 0) <= lanes((TILE, TILE))

    def folded(v, op):
        parts = [v[j * 8 : j * 8 + 8] for j in range(TILE // 8)]
        while len(parts) > 1:
            parts = [op(parts[j], parts[j + 1]) for j in range(0, len(parts), 2)]
        return parts[0]

    def tile(i, j):
        return i * (i + 1) // 2 + j

    def at_tile(i):
        return slice(i * TILE, i * TILE + TILE)

    for i in range(8):
        cols = at_tile(i)
        q_i = s.qz[cols, :]
        peak = None
        for j in range(i + 1):
            score = nt(s.kv[at_tile(j), :], q_i)
            if j == i:
                score = jnp.where(seen, score, -jnp.inf)
            s.sc[at_tile(j), :] = score
            high = folded(score, jnp.maximum)
            peak = high if peak is None else jnp.maximum(peak, high)
        peak = jnp.max(peak, axis=0, keepdims=True)
        total, mix = jnp.zeros((8, TILE), F32), jnp.zeros((64, TILE), F32)
        for j in range(i + 1):
            e = jnp.exp(s.sc[at_tile(j), :] - peak)
            total += folded(e, jnp.add)
            e_low = e.astype(BF)
            s.es[tile(i, j)] = e_low
            mix += nn(s.kvt[64:128, at_tile(j)], e_low)
        inv = 1.0 / jnp.sum(total, axis=0, keepdims=True)
        mix *= inv
        s.rsum[i : i + 1, :] = inv
        s.mixs[:, cols] = mix
        out = jnp.concatenate([mix, jnp.zeros_like(mix)], axis=0).T
        s.ot[4 * i : 4 * i + 4] = out.astype(BF).reshape(4, 64, 128)
        if i == 3:
            g_zy = tokens_on_z(g_y, s.gs)
    for n in range(8):
        for j in range(2):
            s.o_own[2 * n + j] = s.ot[block_of(k, n, j)]
            s.o_away[2 * n + j] = s.ot[block_of(1 - k, n, j)]
    o_sent = send(s.o_away, s.o_got, KC)

    act = RowSum(send, s.act, s.act_rz, s.act_ry, s.act_t, s.act_rt, s.act_w, s.act_rw)
    o_sent.wait_recv()
    for m in (2, 3, 1, 0):
        rows = slice(m * 256, m * 256 + 256)
        own = s.o_own[4 * m : 4 * m + 4].reshape(256, 128).astype(F32)
        got = s.o_got[4 * m : 4 * m + 4].reshape(256, 128).astype(F32)
        head0, head1 = jnp.where(k == 0, own, got), jnp.where(k == 0, got, own)
        attn_low = jnp.where(low, head0, roll(head1, 64)).astype(BF)
        s.attn[rows, :] = attn_low
        out = nn(attn_low, s.wos[...]) + nn(s.hidden[rows, :], s.wss[...])
        s.act[2 * m : 2 * m + 2] = out.astype(BF).reshape(2, 128, 1024)
        act.start(2 * m)
        act.start(2 * m + 1)

    def back_to_heads(p):
        dmix = nt(s.gs[4 * p : 4 * p + 4].reshape(512, 1024), s.wos[...])
        for m in (2 * p, 2 * p + 1):
            part = dmix[(m - 2 * p) * 256 : (m - 2 * p) * 256 + 256]
            grads_in.append(deal(((part, roll(part, 64)),), s.pd, s.td, s.pd, m))

    def x_hat_of(m):
        rows = slice(m * 256, m * 256 + 256)
        v = s.xs[2 * m : 2 * m + 2].reshape(256, 1024).astype(F32)
        return (v - s.mus[rows, :]) * s.invs[rows, :]

    def forward_back(p):
        half = slice(p * 512, p * 512 + 512)
        d_hidden = nt(s.gs[4 * p : 4 * p + 4].reshape(512, 1024), s.wss[...])
        s.dexp[half, :] = (d_hidden * s.slope[half, :]).astype(BF)
        d_second = nt(s.dexp[half, :], s.was[:, 384:896])
        for m in (2 * p, 2 * p + 1):
            rows = slice(m * 256, m * 256 + 256)
            part = d_second[(m - 2 * p) * 256 : (m - 2 * p) * 256 + 256]
            s.dhat[2 * m : 2 * m + 2] = (part * g2[...]).astype(BF).reshape(2, 128, 1024)
            s.sm[2:3, :] += down(part * x_hat_of(m))
            s.sm[3:4, :] += down(part)
            s.sm[4:5, :] += down(s.gs[2 * m : 2 * m + 2].reshape(256, 1024).astype(F32))
            s.sm[5:6, 384:896] += down(s.dexp[rows, :].astype(F32))

    grads_in = []
    for i in NEAR_FIRST:
        g_y[i][1].wait_recv()
    back_to_heads(0)
    forward_back(0)
    g_z[1].wait_recv()
    wait(g_yz.values())
    wait(g_zy.values())
    back_to_heads(1)
    forward_back(1)

    gm = WeightSum(send, me, BF, s.gm_r, s.gm_u, s.gm_ru, s.gm_v, s.gm_rv, s.gm_f, s.gm_rf)
    ga = WeightSum(send, me, BF, s.ga_r, s.ga_u, s.ga_ru, s.ga_v, s.ga_rv, s.ga_f, s.ga_rf)
    s.slope[...] = tn(s.second[...], s.dexp[...])
    s.gsh[...] = tn(s.hidden[...], s.gs[...].reshape(1024, 1024))
    for kk in range(2):
        for ff in range(8):
            at = [(tt * 2 + kk) * 64 + ff * 8 for tt in range(8)]
            own = slice((kk * 8 + ff) * 32, (kk * 8 + ff) * 32 + 32)
            s.gm[kk, ff, 0:64, :] = jnp.concatenate(
                [s.slope[r : r + 8, :] for r in at], axis=0
            ).astype(BF)
            s.gm[kk, ff, 64:96, :] = s.gsh[own, 0:512].astype(BF)
            s.gm[kk, ff, 96:128, :] = s.gsh[own, 512:1024].astype(BF)
    gm.core(s.gm)

    wait(grads_in)

    for i in range(8):
        quad = [s.pd[inv_slot[4 * i + q]].astype(F32) for q in range(4)]
        s.dt[:, at_tile(i)] = jnp.concatenate(quad, axis=0).T[0:64].astype(BF)
    for i in range(8):
        cols = at_tile(i)
        scaled = (s.dt[:, cols].astype(F32) * s.rsum[i : i + 1, :]).astype(BF).astype(F32)
        inner = jnp.sum(s.mixs[:, cols] * scaled, axis=0, keepdims=True)
        d_i = jnp.concatenate([jnp.zeros_like(scaled), scaled], axis=0).T.astype(BF)
        right = jnp.concatenate([s.qz[cols, :], d_i], axis=0)
        dq = jnp.zeros((64, TILE), F32)
        for j in range(i + 1):
            rows = at_tile(j)
            e_low = s.es[tile(i, j)]
            ds = (e_low.astype(F32) * (nt(s.kv[rows, :], d_i) - inner)).astype(BF)
            both = nn(jnp.concatenate([ds, e_low], axis=1), right)
            s.acc[rows, :] = both if i == j else s.acc[rows, :] + both
            dq += nn(s.kvt[0:64, rows], ds)
        s.mixs[:, cols] = dq * SCALE
        if i == 4:
            gm.along_x()
        if i == 5:
            act.middle()

    def turned_back(v, cols):
        cos, sin = s.cst[0:8, cols], s.cst[8:16, cols]
        f1, f2 = v[0:8], v[8:16]
        return [f1 * cos + f2 * sin, f2 * cos - f1 * sin, v[16:64]]

    for i in range(8):
        cols = at_tile(i)
        tail = s.acc[cols, :]
        both = turned_back(s.mixs[:, cols], cols) + turned_back(tail.T[0:64], cols)
        s.dd[4 * i : 4 * i + 4, :, 0:128] = (
            jnp.concatenate(both, axis=0).T.astype(BF).reshape(4, 64, 128)
        )
        s.dd[4 * i : 4 * i + 4, :, 128:256] = tail.astype(BF).reshape(4, 64, 128)
    for n in range(8):
        for j in range(2):
            s.d_own[2 * n + j] = s.dd[block_of(k, n, j)]
            s.d_away[2 * n + j] = s.dd[block_of(1 - k, n, j)]
    d_sent = send(s.d_away, s.d_got, KC)

    dhat = RowSum(
        send, s.dhat, s.dhat_rz, s.dhat_ry, s.dhat_t, s.dhat_rt, s.dhat_w, s.dhat_rw
    )
    s.go[...] = tn(s.attn[...], s.gs[...].reshape(1024, 1024))
    d_sent.wait_recv()
    for m in (2, 3, 1, 0):
        rows = slice(m * 256, m * 256 + 256)
        quads = slice(4 * m, 4 * m + 4)
        tiles = []
        for at in (slice(0, 128), slice(128, 256)):
            own = s.d_own[quads, :, at].reshape(256, 128).astype(F32)
            got = s.d_got[quads, :, at].reshape(256, 128).astype(F32)
            tiles.append((jnp.where(k == 0, own, got), jnp.where(k == 0, got, own)))
        (p_0, p_1), (r_0, r_1) = tiles
        turned = jnp.concatenate(
            [
                jnp.where(low, p_0, roll(p_1, 64)),
                jnp.where(low, roll(p_0, 64), p_1),
                jnp.where(low, roll(r_0, 64), r_1),
            ],
            axis=1,
        )
        turned_low = turned.astype(BF)
        s.dtr[rows, :] = turned_low
        d_first = nt(turned_low, s.was[:, 0:384])
        before = s.dhat[2 * m : 2 * m + 2].reshape(256, 1024).astype(F32)
        s.dhat[2 * m : 2 * m + 2] = (
            (before + d_first * g1[...]).astype(BF).reshape(2, 128, 1024)
        )
        dhat.start(2 * m)
        dhat.start(2 * m + 1)
        s.sm[0:1, :] += down(d_first * x_hat_of(m))
        s.sm[1:2, :] += down(d_first)
        s.sm[5:6, 0:384] += down(turned)

    sm_core = send(s.sm, s.sm_r, KC)
    s.slope[:, 0:384] = tn(s.first[...].reshape(1024, 1024), s.dtr[...])
    for kk in range(2):
        for ff in range(8):
            at = [(tt * 2 + kk) * 64 + ff * 8 for tt in range(8)]
            r = (kk * 8 + ff) * 8
            s.ga[kk, ff, :, 0:384] = jnp.concatenate(
                [s.slope[q : q + 8, 0:384] for q in at], axis=0
            ).astype(BF)
            s.ga[kk, ff, :, 384:512] = jnp.concatenate(
                [s.go[r : r + 8, j * 128 : j * 128 + 128] for j in range(8)], axis=0
            ).astype(BF)
    ga.core(s.ga)
    gm.along_z()
    sm_core.wait_recv()
    s.sm_u[...] = s.sm[...] + s.sm_r[...]
    sm_x = [send(s.sm_u, s.sm_ru.at[j], XS[i]) for j, i in enumerate(NEAR_FIRST)]
    ga.along_x()
    act_o[...] = (s.xs[0].astype(F32) + (ob[...] + sb[...]) + act.end()).astype(BF)
    wait(sm_x)
    s.sm_v[...] = s.sm_u[...] + s.sm_ru[0] + s.sm_ru[1] + s.sm_ru[2]
    sm_zh = send(s.sm_v, s.sm_rv, ZH)
    dhat.middle()
    ga.along_z()
    total = gm.total()
    for j in range(8):
        s.gm_f[j] = total[j * 8 : j * 8 + 8, :]
    gsw_o[:, 0:512] = total[64:96, :]
    gsw_o[:, 512:1024] = total[96:128, :]
    gm.to_owners()
    sm_zh.wait_recv()
    total = s.sm_v[...] + s.sm_rv[...]
    for j in range(8):
        s.sm_f[j, 0:4, :] = total[0:4, j * 128 : j * 128 + 128]
        s.sm_f[j, 4:5, :] = total[5:6, 0:128]
        s.sm_f[j, 5:6, :] = total[5:6, 128:256]
        s.sm_f[j, 6:7, :] = total[4:5, j * 128 : j * 128 + 128]
        s.sm_f[j, 7:8, :] = total[5:6, 256:384]
    small_o[8:12, :] = jnp.concatenate(
        [total[5:6, 384 + j * 128 : 512 + j * 128] for j in range(4)], axis=0
    )
    small_o[12:16, :] = jnp.zeros((4, 128), F32)
    sm = WeightSum(send, me, F32, None, None, None, None, None, s.sm_f, s.sm_rf)
    sm.to_owners()
    total = ga.total()
    for j in range(8):
        s.ga_f[j] = total[j * 8 : j * 8 + 8, 0:384]
        gow_o[:, j * 128 : j * 128 + 128] = total[j * 8 : j * 8 + 8, 384:512]
    ga.to_owners()
    d_hat = dhat.end()
    inv = s.invs[0:128, :]
    x_hat = (s.xs[0].astype(F32) - s.mus[0:128, :]) * inv
    tok_o[...] = s.gs[0].astype(F32) + inv * (
        d_hat
        - jnp.mean(d_hat, axis=1, keepdims=True)
        - x_hat * jnp.mean(d_hat * x_hat, axis=1, keepdims=True)
    )
    gm.wait()
    for n in range(8):
        gew_o[:, pl.ds(pl.multiple_of(chip_at(n) * 512, 512), 512)] = s.gm_rf[n]
    sm.wait()
    total = s.sm_rf[0]
    for n in range(1, 8):
        total += s.sm_rf[n]
    small_o[0:4, :] = total[0:4, :]
    source = lax.rem(2 * t + k, 8)
    bias_rows = jnp.zeros((2, 128), F32)
    for n in range(8):
        bias_rows = jnp.where(chip_at(n) == source, s.sm_rf[n, 4:6, :], bias_rows)
    small_o[4:5, :] = jnp.where(a == 0, bias_rows[0:1], bias_rows[1:2])
    small_o[5:6, :] = s.sm_f[t, 6:7, :]
    small_o[6:7, :] = s.sm_f[t, 7:8, :]
    small_o[7:8, :] = jnp.zeros((1, 128), F32)
    ga.wait()
    for n in range(8):
        for o in range(3):
            at = pl.ds(pl.multiple_of(o * 1024 + chip_at(n) * 128, 128), 128)
            gtw_o[:, at] = s.ga_rf[n, :, o * 128 : o * 128 + 128]
    send.finish()


def block(pairs, pos, x, g, tw, ow, ew, sw, tb, eb, g1, b1, g2, b2, ob, sb):
    return pl.pallas_call(
        block_kernel,
        out_shape=(
            jax.ShapeDtypeStruct((128, 1024), BF),
            jax.ShapeDtypeStruct((128, 1024), F32),
            jax.ShapeDtypeStruct((8, 3072), F32),
            jax.ShapeDtypeStruct((8, 4096), F32),
            jax.ShapeDtypeStruct((8, 1024), F32),
            jax.ShapeDtypeStruct((32, 1024), F32),
            jax.ShapeDtypeStruct((16, 128), F32),
        ),
        in_specs=[pl.BlockSpec(memory_space=pltpu.SMEM), VM] + [ANY] * 6 + [VM] * 8,
        out_specs=(VM,) * 7,
        scratch_shapes=[pltpu.VMEM(shape, kind) for _, shape, kind in SCRATCH]
        + [
            pltpu.SemaphoreType.DMA((COPIES,)),
            pltpu.SemaphoreType.DMA((COPIES,)),
            pltpu.SemaphoreType.DMA((LOADS,)),
            pltpu.SMEM((32,), jnp.int32),
        ],
        compiler_params=pltpu.CompilerParams(
            collective_id=0, has_side_effects=True, vmem_limit_bytes=62 * MIB
        ),
        name="block",
    )(pairs, pos, x, g, tw, ow, ew, sw, tb, eb, g1, b1, g2, b2, ob, sb)


def results_kernel(
    act, tok, gtw, gew, gow, gsw, small,
    act_o, tok_o, gtw_o, gew_o, gow_o, gsw_o,
    fg_o, fb_o, sg_o, sb_o, tb_o, vb_o, ob_o, eb_o, hb_o,
):
    for src, dst in (
        (act, act_o), (tok, tok_o), (gtw, gtw_o), (gew, gew_o), (gow, gow_o), (gsw, gsw_o)
    ):
        dst[...] = src[...]
    k, f = lax.rem(lax.axis_index("ctx"), 2), lax.axis_index("fsdp")
    rows = small[0:8, :]
    eights = pltpu.roll(rows, lax.rem(128 - (k * 64 + f * 8), 128), 1)
    for j, dst in enumerate((fg_o, fb_o, sg_o, sb_o)):
        dst[...] = eights[j : j + 1, 0:8]
    vb_o[...] = eights[6:7, 0:8]
    ob_o[...] = eights[5:6, 0:8]
    hb_o[...] = eights[5:6, 0:8]
    tb_o[...] = pltpu.roll(rows, lax.rem(128 - f * 16, 128), 1)[4:5, 0:16]
    wide = small[pl.ds(8 + k * 2 + lax.div(f, 4), 1), :]
    wide = jnp.broadcast_to(wide, (8, 128))
    eb_o[...] = pltpu.roll(wide, lax.rem(128 - lax.rem(f, 4) * 32, 128), 1)[0:1, 0:32]


def results(*arrays):
    vectors = (8, 8, 8, 8, 16, 8, 8, 32, 8)
    return pl.pallas_call(
        results_kernel,
        out_shape=tuple(jax.ShapeDtypeStruct(v.shape, v.dtype) for v in arrays[:6])
        + tuple(jax.ShapeDtypeStruct((1, n), F32) for n in vectors),
        compiler_params=pltpu.CompilerParams(vmem_limit_bytes=62 * MIB),
        name="results",
    )(*arrays)


def shards(
    tokens_in,
    positions,
    block_pairs,
    first_gain,
    first_bias,
    second_gain,
    second_bias,
    triple_weight,
    triple_bias,
    output_weight,
    output_bias,
    expand_weight,
    expand_bias,
    shrink_weight,
    shrink_bias,
    cotangent,
):
    x, g = tokens_in.reshape(128, 1024), cotangent.reshape(128, 1024)

    def line(v):
        return v.reshape(1, -1)

    found = block(
        block_pairs.T,
        positions,
        x,
        g,
        triple_weight,
        output_weight,
        expand_weight,
        shrink_weight,
        line(triple_bias),
        line(expand_bias),
        line(first_gain),
        line(first_bias),
        line(second_gain),
        line(second_bias),
        line(output_bias),
        line(shrink_bias),
    )
    act, tok, gtw, gew, gow, gsw, fg, fb, sg, sb, tb, vb, ob, eb, hb = results(*found)
    return (
        act.reshape(tokens_in.shape),
        tok.reshape(tokens_in.shape),
        fg.reshape(8),
        fb.reshape(8),
        sg.reshape(8),
        sb.reshape(8),
        gtw,
        tb.reshape(16),
        vb.reshape(8),
        gow,
        ob.reshape(8),
        gew,
        eb.reshape(32),
        gsw,
        hb.reshape(8),
    )


def solution(mesh):
    return jax.shard_map(
        shards,
        mesh=mesh,
        in_specs=(
            P("fsdp", "ctx", None, None, None),
            P("fsdp", None),
            P(),
            P(),
            P(),
            P(),
            P(),
            P("fsdp", None),
            P(),
            P(None, "fsdp"),
            P(),
            P("fsdp", None),
            P(),
            P(None, "fsdp"),
            P(),
            P("fsdp", "ctx", None, None, None),
        ),
        out_specs=(
            P("fsdp", "ctx", None, None, None),
            P("fsdp", "ctx", None, None, None),
            P(("ctx", "fsdp")),
            P(("ctx", "fsdp")),
            P(("ctx", "fsdp")),
            P(("ctx", "fsdp")),
            P(("ctx", "fsdp"), None),
            P(("ctx", "fsdp")),
            P(("ctx", "fsdp")),
            P(("ctx", "fsdp"), None),
            P(("ctx", "fsdp")),
            P(("ctx", "fsdp"), None),
            P(("ctx", "fsdp")),
            P(("ctx", "fsdp"), None),
            P(("ctx", "fsdp")),
        ),
        check_vma=False,
    )
```

```python
import math

import jax
import jax.numpy as jnp
import numpy as np
from jax import lax
from jax.experimental import pallas as pl
from jax.experimental.pallas import tpu as pltpu
from jax.sharding import PartitionSpec as P

MESH = pl.DeviceIdType.MESH
BF, F32 = jnp.bfloat16, jnp.float32
EPS = 1e-05
BASE = 10000.0
MIB = 1 << 20
SCALE = 0.125
TILE = 256
RATES = 1.0 / BASE ** (np.arange(0, 16, 2, dtype=np.float32) / 16)

ZL, KC, ZH = (1, 0, 0, 0, 0), (0, 0, 1, 0, 0), (0, 0, 0, 0, 1)
YS = {i: (0, i, 0, 0, 0) for i in (1, 2, 3)}
XS = {i: (0, 0, 0, i, 0) for i in (1, 2, 3)}
NEAR_FIRST = (1, 3, 2)
OFFS = ((0, 0), (0, 1), (0, 3), (0, 2), (1, 0), (1, 1), (1, 3), (1, 2))
SLOT = {off: n for n, off in enumerate(OFFS)}


def origin(da, i):
    return SLOT[(da, (4 - i) % 4)]


def chips(n):
    return (*OFFS[n], 0, 0, 0)


def coords():
    c, f = lax.axis_index("ctx"), lax.axis_index("fsdp")
    return lax.div(c, 8), lax.rem(lax.div(c, 2), 4), lax.rem(c, 2), lax.div(f, 2), lax.rem(f, 2)


def device_at(me, off):
    a, b, k, x, h = (lax.rem(p + o, n) for p, o, n in zip(me, off, (2, 4, 2, 4, 2)))
    return ((a * 4 + b) * 2 + k, x * 2 + h)


def barrier(me, offs):
    sem = pltpu.get_barrier_semaphore()
    for off in offs:
        pl.semaphore_signal(sem, inc=1, device_id=device_at(me, off), device_id_type=MESH)
    pl.semaphore_wait(sem, len(offs))


class Sender:
    def __init__(self, me, send_sems, recv_sems):
        self.me, self.send_sems, self.recv_sems, self.copies = me, send_sems, recv_sems, []

    def __call__(self, src, dst, off):
        i = len(self.copies)
        copy = pltpu.make_async_remote_copy(
            src_ref=src,
            dst_ref=dst,
            send_sem=self.send_sems.at[i],
            recv_sem=self.recv_sems.at[i],
            device_id=device_at(self.me, off),
            device_id_type=MESH,
        )
        copy.start()
        self.copies.append(copy)
        return copy

    def finish(self):
        for copy in self.copies:
            copy.wait_send()


def nt(left, right):
    return lax.dot_general(left, right, (((1,), (1,)), ((), ())), preferred_element_type=F32)


def tn(left, right):
    return lax.dot_general(left, right, (((0,), (0,)), ((), ())), preferred_element_type=F32)


def nn(left, right):
    return jnp.dot(left, right, preferred_element_type=F32)


def down(v):
    return jnp.sum(v, axis=0, keepdims=True)


def lanes(shape):
    return lax.broadcasted_iota(jnp.int32, shape, 1)


def roll(v, shift):
    return pltpu.roll(v, shift, 1)


ANY = pl.BlockSpec(memory_space=pl.ANY)
VM = pl.BlockSpec(memory_space=pltpu.VMEM)


def row_sum_scratch(name, rows):
    low = 128 - rows
    return (
        (name + "_rz", (4, rows, 1024), BF),
        (name + "_t", (4, rows, 1024), BF),
        (name + "_tr", (2, rows // 2, 1024), BF),
        (name + "_rt", (2, rows, 1024), BF),
        (name + "_yr", (2, 2, low // 2, 1024), BF),
        (name + "_u", (2, 2, low, 1024), BF),
        (name + "_ry", (2, 2, low, 1024), BF),
        (name + "_w", (low, 1024), BF),
        (name + "_rw", (low, 1024), BF),
    )


COPIES = 60 + 2 * 17 + 10 + 2 * 17 + 5 + 5 + 5 + 21
LOADS = 8
TOK = (8, 128, 1024)
SCRATCH = (
    ("xs", TOK, BF),
    ("gs", TOK, BF),
    ("first", TOK, BF),
    ("second", (1024, 1024), BF),
    ("mus", (1024, 1), F32),
    ("invs", (1024, 1), F32),
    ("was", (1024, 896), BF),
    ("wos", (128, 1024), BF),
    ("wss", (512, 1024), BF),
    ("slope", (1024, 512), F32),
    ("hidden", (1024, 512), BF),
    ("dexp", (1024, 512), BF),
    ("cst", (16, 2048), F32),
    ("cs3", (32, 16, 128), F32),
    ("pk", (32, 64, 256), BF),
    ("th", (16, 64, 256), BF),
    ("pd", (32, 64, 128), BF),
    ("td", (16, 64, 128), BF),
    ("kv", (2048, 128), BF),
    ("qz", (2048, 128), BF),
    ("kvt", (128, 2048), BF),
    ("dt", (64, 2048), BF),
    ("sc", (2048, TILE), F32),
    ("es", (36, TILE, TILE), BF),
    ("acc", (2048, 128), F32),
    ("mixs", (64, 2048), F32),
    ("rsum", (8, TILE), F32),
    ("ot", (32, 64, 128), BF),
    ("o_own", (16, 64, 128), BF),
    ("o_away", (16, 64, 128), BF),
    ("o_got", (16, 64, 128), BF),
    ("dd", (32, 64, 256), BF),
    ("d_own", (16, 64, 256), BF),
    ("d_away", (16, 64, 256), BF),
    ("d_got", (16, 64, 256), BF),
    ("attn", (1024, 128), BF),
    ("dtr", (1024, 384), BF),
    ("act", TOK, BF),
    *row_sum_scratch("act", 64),
    ("dhat", TOK, BF),
    *row_sum_scratch("dhat", 32),
    ("gsh", (512, 1024), F32),
    ("gm", (2, 8, 144, 512), BF),
    ("gm_r", (8, 144, 512), BF),
    ("gm_u", (8, 144, 512), BF),
    ("gm_ru", (3, 2, 144, 512), BF),
    ("gm_v", (2, 144, 512), BF),
    ("gm_rv", (144, 512), BF),
    ("gm_f", (8, 8, 512), F32),
    ("gm_rf", (8, 8, 512), F32),
    ("go", (128, 1024), F32),
    ("ga", (2, 8, 64, 384), BF),
    ("ga_r", (8, 64, 384), BF),
    ("ga_u", (8, 64, 384), BF),
    ("ga_ru", (3, 2, 64, 384), BF),
    ("ga_v", (2, 64, 384), BF),
    ("ga_rv", (64, 384), BF),
    ("ga_f", (8, 8, 384), F32),
    ("ga_rf", (8, 8, 384), F32),
    ("sm", (8, 1024), F32),
    ("sm_r", (8, 1024), F32),
    ("sm_u", (8, 1024), F32),
    ("sm_ru", (3, 8, 1024), F32),
    ("sm_v", (8, 1024), F32),
    ("sm_rv", (8, 1024), F32),
    ("sm_f", (8, 8, 128), F32),
    ("sm_rf", (8, 8, 128), F32),
)
ZR, YR = slice(0, 64), slice(64, 128)


class Refs:
    pass


def halves(rows):
    middle = (rows.start + rows.stop) // 2
    return {1: slice(rows.start, middle), 3: slice(middle, rows.stop)}


class TokenGather:
    def __init__(self, send, dst):
        self.send, self.dst = send, dst
        self.zy, self.far_y, self.far_z = [], [], []

    def first(self):
        send, d = self.send, self.dst
        self.y = {i: send(d.at[0, YR], d.at[origin(0, i), YR], YS[i]) for i in (1, 3)}
        self.z = send(d.at[0, ZR], d.at[4, ZR], ZL)

    def rest(self):
        send, d = self.send, self.dst
        self.own_z = send(d.at[0, YR], d.at[4, YR], ZL)
        self.own_y = {i: send(d.at[0, ZR], d.at[origin(0, i), ZR], YS[i]) for i in (1, 3)}

    def relay(self, i, da, rows):
        part, src, dst = halves(rows)[i], origin(da, i), SLOT[(da, 2)]
        return self.send(self.dst.at[src, part], self.dst.at[dst, part], YS[i])

    def second(self):
        send, d = self.send, self.dst
        self.far = []
        for i in (1, 3):
            self.y[i].wait_recv()
            self.far.append(self.relay(i, 0, YR))
            self.zy.append(send(d.at[origin(0, i), YR], d.at[origin(1, i), YR], ZL))
        self.z.wait_recv()
        self.yz = {i: send(d.at[4, ZR], d.at[origin(1, i), ZR], YS[i]) for i in (1, 3)}

    def third(self):
        send, d = self.send, self.dst
        for copy in self.far:
            copy.wait_recv()
        self.zy.append(send(d.at[3, YR], d.at[7, YR], ZL))
        for i in (1, 3):
            self.own_y[i].wait_recv()
            self.far_y.append(self.relay(i, 0, ZR))

    def fourth(self):
        for i in (1, 3):
            self.yz[i].wait_recv()
            self.far_z.append(self.relay(i, 1, ZR))

    def near(self):
        for copy in self.far_y:
            copy.wait_recv()

    def beside(self):
        self.own_z.wait_recv()

    def end(self):
        for copy in self.zy + self.far_z:
            copy.wait_recv()


class RowSum:
    def __init__(self, send, src, rz, t, tr, rt, yr, u, ry, w, rw):
        self.send, self.src, self.rz, self.t, self.tr, self.rt = send, src, rz, t, tr, rt
        self.yr, self.u, self.ry, self.w, self.rw = yr, u, ry, w, rw
        self.top, self.low = slice(0, rz.shape[1]), slice(rz.shape[1], 128)
        self.z, self.far, self.on = {}, {}, []

    def start(self, n):
        self.start_z(n)
        self.start_far(n)

    def start_z(self, n):
        if n > 3:
            self.z[n - 4] = self.send(self.src.at[n, self.top], self.rz.at[n - 4], ZL)

    def start_far(self, n):
        da, db = OFFS[n]
        if db == 2:
            for i, part in halves(self.low).items():
                self.far[da, i] = self.send(self.src.at[n, part], self.yr.at[da, i // 2], YS[i])

    def along_y(self):
        split = halves(self.low)
        own = halves(slice(0, self.low.stop - self.low.start))
        for da in (1, 0):
            for i in (1, 3):
                n, j = SLOT[(da, i)], i // 2
                self.far[da, i].wait_recv()
                self.u[da, j, own[i]] = (
                    self.src[n, split[i]].astype(F32) + self.yr[da, j].astype(F32)
                ).astype(BF)
                self.u[da, j, own[4 - i]] = self.src[n, split[4 - i]]
                self.far[da, i] = self.send(self.u.at[da, j], self.ry.at[da, j], YS[i])

    def after_z(self, m):
        self.z[m].wait_recv()
        total = self.src[m, self.top].astype(F32) + self.rz[m].astype(F32)
        self.t[m] = total.astype(BF)
        if m == 3:
            self.far_t = {
                i: self.send(self.t.at[3, part], self.tr.at[i // 2], YS[i])
                for i, part in halves(self.top).items()
            }

    def after_y(self):
        for i in (1, 3):
            self.far[1, i].wait_recv()
        total = self.src[4, self.low].astype(F32)
        total += self.ry[1, 0].astype(F32) + self.ry[1, 1].astype(F32)
        self.w[...] = total.astype(BF)
        self.on.append(self.send(self.w, self.rw, ZL))

    def last_y(self):
        for i, part in halves(self.top).items():
            m, j = SLOT[(0, i)], i // 2
            self.far_t[i].wait_recv()
            self.t[m, part] = (self.t[m, part].astype(F32) + self.tr[j].astype(F32)).astype(BF)
            self.on.append(self.send(self.t.at[m], self.rt.at[j], YS[i]))

    def end(self):
        for copy in [self.far[0, 1], self.far[0, 3], *self.on]:
            copy.wait_recv()
        upper = self.t[0].astype(F32) + self.rt[0].astype(F32) + self.rt[1].astype(F32)
        lower = self.src[0, self.low].astype(F32) + self.rw[...].astype(F32)
        lower += self.ry[0, 0].astype(F32) + self.ry[0, 1].astype(F32)
        return jnp.concatenate([upper, lower], axis=0)


class WeightSum:
    def __init__(self, send, me, kind, r, u, ru, v, rv, f, rf):
        self.send, self.me, self.kind = send, me, kind
        self.r, self.u, self.ru, self.v, self.rv, self.f, self.rf = r, u, ru, v, rv, f, rf

    def core(self, src):
        self.src = src
        self.sent = [self.send(src.at[1 - self.me[2]], self.r, KC)]

    def wait(self):
        for copy in self.sent:
            copy.wait_recv()

    def along_x(self):
        x = self.me[3]
        self.core_sum()
        self.sent = []
        for j, i in enumerate(NEAR_FIRST):
            there = pl.ds(lax.rem(x + i, 4) * 2, 2)
            self.sent.append(self.send(self.u.at[there], self.ru.at[j], XS[i]))

    def along_z(self):
        x, h = self.me[3], self.me[4]
        self.wait()
        for hh in range(2):
            total = self.u[x * 2 + hh].astype(F32)
            for j in range(3):
                total += self.ru[j, hh].astype(F32)
            self.v[hh] = total.astype(self.kind)
        self.sent = [self.send(self.v.at[1 - h], self.rv, ZH)]

    def core_sum(self):
        self.wait()
        k = self.me[2]

        def one(f, _):
            self.u[f] = (self.src[k, f].astype(F32) + self.r[f].astype(F32)).astype(self.kind)
            return 0

        lax.fori_loop(0, 8, one, 0)

    def total(self):
        self.wait()
        return self.v[self.me[4]].astype(F32) + self.rv[...].astype(F32)

    def to_owners(self):
        a, b = self.me[0], self.me[1]
        self.sent = []
        for n in range(1, 8):
            da, db = OFFS[n]
            there = lax.rem(a + da, 2) * 4 + lax.rem(b + db, 4)
            self.sent.append(self.send(self.f.at[there], self.rf.at[origin(da, db)], chips(n)))
        self.rf[0] = self.f[a * 4 + b]


def block_kernel(
    pairs, pos, x, g, tw, ow, ew, sw, tb, eb, g1, b1, g2, b2, ob, sb,
    act_o, tok_o, gtw_o, gew_o, gow_o, gsw_o, small_o, *scratch,
):
    s = Refs()
    for (name, _, _), ref in zip(SCRATCH, scratch):
        setattr(s, name, ref)
    ss, rs, ls, inv_slot = scratch[len(SCRATCH) :]
    me = coords()
    a, b, k, xx, h = me
    t, f = a * 4 + b, xx * 2 + h
    local = []

    def load(src, dst):
        copy = pltpu.make_async_copy(src, dst, ls.at[len(local)])
        copy.start()
        local.append(copy)

    def cols_at(ff):
        return pl.ds(pl.multiple_of(ff * 128, 128), 128)

    def pieces(ff):
        rows = pl.ds(pl.multiple_of(ff * 128 + k * 64, 64), 64)
        return (
            s.was.at[rows, 0:384],
            s.was.at[rows, 384:896],
            s.wos.at[pl.ds(pl.multiple_of(k * 64, 64), 64), cols_at(ff)],
            s.wss.at[pl.ds(pl.multiple_of(k * 256, 256), 256), cols_at(ff)],
        )

    half = pl.ds(pl.multiple_of(k * 64, 64), 64)
    mine = pl.ds(pl.multiple_of(f * 128 + k * 64, 64), 64)
    for o in range(3):
        load(
            tw.at[half, pl.ds(pl.multiple_of(o * 1024 + t * 128, 128), 128)],
            s.was.at[mine, pl.ds(o * 128, 128)],
        )
    load(ew.at[half, pl.ds(pl.multiple_of(t * 512, 512), 512)], s.was.at[mine, pl.ds(384, 512)])
    load(ow.at[pl.ds(pl.multiple_of(t * 128 + k * 64, 64), 64)], pieces(f)[2])
    load(sw.at[pl.ds(pl.multiple_of(t * 512 + k * 256, 256), 256)], pieces(f)[3])
    load(x, s.xs.at[0])
    load(g, s.gs.at[0])
    barrier(me, [*(chips(n) for n in range(1, 8)), *XS.values(), ZH, KC])
    send = Sender(me, ss, rs)

    def wait(copies):
        for copy in copies:
            copy.wait_recv()

    for copy in local:
        copy.wait()
    ways = {0: ZH, **XS}
    weights = {0: [], 1: []}

    def weights_out(ff, part, ways):
        refs = pieces(ff)[:1] if part == 0 else pieces(ff)[1:]
        sent = {i: [send(ref, ref, way) for ref in refs] for i, way in ways.items()}
        weights[part] += [send(ref, ref, KC) for ref in refs]
        return sent

    def weights_on(came, part, hh):
        for i in NEAR_FIRST:
            wait(came[i])
            weights_out(lax.rem(xx + 4 - i, 4) * 2 + hh, part, {})

    w_own = {0: weights_out(f, 0, ways)}
    xt, gt = TokenGather(send, s.xs), TokenGather(send, s.gs)
    xt.first()
    xt.rest()

    def chip_at(n):
        da, db = OFFS[n]
        return lax.rem(a + da, 2) * 4 + lax.rem(b + db, 4)

    def block_of(kk, n, j):
        return pairs[j, chip_at(n) * 2 + kk]

    held = [block_of(kk, n, j) for kk in range(2) for n in range(8) for j in range(2)]

    def find(j, _):
        at = jnp.int32(0)
        for q, block in enumerate(held):
            at = jnp.where(block == j, q, at)
        inv_slot[j] = at
        return 0

    lax.fori_loop(0, 32, find, 0)
    row = lax.broadcasted_iota(jnp.int32, (8, 1), 0)
    rates = jnp.zeros((8, 1), F32)
    for j in range(8):
        rates = jnp.where(row == j, float(RATES[j]), rates)
    angles = rates * pos[...].astype(F32)
    s.cst[0:8, :] = jnp.cos(angles)
    s.cst[8:16, :] = jnp.sin(angles)
    low16 = lanes((16, 128)) < 64
    for j in range(16):
        both = s.cst[:, j * 128 : j * 128 + 128]
        turned = roll(both, 64)
        s.cs3[2 * j] = jnp.where(low16, both, turned)
        s.cs3[2 * j + 1] = jnp.where(low16, turned, both)
    s.sm[...] = jnp.zeros_like(s.sm)

    def norm(n):
        rows = slice(n * 128, n * 128 + 128)
        v = s.xs[n].astype(F32)
        mean = jnp.mean(v, axis=1, keepdims=True)
        centred = v - mean
        inv = lax.rsqrt(jnp.mean(centred * centred, axis=1, keepdims=True) + EPS)
        s.mus[rows, :] = mean
        s.invs[rows, :] = inv
        x_hat = centred * inv
        s.first[n] = (x_hat * g1[...] + b1[...]).astype(BF)
        s.second[rows, :] = (x_hat * g2[...] + b2[...]).astype(BF)

    norm(0)
    fz = xx * 2 + (1 - h)
    wait(w_own[0][0])
    w_z = {0: weights_out(fz, 0, XS)}
    xt.second()
    xt.third()
    norm(1)
    norm(2)
    xt.fourth()
    w_own[1] = weights_out(f, 1, ways)
    gt.first()
    gt.rest()
    weights_on(w_own[0], 0, h)
    weights_on(w_z[0], 0, 1 - h)
    xt.near()
    norm(3)

    low = lanes((256, 128)) < 64
    low128 = lanes((16, 128)) < 64
    early = (lanes((256, 128)) & 63) < 8
    bias_at = [tb[0:1, pl.ds(pl.multiple_of(o * 1024 + t * 128, 128), 128)] for o in range(3)]
    triple_bias = jnp.concatenate(bias_at, axis=1)
    expand_bias = eb[0:1, pl.ds(pl.multiple_of(t * 512, 512), 512)]

    def deal(tiles, own, away, to, m):
        quads = pl.ds(4 * m, 4)
        for j, (head0, head1) in enumerate(tiles):
            at = slice(j * 128, j * 128 + 128)
            keep = jnp.where(k == 0, head0, head1).astype(BF).reshape(4, 64, 128)
            give = jnp.where(k == 0, head1, head0).astype(BF).reshape(4, 64, 128)
            own[pl.ds(k * 16 + 4 * m, 4), :, at] = keep
            away[quads, :, at] = give
        return send(away.at[quads], to.at[pl.ds(k * 16 + 4 * m, 4)], KC)

    def attend_in(m):
        rows = slice(m * 256, m * 256 + 256)
        tables = []
        for n in (2 * m, 2 * m + 1):
            tables.append(
                jnp.where(low128, s.cs3[block_of(k, n, 0)], s.cs3[block_of(k, n, 1)])
            )
        cs = jnp.concatenate(tables, axis=1)
        cos, sin = cs[0:8], cs[8:16]
        one, zero = jnp.ones((48, 256), F32), jnp.zeros((48, 256), F32)
        tc = jnp.concatenate([cos, cos, one, cos, cos, one], axis=0).T
        ts = jnp.concatenate([-sin, sin, zero, -sin, sin, zero], axis=0).T

        def turn(v):
            return v * tc + jnp.where(early, roll(v, 120), roll(v, 8)) * ts

        left = s.first[2 * m : 2 * m + 2].reshape(256, 1024)
        triple = nn(left, s.was[:, 0:384]) + triple_bias
        query, key, value = turn(triple[:, 0:128]), turn(triple[:, 128:256]), triple[:, 256:384]
        query *= SCALE
        zeros = jnp.zeros_like(value)
        return deal(
            (
                (jnp.where(low, key, roll(value, 64)), jnp.where(low, roll(key, 64), value)),
                (jnp.where(low, query, zeros), jnp.where(low, roll(query, 64), zeros)),
            ),
            s.pk,
            s.th,
            s.pk,
            m,
        )

    def forward_in(m):
        rows = slice(m * 256, m * 256 + 256)
        u = nn(s.second[rows, :], s.was[:, 384:896]) + expand_bias
        cdf = 0.5 * (1.0 + lax.erf(u * math.sqrt(0.5)))
        pdf = jnp.exp(-0.5 * u * u) * (1.0 / math.sqrt(2.0 * math.pi))
        s.hidden[rows, :] = (u * cdf).astype(BF)
        s.slope[rows, :] = cdf + u * pdf

    wait(weights[0])
    heads_in = [attend_in(0), attend_in(1)]
    xt.beside()
    norm(4)
    xt.end()
    for n in (5, 6, 7):
        norm(n)
    heads_in += [attend_in(2), attend_in(3)]
    wait(w_own[1][0])
    w_z[1] = weights_out(fz, 1, XS)
    gt.second()

    wait(heads_in)
    def place(j, _):
        at = pl.ds(pl.multiple_of(j * 64, 64), 64)
        s.kv[at, :] = s.pk[inv_slot[j], :, 0:128]
        s.qz[at, :] = s.pk[inv_slot[j], :, 128:256]
        return 0

    lax.fori_loop(0, 32, place, 0, unroll=4)
    for i in range(8):
        cols = slice(i * TILE, i * TILE + TILE)
        s.kvt[:, cols] = s.kv[cols, :].astype(F32).T.astype(BF)
    seen = lax.broadcasted_iota(jnp.int32, (TILE, TILE), 0) <= lanes((TILE, TILE))

    def folded(v, op):
        parts = [v[j * 8 : j * 8 + 8] for j in range(TILE // 8)]
        while len(parts) > 1:
            parts = [op(parts[j], parts[j + 1]) for j in range(0, len(parts), 2)]
        return parts[0]

    def tile(i, j):
        return i * (i + 1) // 2 + j

    def at_tile(i):
        return slice(i * TILE, i * TILE + TILE)

    for i in range(8):
        cols = at_tile(i)
        q_i = s.qz[cols, :]
        peak = None
        for j in range(i + 1):
            score = nt(s.kv[at_tile(j), :], q_i)
            if j == i:
                score = jnp.where(seen, score, -jnp.inf)
            s.sc[at_tile(j), :] = score
            high = folded(score, jnp.maximum)
            peak = high if peak is None else jnp.maximum(peak, high)
        peak = jnp.max(peak, axis=0, keepdims=True)
        total, mix = jnp.zeros((8, TILE), F32), jnp.zeros((64, TILE), F32)
        for j in range(i + 1):
            e = jnp.exp(s.sc[at_tile(j), :] - peak)
            total += folded(e, jnp.add)
            e_low = e.astype(BF)
            s.es[tile(i, j)] = e_low
            mix += nn(s.kvt[64:128, at_tile(j)], e_low)
        inv = 1.0 / jnp.sum(total, axis=0, keepdims=True)
        mix *= inv
        s.rsum[i : i + 1, :] = inv
        s.mixs[:, cols] = mix
        out = jnp.concatenate([mix, jnp.zeros_like(mix)], axis=0).T
        s.ot[4 * i : 4 * i + 4] = out.astype(BF).reshape(4, 64, 128)
        if i == 3:
            weights_on(w_own[1], 1, h)
        if i == 5:
            gt.third()
        if i == 6:
            weights_on(w_z[1], 1, 1 - h)
    for n in range(8):
        for j in range(2):
            s.o_own[2 * n + j] = s.ot[block_of(k, n, j)]
            s.o_away[2 * n + j] = s.ot[block_of(1 - k, n, j)]
    o_sent = send(s.o_away, s.o_got, KC)
    wait(weights[1])
    for m in range(4):
        forward_in(m)
    gt.fourth()

    act = RowSum(send, s.act, *(getattr(s, n) for n, _, _ in row_sum_scratch("act", 64)))
    o_sent.wait_recv()
    for m in (3, 1, 2, 0):
        rows = slice(m * 256, m * 256 + 256)
        own = s.o_own[4 * m : 4 * m + 4].reshape(256, 128).astype(F32)
        got = s.o_got[4 * m : 4 * m + 4].reshape(256, 128).astype(F32)
        head0, head1 = jnp.where(k == 0, own, got), jnp.where(k == 0, got, own)
        attn_low = jnp.where(low, head0, roll(head1, 64)).astype(BF)
        s.attn[rows, :] = attn_low
        out = nn(attn_low, s.wos[...]) + nn(s.hidden[rows, :], s.wss[...])
        s.act[2 * m : 2 * m + 2] = out.astype(BF).reshape(2, 128, 1024)
        act.start(2 * m + 1)
        act.start(2 * m)

    def back_to_heads(p):
        dmix = nt(s.gs[4 * p : 4 * p + 4].reshape(512, 1024), s.wos[...])
        for m in (2 * p, 2 * p + 1):
            part = dmix[(m - 2 * p) * 256 : (m - 2 * p) * 256 + 256]
            grads_in.append(deal(((part, roll(part, 64)),), s.pd, s.td, s.pd, m))

    def x_hat_of(m):
        rows = slice(m * 256, m * 256 + 256)
        v = s.xs[2 * m : 2 * m + 2].reshape(256, 1024).astype(F32)
        return (v - s.mus[rows, :]) * s.invs[rows, :]

    def forward_back(p):
        half = slice(p * 512, p * 512 + 512)
        d_hidden = nt(s.gs[4 * p : 4 * p + 4].reshape(512, 1024), s.wss[...])
        s.dexp[half, :] = (d_hidden * s.slope[half, :]).astype(BF)
        d_second = nt(s.dexp[half, :], s.was[:, 384:896])
        for m in (2 * p, 2 * p + 1):
            rows = slice(m * 256, m * 256 + 256)
            part = d_second[(m - 2 * p) * 256 : (m - 2 * p) * 256 + 256]
            s.dhat[2 * m : 2 * m + 2] = (part * g2[...]).astype(BF).reshape(2, 128, 1024)
            s.sm[2:3, :] += down(part * x_hat_of(m))
            s.sm[3:4, :] += down(part)
            s.sm[4:5, :] += down(s.gs[2 * m : 2 * m + 2].reshape(256, 1024).astype(F32))
            s.sm[5:6, 384:896] += down(s.dexp[rows, :].astype(F32))

    grads_in = []
    gt.near()
    back_to_heads(0)
    forward_back(0)
    act.along_y()
    act.after_z(3)
    gt.beside()
    gt.end()
    back_to_heads(1)
    forward_back(1)

    gm = WeightSum(send, me, BF, s.gm_r, s.gm_u, s.gm_ru, s.gm_v, s.gm_rv, s.gm_f, s.gm_rf)
    ga = WeightSum(send, me, BF, s.ga_r, s.ga_u, s.ga_ru, s.ga_v, s.ga_rv, s.ga_f, s.ga_rf)
    s.slope[...] = tn(s.second[...], s.dexp[...])
    s.gsh[...] = tn(s.hidden[...], s.gs[...].reshape(1024, 1024))
    s.go[...] = tn(s.attn[...], s.gs[...].reshape(1024, 1024))
    for kk in range(2):
        for ff in range(8):
            at = [(tt * 2 + kk) * 64 + ff * 8 for tt in range(8)]
            own = slice((kk * 8 + ff) * 32, (kk * 8 + ff) * 32 + 32)
            s.gm[kk, ff, 0:64, :] = jnp.concatenate(
                [s.slope[r : r + 8, :] for r in at], axis=0
            ).astype(BF)
            s.gm[kk, ff, 64:96, :] = s.gsh[own, 0:512].astype(BF)
            s.gm[kk, ff, 96:128, :] = s.gsh[own, 512:1024].astype(BF)
            r = (kk * 8 + ff) * 8
            s.gm[kk, ff, 128:144, :] = jnp.concatenate(
                [s.go[r : r + 8, 0:512], s.go[r : r + 8, 512:1024]], axis=0
            ).astype(BF)
    gm.core(s.gm)

    wait(grads_in)

    for i in range(8):
        quad = [s.pd[inv_slot[4 * i + q]].astype(F32) for q in range(4)]
        s.dt[:, at_tile(i)] = jnp.concatenate(quad, axis=0).T[0:64].astype(BF)
    for i in range(8):
        cols = at_tile(i)
        scaled = (s.dt[:, cols].astype(F32) * s.rsum[i : i + 1, :]).astype(BF).astype(F32)
        inner = jnp.sum(s.mixs[:, cols] * scaled, axis=0, keepdims=True)
        d_i = jnp.concatenate([jnp.zeros_like(scaled), scaled], axis=0).T.astype(BF)
        right = jnp.concatenate([s.qz[cols, :], d_i], axis=0)
        dq = jnp.zeros((64, TILE), F32)
        for j in range(i + 1):
            rows = at_tile(j)
            e_low = s.es[tile(i, j)]
            ds = (e_low.astype(F32) * (nt(s.kv[rows, :], d_i) - inner)).astype(BF)
            both = nn(jnp.concatenate([ds, e_low], axis=1), right)
            s.acc[rows, :] = both if i == j else s.acc[rows, :] + both
            dq += nn(s.kvt[0:64, rows], ds)
        s.mixs[:, cols] = dq * SCALE
        if i == 2:
            gm.along_x()
        if i == 5:
            act.after_y()
            act.after_z(1)
            act.after_z(2)
            act.last_y()
            act.after_z(0)

    def turned_back(v, cols):
        cos, sin = s.cst[0:8, cols], s.cst[8:16, cols]
        f1, f2 = v[0:8], v[8:16]
        return [f1 * cos + f2 * sin, f2 * cos - f1 * sin, v[16:64]]

    for i in range(8):
        cols = at_tile(i)
        tail = s.acc[cols, :]
        both = turned_back(s.mixs[:, cols], cols) + turned_back(tail.T[0:64], cols)
        s.dd[4 * i : 4 * i + 4, :, 0:128] = (
            jnp.concatenate(both, axis=0).T.astype(BF).reshape(4, 64, 128)
        )
        s.dd[4 * i : 4 * i + 4, :, 128:256] = tail.astype(BF).reshape(4, 64, 128)
    for n in range(8):
        for j in range(2):
            s.d_own[2 * n + j] = s.dd[block_of(k, n, j)]
            s.d_away[2 * n + j] = s.dd[block_of(1 - k, n, j)]
    d_sent = send(s.d_away, s.d_got, KC)

    dhat = RowSum(send, s.dhat, *(getattr(s, n) for n, _, _ in row_sum_scratch("dhat", 32)))
    d_sent.wait_recv()
    for m in (3, 1, 2, 0):
        rows = slice(m * 256, m * 256 + 256)
        quads = slice(4 * m, 4 * m + 4)
        tiles = []
        for at in (slice(0, 128), slice(128, 256)):
            own = s.d_own[quads, :, at].reshape(256, 128).astype(F32)
            got = s.d_got[quads, :, at].reshape(256, 128).astype(F32)
            tiles.append((jnp.where(k == 0, own, got), jnp.where(k == 0, got, own)))
        (p_0, p_1), (r_0, r_1) = tiles
        turned = jnp.concatenate(
            [
                jnp.where(low, p_0, roll(p_1, 64)),
                jnp.where(low, roll(p_0, 64), p_1),
                jnp.where(low, roll(r_0, 64), r_1),
            ],
            axis=1,
        )
        turned_low = turned.astype(BF)
        s.dtr[rows, :] = turned_low
        d_first = nt(turned_low, s.was[:, 0:384])
        before = s.dhat[2 * m : 2 * m + 2].reshape(256, 1024).astype(F32)
        s.dhat[2 * m : 2 * m + 2] = (
            (before + d_first * g1[...]).astype(BF).reshape(2, 128, 1024)
        )
        dhat.start(2 * m + 1)
        dhat.start(2 * m)
        s.sm[0:1, :] += down(d_first * x_hat_of(m))
        s.sm[1:2, :] += down(d_first)
        s.sm[5:6, 0:384] += down(turned)

    sm_core = send(s.sm, s.sm_r, KC)
    s.slope[:, 0:384] = tn(s.first[...].reshape(1024, 1024), s.dtr[...])
    dhat.after_z(3)
    dhat.along_y()
    for kk in range(2):
        for ff in range(8):
            at = [(tt * 2 + kk) * 64 + ff * 8 for tt in range(8)]
            s.ga[kk, ff] = jnp.concatenate(
                [s.slope[q : q + 8, 0:384] for q in at], axis=0
            ).astype(BF)
    ga.core(s.ga)
    gm.along_z()
    sm_core.wait_recv()
    s.sm_u[...] = s.sm[...] + s.sm_r[...]
    sm_x = [send(s.sm_u, s.sm_ru.at[j], XS[i]) for j, i in enumerate(NEAR_FIRST)]
    ga.along_x()
    act_o[...] = (s.xs[0].astype(F32) + (ob[...] + sb[...]) + act.end()).astype(BF)
    dhat.after_z(1)
    dhat.after_z(2)
    dhat.last_y()
    dhat.after_y()
    total = gm.total()
    for j in range(8):
        s.gm_f[j] = total[j * 8 : j * 8 + 8, :]
    gsw_o[:, 0:512] = total[64:96, :]
    gsw_o[:, 512:1024] = total[96:128, :]
    gow_o[:, 0:512] = total[128:136, :]
    gow_o[:, 512:1024] = total[136:144, :]
    gm.to_owners()
    wait(sm_x)
    s.sm_v[...] = s.sm_u[...] + s.sm_ru[0] + s.sm_ru[1] + s.sm_ru[2]
    sm_zh = send(s.sm_v, s.sm_rv, ZH)
    ga.along_z()
    dhat.after_z(0)
    sm_zh.wait_recv()
    total = s.sm_v[...] + s.sm_rv[...]
    for j in range(8):
        s.sm_f[j, 0:4, :] = total[0:4, j * 128 : j * 128 + 128]
        s.sm_f[j, 4:5, :] = total[5:6, 0:128]
        s.sm_f[j, 5:6, :] = total[5:6, 128:256]
        s.sm_f[j, 6:7, :] = total[4:5, j * 128 : j * 128 + 128]
        s.sm_f[j, 7:8, :] = total[5:6, 256:384]
    small_o[8:12, :] = jnp.concatenate(
        [total[5:6, 384 + j * 128 : 512 + j * 128] for j in range(4)], axis=0
    )
    small_o[12:16, :] = jnp.zeros((4, 128), F32)
    sm = WeightSum(send, me, F32, None, None, None, None, None, s.sm_f, s.sm_rf)
    sm.to_owners()
    total = ga.total()
    for j in range(8):
        s.ga_f[j] = total[j * 8 : j * 8 + 8, :]
    ga.to_owners()
    d_hat = dhat.end()
    inv = s.invs[0:128, :]
    x_hat = (s.xs[0].astype(F32) - s.mus[0:128, :]) * inv
    tok_o[...] = s.gs[0].astype(F32) + inv * (
        d_hat
        - jnp.mean(d_hat, axis=1, keepdims=True)
        - x_hat * jnp.mean(d_hat * x_hat, axis=1, keepdims=True)
    )
    gm.wait()
    for n in range(8):
        gew_o[:, pl.ds(pl.multiple_of(chip_at(n) * 512, 512), 512)] = s.gm_rf[n]
    sm.wait()
    total = s.sm_rf[0]
    for n in range(1, 8):
        total += s.sm_rf[n]
    small_o[0:4, :] = total[0:4, :]
    source = lax.rem(2 * t + k, 8)
    bias_rows = jnp.zeros((2, 128), F32)
    for n in range(8):
        bias_rows = jnp.where(chip_at(n) == source, s.sm_rf[n, 4:6, :], bias_rows)
    small_o[4:5, :] = jnp.where(a == 0, bias_rows[0:1], bias_rows[1:2])
    small_o[5:6, :] = s.sm_f[t, 6:7, :]
    small_o[6:7, :] = s.sm_f[t, 7:8, :]
    small_o[7:8, :] = jnp.zeros((1, 128), F32)
    ga.wait()
    for n in range(8):
        for o in range(3):
            at = pl.ds(pl.multiple_of(o * 1024 + chip_at(n) * 128, 128), 128)
            gtw_o[:, at] = s.ga_rf[n, :, o * 128 : o * 128 + 128]
    send.finish()


def block(pairs, pos, x, g, tw, ow, ew, sw, tb, eb, g1, b1, g2, b2, ob, sb):
    return pl.pallas_call(
        block_kernel,
        out_shape=(
            jax.ShapeDtypeStruct((128, 1024), BF),
            jax.ShapeDtypeStruct((128, 1024), F32),
            jax.ShapeDtypeStruct((8, 3072), F32),
            jax.ShapeDtypeStruct((8, 4096), F32),
            jax.ShapeDtypeStruct((8, 1024), F32),
            jax.ShapeDtypeStruct((32, 1024), F32),
            jax.ShapeDtypeStruct((16, 128), F32),
        ),
        in_specs=[pl.BlockSpec(memory_space=pltpu.SMEM), VM] + [ANY] * 6 + [VM] * 8,
        out_specs=(VM,) * 7,
        scratch_shapes=[pltpu.VMEM(shape, kind) for _, shape, kind in SCRATCH]
        + [
            pltpu.SemaphoreType.DMA((COPIES,)),
            pltpu.SemaphoreType.DMA((COPIES,)),
            pltpu.SemaphoreType.DMA((LOADS,)),
            pltpu.SMEM((32,), jnp.int32),
        ],
        compiler_params=pltpu.CompilerParams(
            collective_id=0, has_side_effects=True, vmem_limit_bytes=62 * MIB
        ),
        name="block",
    )(pairs, pos, x, g, tw, ow, ew, sw, tb, eb, g1, b1, g2, b2, ob, sb)


def results_kernel(
    act, tok, gtw, gew, gow, gsw, small,
    act_o, tok_o, gtw_o, gew_o, gow_o, gsw_o,
    fg_o, fb_o, sg_o, sb_o, tb_o, vb_o, ob_o, eb_o, hb_o,
):
    for src, dst in (
        (act, act_o), (tok, tok_o), (gtw, gtw_o), (gew, gew_o), (gow, gow_o), (gsw, gsw_o)
    ):
        dst[...] = src[...]
    k, f = lax.rem(lax.axis_index("ctx"), 2), lax.axis_index("fsdp")
    rows = small[0:8, :]
    eights = pltpu.roll(rows, lax.rem(128 - (k * 64 + f * 8), 128), 1)
    for j, dst in enumerate((fg_o, fb_o, sg_o, sb_o)):
        dst[...] = eights[j : j + 1, 0:8]
    vb_o[...] = eights[6:7, 0:8]
    ob_o[...] = eights[5:6, 0:8]
    hb_o[...] = eights[5:6, 0:8]
    tb_o[...] = pltpu.roll(rows, lax.rem(128 - f * 16, 128), 1)[4:5, 0:16]
    wide = small[pl.ds(8 + k * 2 + lax.div(f, 4), 1), :]
    wide = jnp.broadcast_to(wide, (8, 128))
    eb_o[...] = pltpu.roll(wide, lax.rem(128 - lax.rem(f, 4) * 32, 128), 1)[0:1, 0:32]


def results(*arrays):
    vectors = (8, 8, 8, 8, 16, 8, 8, 32, 8)
    return pl.pallas_call(
        results_kernel,
        out_shape=tuple(jax.ShapeDtypeStruct(v.shape, v.dtype) for v in arrays[:6])
        + tuple(jax.ShapeDtypeStruct((1, n), F32) for n in vectors),
        compiler_params=pltpu.CompilerParams(vmem_limit_bytes=62 * MIB),
        name="results",
    )(*arrays)


def shards(
    tokens_in,
    positions,
    block_pairs,
    first_gain,
    first_bias,
    second_gain,
    second_bias,
    triple_weight,
    triple_bias,
    output_weight,
    output_bias,
    expand_weight,
    expand_bias,
    shrink_weight,
    shrink_bias,
    cotangent,
):
    x, g = tokens_in.reshape(128, 1024), cotangent.reshape(128, 1024)

    def line(v):
        return v.reshape(1, -1)

    found = block(
        block_pairs.T,
        positions,
        x,
        g,
        triple_weight,
        output_weight,
        expand_weight,
        shrink_weight,
        line(triple_bias),
        line(expand_bias),
        line(first_gain),
        line(first_bias),
        line(second_gain),
        line(second_bias),
        line(output_bias),
        line(shrink_bias),
    )
    act, tok, gtw, gew, gow, gsw, fg, fb, sg, sb, tb, vb, ob, eb, hb = results(*found)
    return (
        act.reshape(tokens_in.shape),
        tok.reshape(tokens_in.shape),
        fg.reshape(8),
        fb.reshape(8),
        sg.reshape(8),
        sb.reshape(8),
        gtw,
        tb.reshape(16),
        vb.reshape(8),
        gow,
        ob.reshape(8),
        gew,
        eb.reshape(32),
        gsw,
        hb.reshape(8),
    )


def solution(mesh):
    return jax.shard_map(
        shards,
        mesh=mesh,
        in_specs=(
            P("fsdp", "ctx", None, None, None),
            P("fsdp", None),
            P(),
            P(),
            P(),
            P(),
            P(),
            P("fsdp", None),
            P(),
            P(None, "fsdp"),
            P(),
            P("fsdp", None),
            P(),
            P(None, "fsdp"),
            P(),
            P("fsdp", "ctx", None, None, None),
        ),
        out_specs=(
            P("fsdp", "ctx", None, None, None),
            P("fsdp", "ctx", None, None, None),
            P(("ctx", "fsdp")),
            P(("ctx", "fsdp")),
            P(("ctx", "fsdp")),
            P(("ctx", "fsdp")),
            P(("ctx", "fsdp"), None),
            P(("ctx", "fsdp")),
            P(("ctx", "fsdp")),
            P(("ctx", "fsdp"), None),
            P(("ctx", "fsdp")),
            P(("ctx", "fsdp"), None),
            P(("ctx", "fsdp")),
            P(("ctx", "fsdp"), None),
            P(("ctx", "fsdp")),
        ),
        check_vma=False,
    )
```

```python
import math

import jax
import jax.numpy as jnp
import numpy as np
from jax import lax
from jax.experimental import pallas as pl
from jax.experimental.pallas import tpu as pltpu
from jax.sharding import PartitionSpec as P

MESH = pl.DeviceIdType.MESH
BF, F32 = jnp.bfloat16, jnp.float32
EPS = 1e-05
BASE = 10000.0
MIB = 1 << 20
SCALE = 0.125
TILE = 256
RATES = 1.0 / BASE ** (np.arange(0, 16, 2, dtype=np.float32) / 16)

ZL, KC, ZH = (1, 0, 0, 0, 0), (0, 0, 1, 0, 0), (0, 0, 0, 0, 1)
YS = {i: (0, i, 0, 0, 0) for i in (1, 2, 3)}
XS = {i: (0, 0, 0, i, 0) for i in (1, 2, 3)}
NEAR_FIRST = (1, 3, 2)
OFFS = ((0, 0), (0, 1), (0, 3), (0, 2), (1, 0), (1, 1), (1, 3), (1, 2))
SLOT = {off: n for n, off in enumerate(OFFS)}


def origin(da, i):
    return SLOT[(da, (4 - i) % 4)]


def chips(n):
    return (*OFFS[n], 0, 0, 0)


def coords():
    c, f = lax.axis_index("ctx"), lax.axis_index("fsdp")
    return lax.div(c, 8), lax.rem(lax.div(c, 2), 4), lax.rem(c, 2), lax.div(f, 2), lax.rem(f, 2)


def device_at(me, off):
    a, b, k, x, h = (lax.rem(p + o, n) for p, o, n in zip(me, off, (2, 4, 2, 4, 2)))
    return ((a * 4 + b) * 2 + k, x * 2 + h)


def barrier(me, offs):
    sem = pltpu.get_barrier_semaphore()
    for off in offs:
        pl.semaphore_signal(sem, inc=1, device_id=device_at(me, off), device_id_type=MESH)
    pl.semaphore_wait(sem, len(offs))


class Sender:
    def __init__(self, me, send_sems, recv_sems):
        self.me, self.send_sems, self.recv_sems, self.copies = me, send_sems, recv_sems, []

    def __call__(self, src, dst, off):
        i = len(self.copies)
        copy = pltpu.make_async_remote_copy(
            src_ref=src,
            dst_ref=dst,
            send_sem=self.send_sems.at[i],
            recv_sem=self.recv_sems.at[i],
            device_id=device_at(self.me, off),
            device_id_type=MESH,
        )
        copy.start()
        self.copies.append(copy)
        return copy

    def finish(self):
        for copy in self.copies:
            copy.wait_send()


def nt(left, right):
    return lax.dot_general(left, right, (((1,), (1,)), ((), ())), preferred_element_type=F32)


def tn(left, right):
    return lax.dot_general(left, right, (((0,), (0,)), ((), ())), preferred_element_type=F32)


def nn(left, right):
    return jnp.dot(left, right, preferred_element_type=F32)


def down(v):
    return jnp.sum(v, axis=0, keepdims=True)


def lanes(shape):
    return lax.broadcasted_iota(jnp.int32, shape, 1)


def roll(v, shift):
    return pltpu.roll(v, shift, 1)


ANY = pl.BlockSpec(memory_space=pl.ANY)
VM = pl.BlockSpec(memory_space=pltpu.VMEM)


def row_sum_scratch(name, rows):
    low = 128 - rows
    return (
        (name + "_rz", (4, rows, 1024), BF),
        (name + "_t", (4, rows, 1024), BF),
        (name + "_tr", (2, rows // 2, 1024), BF),
        (name + "_rt", (2, rows, 1024), BF),
        (name + "_yr", (2, 2, low // 2, 1024), BF),
        (name + "_u", (2, 2, low, 1024), BF),
        (name + "_ry", (2, 2, low, 1024), BF),
        (name + "_w", (low, 1024), BF),
        (name + "_rw", (low, 1024), BF),
    )


COPIES = 60 + 2 * 17 + 10 + 2 * 17 + 5 + 5 + 5 + 21
LOADS = 8
TOK = (8, 128, 1024)
SCRATCH = (
    ("xs", TOK, BF),
    ("gs", TOK, BF),
    ("first", TOK, BF),
    ("second", (1024, 1024), BF),
    ("mus", (1024, 1), F32),
    ("invs", (1024, 1), F32),
    ("was", (1024, 896), BF),
    ("wos", (128, 1024), BF),
    ("wss", (512, 1024), BF),
    ("slope", (1024, 512), F32),
    ("hidden", (1024, 512), BF),
    ("dexp", (1024, 512), BF),
    ("cst", (16, 2048), F32),
    ("cs3", (32, 16, 128), F32),
    ("pk", (32, 64, 256), BF),
    ("th", (16, 64, 256), BF),
    ("pd", (32, 64, 128), BF),
    ("td", (16, 64, 128), BF),
    ("kv", (2048, 128), BF),
    ("qz", (2048, 128), BF),
    ("kvt", (128, 2048), BF),
    ("dt", (64, 2048), BF),
    ("sc", (2048, TILE), F32),
    ("es", (36, TILE, TILE), BF),
    ("acc", (2048, 128), F32),
    ("mixs", (64, 2048), F32),
    ("rsum", (8, TILE), F32),
    ("ot", (32, 64, 128), BF),
    ("o_own", (16, 64, 128), BF),
    ("o_away", (16, 64, 128), BF),
    ("o_got", (16, 64, 128), BF),
    ("dd", (32, 64, 256), BF),
    ("d_own", (16, 64, 256), BF),
    ("d_away", (16, 64, 256), BF),
    ("d_got", (16, 64, 256), BF),
    ("attn", (1024, 128), BF),
    ("dtr", (1024, 384), BF),
    ("act", TOK, BF),
    *row_sum_scratch("act", 64),
    ("dhat", TOK, BF),
    *row_sum_scratch("dhat", 32),
    ("gsh", (512, 1024), F32),
    ("gm", (2, 8, 144, 512), BF),
    ("gm_r", (8, 144, 512), BF),
    ("gm_u", (8, 144, 512), BF),
    ("gm_ru", (3, 2, 144, 512), BF),
    ("gm_v", (2, 144, 512), BF),
    ("gm_rv", (144, 512), BF),
    ("gm_f", (8, 8, 512), F32),
    ("gm_rf", (8, 8, 512), F32),
    ("go", (128, 1024), F32),
    ("ga", (2, 8, 64, 384), BF),
    ("ga_r", (8, 64, 384), BF),
    ("ga_u", (8, 64, 384), BF),
    ("ga_ru", (3, 2, 64, 384), BF),
    ("ga_v", (2, 64, 384), BF),
    ("ga_rv", (64, 384), BF),
    ("ga_f", (8, 8, 384), F32),
    ("ga_rf", (8, 8, 384), F32),
    ("sm", (8, 1024), F32),
    ("sm_r", (8, 1024), F32),
    ("sm_u", (8, 1024), F32),
    ("sm_ru", (3, 8, 1024), F32),
    ("sm_v", (8, 1024), F32),
    ("sm_rv", (8, 1024), F32),
    ("sm_f", (8, 8, 128), F32),
    ("sm_rf", (8, 8, 128), F32),
)


class Refs:
    pass


def halves(rows):
    middle = (rows.start + rows.stop) // 2
    return {1: slice(rows.start, middle), 3: slice(middle, rows.stop)}


class TokenGather:
    def __init__(self, send, dst, rows):
        self.send, self.dst = send, dst
        self.top, self.low = slice(0, rows), slice(rows, 128)
        self.zy, self.far_y, self.far_z = [], [], []

    def first(self):
        send, d = self.send, self.dst
        self.y = {i: send(d.at[0, self.low], d.at[origin(0, i), self.low], YS[i]) for i in (1, 3)}
        self.z = send(d.at[0, self.top], d.at[4, self.top], ZL)

    def rest(self):
        send, d = self.send, self.dst
        self.own_z = send(d.at[0, self.low], d.at[4, self.low], ZL)
        self.own_y = {i: send(d.at[0, self.top], d.at[origin(0, i), self.top], YS[i]) for i in (1, 3)}

    def relay(self, i, da, rows):
        part, src, dst = halves(rows)[i], origin(da, i), SLOT[(da, 2)]
        return self.send(self.dst.at[src, part], self.dst.at[dst, part], YS[i])

    def second(self):
        send, d = self.send, self.dst
        self.far = []
        for i in (1, 3):
            self.y[i].wait_recv()
            self.far.append(self.relay(i, 0, self.low))
            self.zy.append(send(d.at[origin(0, i), self.low], d.at[origin(1, i), self.low], ZL))
        self.z.wait_recv()
        self.yz = {i: send(d.at[4, self.top], d.at[origin(1, i), self.top], YS[i]) for i in (1, 3)}

    def third(self):
        send, d = self.send, self.dst
        for copy in self.far:
            copy.wait_recv()
        self.zy.append(send(d.at[3, self.low], d.at[7, self.low], ZL))
        for i in (1, 3):
            self.own_y[i].wait_recv()
            self.far_y.append(self.relay(i, 0, self.top))

    def fourth(self):
        for i in (1, 3):
            self.yz[i].wait_recv()
            self.far_z.append(self.relay(i, 1, self.top))

    def near(self):
        for copy in self.far_y:
            copy.wait_recv()

    def beside(self):
        self.own_z.wait_recv()

    def end(self):
        for copy in self.zy + self.far_z:
            copy.wait_recv()


class RowSum:
    def __init__(self, send, src, rz, t, tr, rt, yr, u, ry, w, rw):
        self.send, self.src, self.rz, self.t, self.tr, self.rt = send, src, rz, t, tr, rt
        self.yr, self.u, self.ry, self.w, self.rw = yr, u, ry, w, rw
        self.top, self.low = slice(0, rz.shape[1]), slice(rz.shape[1], 128)
        self.z, self.far, self.on = {}, {}, []

    def start(self, n):
        self.start_z(n)
        self.start_far(n)

    def start_z(self, n):
        if n > 3:
            self.z[n - 4] = self.send(self.src.at[n, self.top], self.rz.at[n - 4], ZL)

    def start_far(self, n):
        da, db = OFFS[n]
        if db == 2:
            for i, part in halves(self.low).items():
                self.far[da, i] = self.send(self.src.at[n, part], self.yr.at[da, i // 2], YS[i])

    def along_y(self):
        split = halves(self.low)
        own = halves(slice(0, self.low.stop - self.low.start))
        for da in (1, 0):
            for i in (1, 3):
                n, j = SLOT[(da, i)], i // 2
                self.far[da, i].wait_recv()
                self.u[da, j, own[i]] = (
                    self.src[n, split[i]].astype(F32) + self.yr[da, j].astype(F32)
                ).astype(BF)
                self.u[da, j, own[4 - i]] = self.src[n, split[4 - i]]
                self.far[da, i] = self.send(self.u.at[da, j], self.ry.at[da, j], YS[i])

    def after_z(self, m):
        self.z[m].wait_recv()
        total = self.src[m, self.top].astype(F32) + self.rz[m].astype(F32)
        self.t[m] = total.astype(BF)
        if m == 3:
            self.far_t = {
                i: self.send(self.t.at[3, part], self.tr.at[i // 2], YS[i])
                for i, part in halves(self.top).items()
            }

    def after_y(self):
        for i in (1, 3):
            self.far[1, i].wait_recv()
        total = self.src[4, self.low].astype(F32)
        total += self.ry[1, 0].astype(F32) + self.ry[1, 1].astype(F32)
        self.w[...] = total.astype(BF)
        self.on.append(self.send(self.w, self.rw, ZL))

    def last_y(self):
        for i, part in halves(self.top).items():
            m, j = SLOT[(0, i)], i // 2
            self.far_t[i].wait_recv()
            self.t[m, part] = (self.t[m, part].astype(F32) + self.tr[j].astype(F32)).astype(BF)
            self.on.append(self.send(self.t.at[m], self.rt.at[j], YS[i]))

    def end(self):
        for copy in [self.far[0, 1], self.far[0, 3], *self.on]:
            copy.wait_recv()
        upper = self.t[0].astype(F32) + self.rt[0].astype(F32) + self.rt[1].astype(F32)
        lower = self.src[0, self.low].astype(F32) + self.rw[...].astype(F32)
        lower += self.ry[0, 0].astype(F32) + self.ry[0, 1].astype(F32)
        return jnp.concatenate([upper, lower], axis=0)


class WeightSum:
    def __init__(self, send, me, kind, r, u, ru, v, rv, f, rf):
        self.send, self.me, self.kind = send, me, kind
        self.r, self.u, self.ru, self.v, self.rv, self.f, self.rf = r, u, ru, v, rv, f, rf

    def core(self, src):
        self.src = src
        self.sent = [self.send(src.at[1 - self.me[2]], self.r, KC)]

    def wait(self):
        for copy in self.sent:
            copy.wait_recv()

    def along_x(self):
        x = self.me[3]
        self.core_sum()
        self.sent = []
        for j, i in enumerate(NEAR_FIRST):
            there = pl.ds(lax.rem(x + i, 4) * 2, 2)
            self.sent.append(self.send(self.u.at[there], self.ru.at[j], XS[i]))

    def along_z(self):
        x, h = self.me[3], self.me[4]
        self.wait()
        for hh in range(2):
            total = self.u[x * 2 + hh].astype(F32)
            for j in range(3):
                total += self.ru[j, hh].astype(F32)
            self.v[hh] = total.astype(self.kind)
        self.sent = [self.send(self.v.at[1 - h], self.rv, ZH)]

    def core_sum(self):
        self.wait()
        k = self.me[2]

        def one(f, _):
            self.u[f] = (self.src[k, f].astype(F32) + self.r[f].astype(F32)).astype(self.kind)
            return 0

        lax.fori_loop(0, 8, one, 0)

    def total(self):
        self.wait()
        return self.v[self.me[4]].astype(F32) + self.rv[...].astype(F32)

    def to_owners(self):
        a, b = self.me[0], self.me[1]
        self.sent = []
        for n in range(1, 8):
            da, db = OFFS[n]
            there = lax.rem(a + da, 2) * 4 + lax.rem(b + db, 4)
            self.sent.append(self.send(self.f.at[there], self.rf.at[origin(da, db)], chips(n)))
        self.rf[0] = self.f[a * 4 + b]


def block_kernel(
    pairs, pos, x, g, tw, ow, ew, sw, tb, eb, g1, b1, g2, b2, ob, sb,
    act_o, tok_o, gtw_o, gew_o, gow_o, gsw_o, small_o, *scratch,
):
    s = Refs()
    for (name, _, _), ref in zip(SCRATCH, scratch):
        setattr(s, name, ref)
    ss, rs, ls, inv_slot, os, *values = scratch[len(SCRATCH) :]
    act_v, tok_v, gtw_v, gew_v, gow_v, gsw_v, small_v = values
    me = coords()
    a, b, k, xx, h = me
    t, f = a * 4 + b, xx * 2 + h
    local = []

    def load(src, dst):
        copy = pltpu.make_async_copy(src, dst, ls.at[len(local)])
        copy.start()
        local.append(copy)

    stored = []

    def store(src, dst):
        copy = pltpu.make_async_copy(src, dst, os.at[len(stored)])
        copy.start()
        stored.append(copy)

    def cols_at(ff):
        return pl.ds(pl.multiple_of(ff * 128, 128), 128)

    def pieces(ff):
        rows = pl.ds(pl.multiple_of(ff * 128 + k * 64, 64), 64)
        return (
            s.was.at[rows, 0:384],
            s.was.at[rows, 384:896],
            s.wos.at[pl.ds(pl.multiple_of(k * 64, 64), 64), cols_at(ff)],
            s.wss.at[pl.ds(pl.multiple_of(k * 256, 256), 256), cols_at(ff)],
        )

    half = pl.ds(pl.multiple_of(k * 64, 64), 64)
    mine = pl.ds(pl.multiple_of(f * 128 + k * 64, 64), 64)
    for o in range(3):
        load(
            tw.at[half, pl.ds(pl.multiple_of(o * 1024 + t * 128, 128), 128)],
            s.was.at[mine, pl.ds(o * 128, 128)],
        )
    load(ew.at[half, pl.ds(pl.multiple_of(t * 512, 512), 512)], s.was.at[mine, pl.ds(384, 512)])
    load(ow.at[pl.ds(pl.multiple_of(t * 128 + k * 64, 64), 64)], pieces(f)[2])
    load(sw.at[pl.ds(pl.multiple_of(t * 512 + k * 256, 256), 256)], pieces(f)[3])
    load(x, s.xs.at[0])
    load(g, s.gs.at[0])
    barrier(me, [*(chips(n) for n in range(1, 8)), *XS.values(), ZH, KC])
    send = Sender(me, ss, rs)

    def wait(copies):
        for copy in copies:
            copy.wait_recv()

    for copy in local:
        copy.wait()
    ways = {0: ZH, **XS}
    weights = {0: [], 1: []}

    def weights_out(ff, part, ways):
        refs = pieces(ff)[:1] if part == 0 else pieces(ff)[1:]
        sent = {i: [send(ref, ref, way) for ref in refs] for i, way in ways.items()}
        weights[part] += [send(ref, ref, KC) for ref in refs]
        return sent

    def weights_on(came, part, hh):
        for i in NEAR_FIRST:
            wait(came[i])
            weights_out(lax.rem(xx + 4 - i, 4) * 2 + hh, part, {})

    w_own = {0: weights_out(f, 0, ways)}
    xt, gt = TokenGather(send, s.xs, 96), TokenGather(send, s.gs, 96)
    xt.first()
    xt.rest()

    def chip_at(n):
        da, db = OFFS[n]
        return lax.rem(a + da, 2) * 4 + lax.rem(b + db, 4)

    def block_of(kk, n, j):
        return pairs[j, chip_at(n) * 2 + kk]

    held = [block_of(kk, n, j) for kk in range(2) for n in range(8) for j in range(2)]

    def find(j, _):
        at = jnp.int32(0)
        for q, block in enumerate(held):
            at = jnp.where(block == j, q, at)
        inv_slot[j] = at
        return 0

    lax.fori_loop(0, 32, find, 0)
    row = lax.broadcasted_iota(jnp.int32, (8, 1), 0)
    rates = jnp.zeros((8, 1), F32)
    for j in range(8):
        rates = jnp.where(row == j, float(RATES[j]), rates)
    angles = rates * pos[...].astype(F32)
    s.cst[0:8, :] = jnp.cos(angles)
    s.cst[8:16, :] = jnp.sin(angles)
    low16 = lanes((16, 128)) < 64
    for j in range(16):
        both = s.cst[:, j * 128 : j * 128 + 128]
        turned = roll(both, 64)
        s.cs3[2 * j] = jnp.where(low16, both, turned)
        s.cs3[2 * j + 1] = jnp.where(low16, turned, both)
    s.sm[...] = jnp.zeros_like(s.sm)

    def norm(n):
        rows = slice(n * 128, n * 128 + 128)
        v = s.xs[n].astype(F32)
        mean = jnp.mean(v, axis=1, keepdims=True)
        centred = v - mean
        inv = lax.rsqrt(jnp.mean(centred * centred, axis=1, keepdims=True) + EPS)
        s.mus[rows, :] = mean
        s.invs[rows, :] = inv
        x_hat = centred * inv
        s.first[n] = (x_hat * g1[...] + b1[...]).astype(BF)
        s.second[rows, :] = (x_hat * g2[...] + b2[...]).astype(BF)

    norm(0)
    fz = xx * 2 + (1 - h)
    wait(w_own[0][0])
    w_z = {0: weights_out(fz, 0, XS)}
    w_own[1] = weights_out(f, 1, ways)
    xt.second()
    xt.third()
    norm(1)
    norm(2)
    xt.fourth()
    gt.first()
    gt.rest()
    weights_on(w_own[0], 0, h)
    weights_on(w_z[0], 0, 1 - h)
    xt.near()
    norm(3)
    wait(w_own[1][0])
    w_z[1] = weights_out(fz, 1, XS)

    low = lanes((256, 128)) < 64
    low128 = lanes((16, 128)) < 64
    early = (lanes((256, 128)) & 63) < 8
    bias_at = [tb[0:1, pl.ds(pl.multiple_of(o * 1024 + t * 128, 128), 128)] for o in range(3)]
    triple_bias = jnp.concatenate(bias_at, axis=1)
    expand_bias = eb[0:1, pl.ds(pl.multiple_of(t * 512, 512), 512)]

    def deal(tiles, own, away, to, m):
        quads = pl.ds(4 * m, 4)
        for j, (head0, head1) in enumerate(tiles):
            at = slice(j * 128, j * 128 + 128)
            keep = jnp.where(k == 0, head0, head1).astype(BF).reshape(4, 64, 128)
            give = jnp.where(k == 0, head1, head0).astype(BF).reshape(4, 64, 128)
            own[pl.ds(k * 16 + 4 * m, 4), :, at] = keep
            away[quads, :, at] = give
        return send(away.at[quads], to.at[pl.ds(k * 16 + 4 * m, 4)], KC)

    def attend_in(m):
        rows = slice(m * 256, m * 256 + 256)
        tables = []
        for n in (2 * m, 2 * m + 1):
            tables.append(
                jnp.where(low128, s.cs3[block_of(k, n, 0)], s.cs3[block_of(k, n, 1)])
            )
        cs = jnp.concatenate(tables, axis=1)
        cos, sin = cs[0:8], cs[8:16]
        one, zero = jnp.ones((48, 256), F32), jnp.zeros((48, 256), F32)
        tc = jnp.concatenate([cos, cos, one, cos, cos, one], axis=0).T
        ts = jnp.concatenate([-sin, sin, zero, -sin, sin, zero], axis=0).T

        def turn(v):
            return v * tc + jnp.where(early, roll(v, 120), roll(v, 8)) * ts

        left = s.first[2 * m : 2 * m + 2].reshape(256, 1024)
        triple = nn(left, s.was[:, 0:384]) + triple_bias
        query, key, value = turn(triple[:, 0:128]), turn(triple[:, 128:256]), triple[:, 256:384]
        query *= SCALE
        zeros = jnp.zeros_like(value)
        return deal(
            (
                (jnp.where(low, key, roll(value, 64)), jnp.where(low, roll(key, 64), value)),
                (jnp.where(low, query, zeros), jnp.where(low, roll(query, 64), zeros)),
            ),
            s.pk,
            s.th,
            s.pk,
            m,
        )

    def forward_in(m):
        rows = slice(m * 256, m * 256 + 256)
        u = nn(s.second[rows, :], s.was[:, 384:896]) + expand_bias
        cdf = 0.5 * (1.0 + lax.erf(u * math.sqrt(0.5)))
        pdf = jnp.exp(-0.5 * u * u) * (1.0 / math.sqrt(2.0 * math.pi))
        s.hidden[rows, :] = (u * cdf).astype(BF)
        s.slope[rows, :] = cdf + u * pdf

    wait(weights[0])
    heads_in = [attend_in(0), attend_in(1)]
    xt.beside()
    norm(4)
    xt.end()
    for n in (5, 6, 7):
        norm(n)
    heads_in += [attend_in(2), attend_in(3)]

    wait(heads_in)
    def place(j, _):
        at = pl.ds(pl.multiple_of(j * 64, 64), 64)
        s.kv[at, :] = s.pk[inv_slot[j], :, 0:128]
        s.qz[at, :] = s.pk[inv_slot[j], :, 128:256]
        return 0

    lax.fori_loop(0, 32, place, 0, unroll=4)
    for i in range(8):
        cols = slice(i * TILE, i * TILE + TILE)
        s.kvt[:, cols] = s.kv[cols, :].astype(F32).T.astype(BF)
    seen = lax.broadcasted_iota(jnp.int32, (TILE, TILE), 0) <= lanes((TILE, TILE))

    def folded(v, op):
        parts = [v[j * 8 : j * 8 + 8] for j in range(TILE // 8)]
        while len(parts) > 1:
            parts = [op(parts[j], parts[j + 1]) for j in range(0, len(parts), 2)]
        return parts[0]

    def tile(i, j):
        return i * (i + 1) // 2 + j

    def at_tile(i):
        return slice(i * TILE, i * TILE + TILE)

    for i in range(8):
        cols = at_tile(i)
        q_i = s.qz[cols, :]
        peak = None
        for j in range(i + 1):
            score = nt(s.kv[at_tile(j), :], q_i)
            if j == i:
                score = jnp.where(seen, score, -jnp.inf)
            s.sc[at_tile(j), :] = score
            high = folded(score, jnp.maximum)
            peak = high if peak is None else jnp.maximum(peak, high)
        peak = jnp.max(peak, axis=0, keepdims=True)
        total, mix = jnp.zeros((8, TILE), F32), jnp.zeros((64, TILE), F32)
        for j in range(i + 1):
            e = jnp.exp(s.sc[at_tile(j), :] - peak)
            total += folded(e, jnp.add)
            e_low = e.astype(BF)
            s.es[tile(i, j)] = e_low
            mix += nn(s.kvt[64:128, at_tile(j)], e_low)
        inv = 1.0 / jnp.sum(total, axis=0, keepdims=True)
        mix *= inv
        s.rsum[i : i + 1, :] = inv
        s.mixs[:, cols] = mix
        out = jnp.concatenate([mix, jnp.zeros_like(mix)], axis=0).T
        s.ot[4 * i : 4 * i + 4] = out.astype(BF).reshape(4, 64, 128)
        if i == 1:
            gt.second()
        if i == 0:
            weights_on(w_own[1], 1, h)
        if i == 5:
            gt.third()
        if i == 6:
            weights_on(w_z[1], 1, 1 - h)
    for n in range(8):
        for j in range(2):
            s.o_own[2 * n + j] = s.ot[block_of(k, n, j)]
            s.o_away[2 * n + j] = s.ot[block_of(1 - k, n, j)]
    o_sent = send(s.o_away, s.o_got, KC)
    wait(weights[1])
    for m in range(4):
        forward_in(m)
    gt.fourth()

    act = RowSum(send, s.act, *(getattr(s, n) for n, _, _ in row_sum_scratch("act", 64)))
    o_sent.wait_recv()
    for m in (3, 1, 2, 0):
        rows = slice(m * 256, m * 256 + 256)
        own = s.o_own[4 * m : 4 * m + 4].reshape(256, 128).astype(F32)
        got = s.o_got[4 * m : 4 * m + 4].reshape(256, 128).astype(F32)
        head0, head1 = jnp.where(k == 0, own, got), jnp.where(k == 0, got, own)
        attn_low = jnp.where(low, head0, roll(head1, 64)).astype(BF)
        s.attn[rows, :] = attn_low
        out = nn(attn_low, s.wos[...]) + nn(s.hidden[rows, :], s.wss[...])
        s.act[2 * m : 2 * m + 2] = out.astype(BF).reshape(2, 128, 1024)
        act.start(2 * m + 1)
        act.start(2 * m)

    def back_to_heads(p):
        dmix = nt(s.gs[4 * p : 4 * p + 4].reshape(512, 1024), s.wos[...])
        for m in (2 * p, 2 * p + 1):
            part = dmix[(m - 2 * p) * 256 : (m - 2 * p) * 256 + 256]
            grads_in.append(deal(((part, roll(part, 64)),), s.pd, s.td, s.pd, m))

    def x_hat_of(m):
        rows = slice(m * 256, m * 256 + 256)
        v = s.xs[2 * m : 2 * m + 2].reshape(256, 1024).astype(F32)
        return (v - s.mus[rows, :]) * s.invs[rows, :]

    def forward_back(p):
        half = slice(p * 512, p * 512 + 512)
        d_hidden = nt(s.gs[4 * p : 4 * p + 4].reshape(512, 1024), s.wss[...])
        s.dexp[half, :] = (d_hidden * s.slope[half, :]).astype(BF)
        d_second = nt(s.dexp[half, :], s.was[:, 384:896])
        for m in (2 * p, 2 * p + 1):
            rows = slice(m * 256, m * 256 + 256)
            part = d_second[(m - 2 * p) * 256 : (m - 2 * p) * 256 + 256]
            s.dhat[2 * m : 2 * m + 2] = (part * g2[...]).astype(BF).reshape(2, 128, 1024)
            s.sm[2:3, :] += down(part * x_hat_of(m))
            s.sm[3:4, :] += down(part)
            s.sm[4:5, :] += down(s.gs[2 * m : 2 * m + 2].reshape(256, 1024).astype(F32))
            s.sm[5:6, 384:896] += down(s.dexp[rows, :].astype(F32))

    grads_in = []
    gt.near()
    back_to_heads(0)
    forward_back(0)
    gt.beside()
    gt.end()
    back_to_heads(1)
    forward_back(1)
    act.along_y()
    act.after_z(3)

    gm = WeightSum(send, me, BF, s.gm_r, s.gm_u, s.gm_ru, s.gm_v, s.gm_rv, s.gm_f, s.gm_rf)
    ga = WeightSum(send, me, BF, s.ga_r, s.ga_u, s.ga_ru, s.ga_v, s.ga_rv, s.ga_f, s.ga_rf)
    s.slope[...] = tn(s.second[...], s.dexp[...])
    s.gsh[...] = tn(s.hidden[...], s.gs[...].reshape(1024, 1024))
    s.go[...] = tn(s.attn[...], s.gs[...].reshape(1024, 1024))
    for kk in range(2):
        for ff in range(8):
            at = [(tt * 2 + kk) * 64 + ff * 8 for tt in range(8)]
            own = slice((kk * 8 + ff) * 32, (kk * 8 + ff) * 32 + 32)
            s.gm[kk, ff, 0:64, :] = jnp.concatenate(
                [s.slope[r : r + 8, :] for r in at], axis=0
            ).astype(BF)
            s.gm[kk, ff, 64:96, :] = s.gsh[own, 0:512].astype(BF)
            s.gm[kk, ff, 96:128, :] = s.gsh[own, 512:1024].astype(BF)
            r = (kk * 8 + ff) * 8
            s.gm[kk, ff, 128:144, :] = jnp.concatenate(
                [s.go[r : r + 8, 0:512], s.go[r : r + 8, 512:1024]], axis=0
            ).astype(BF)
    gm.core(s.gm)

    wait(grads_in)

    for i in range(8):
        quad = [s.pd[inv_slot[4 * i + q]].astype(F32) for q in range(4)]
        s.dt[:, at_tile(i)] = jnp.concatenate(quad, axis=0).T[0:64].astype(BF)
    for i in range(8):
        cols = at_tile(i)
        scaled = (s.dt[:, cols].astype(F32) * s.rsum[i : i + 1, :]).astype(BF).astype(F32)
        inner = jnp.sum(s.mixs[:, cols] * scaled, axis=0, keepdims=True)
        d_i = jnp.concatenate([jnp.zeros_like(scaled), scaled], axis=0).T.astype(BF)
        right = jnp.concatenate([s.qz[cols, :], d_i], axis=0)
        dq = jnp.zeros((64, TILE), F32)
        for j in range(i + 1):
            rows = at_tile(j)
            e_low = s.es[tile(i, j)]
            ds = (e_low.astype(F32) * (nt(s.kv[rows, :], d_i) - inner)).astype(BF)
            both = nn(jnp.concatenate([ds, e_low], axis=1), right)
            s.acc[rows, :] = both if i == j else s.acc[rows, :] + both
            dq += nn(s.kvt[0:64, rows], ds)
        s.mixs[:, cols] = dq * SCALE
        if i == 3:
            gm.along_x()
        if i == 6:
            act.after_y()
            act.after_z(1)
            act.after_z(2)
            act.last_y()
            act.after_z(0)

    def turned_back(v, cols):
        cos, sin = s.cst[0:8, cols], s.cst[8:16, cols]
        f1, f2 = v[0:8], v[8:16]
        return [f1 * cos + f2 * sin, f2 * cos - f1 * sin, v[16:64]]

    for i in range(8):
        cols = at_tile(i)
        tail = s.acc[cols, :]
        both = turned_back(s.mixs[:, cols], cols) + turned_back(tail.T[0:64], cols)
        s.dd[4 * i : 4 * i + 4, :, 0:128] = (
            jnp.concatenate(both, axis=0).T.astype(BF).reshape(4, 64, 128)
        )
        s.dd[4 * i : 4 * i + 4, :, 128:256] = tail.astype(BF).reshape(4, 64, 128)
    for n in range(8):
        for j in range(2):
            s.d_own[2 * n + j] = s.dd[block_of(k, n, j)]
            s.d_away[2 * n + j] = s.dd[block_of(1 - k, n, j)]
    d_sent = send(s.d_away, s.d_got, KC)

    dhat = RowSum(send, s.dhat, *(getattr(s, n) for n, _, _ in row_sum_scratch("dhat", 32)))
    d_sent.wait_recv()
    for m in (3, 1, 2, 0):
        rows = slice(m * 256, m * 256 + 256)
        quads = slice(4 * m, 4 * m + 4)
        tiles = []
        for at in (slice(0, 128), slice(128, 256)):
            own = s.d_own[quads, :, at].reshape(256, 128).astype(F32)
            got = s.d_got[quads, :, at].reshape(256, 128).astype(F32)
            tiles.append((jnp.where(k == 0, own, got), jnp.where(k == 0, got, own)))
        (p_0, p_1), (r_0, r_1) = tiles
        turned = jnp.concatenate(
            [
                jnp.where(low, p_0, roll(p_1, 64)),
                jnp.where(low, roll(p_0, 64), p_1),
                jnp.where(low, roll(r_0, 64), r_1),
            ],
            axis=1,
        )
        turned_low = turned.astype(BF)
        s.dtr[rows, :] = turned_low
        d_first = nt(turned_low, s.was[:, 0:384])
        before = s.dhat[2 * m : 2 * m + 2].reshape(256, 1024).astype(F32)
        s.dhat[2 * m : 2 * m + 2] = (
            (before + d_first * g1[...]).astype(BF).reshape(2, 128, 1024)
        )
        dhat.start(2 * m + 1)
        dhat.start(2 * m)
        s.sm[0:1, :] += down(d_first * x_hat_of(m))
        s.sm[1:2, :] += down(d_first)
        s.sm[5:6, 0:384] += down(turned)

    sm_core = send(s.sm, s.sm_r, KC)
    s.slope[:, 0:384] = tn(s.first[...].reshape(1024, 1024), s.dtr[...])
    for kk in range(2):
        for ff in range(8):
            at = [(tt * 2 + kk) * 64 + ff * 8 for tt in range(8)]
            s.ga[kk, ff] = jnp.concatenate(
                [s.slope[q : q + 8, 0:384] for q in at], axis=0
            ).astype(BF)
    ga.core(s.ga)
    dhat.after_z(3)
    dhat.along_y()
    gm.along_z()
    sm_core.wait_recv()
    s.sm_u[...] = s.sm[...] + s.sm_r[...]
    sm_x = [send(s.sm_u, s.sm_ru.at[j], XS[i]) for j, i in enumerate(NEAR_FIRST)]
    ga.along_x()
    act_v[...] = (s.xs[0].astype(F32) + (ob[...] + sb[...]) + act.end()).astype(BF)
    store(act_v, act_o)
    dhat.after_z(1)
    dhat.after_z(2)
    dhat.last_y()
    dhat.after_y()
    total = gm.total()
    for j in range(8):
        s.gm_f[j] = total[j * 8 : j * 8 + 8, :]
    gsw_v[:, 0:512] = total[64:96, :]
    gsw_v[:, 512:1024] = total[96:128, :]
    gow_v[:, 0:512] = total[128:136, :]
    gow_v[:, 512:1024] = total[136:144, :]
    store(gsw_v, gsw_o)
    store(gow_v, gow_o)
    wait(sm_x)
    s.sm_v[...] = s.sm_u[...] + s.sm_ru[0] + s.sm_ru[1] + s.sm_ru[2]
    sm_zh = send(s.sm_v, s.sm_rv, ZH)
    ga.along_z()
    gm.to_owners()
    dhat.after_z(0)
    sm_zh.wait_recv()
    total = s.sm_v[...] + s.sm_rv[...]
    for j in range(8):
        s.sm_f[j, 0:4, :] = total[0:4, j * 128 : j * 128 + 128]
        s.sm_f[j, 4:5, :] = total[5:6, 0:128]
        s.sm_f[j, 5:6, :] = total[5:6, 128:256]
        s.sm_f[j, 6:7, :] = total[4:5, j * 128 : j * 128 + 128]
        s.sm_f[j, 7:8, :] = total[5:6, 256:384]
    small_v[8:12, :] = jnp.concatenate(
        [total[5:6, 384 + j * 128 : 512 + j * 128] for j in range(4)], axis=0
    )
    small_v[12:16, :] = jnp.zeros((4, 128), F32)
    sm = WeightSum(send, me, F32, None, None, None, None, None, s.sm_f, s.sm_rf)
    sm.to_owners()
    total = ga.total()
    for j in range(8):
        s.ga_f[j] = total[j * 8 : j * 8 + 8, :]
    ga.to_owners()
    d_hat = dhat.end()
    inv = s.invs[0:128, :]
    x_hat = (s.xs[0].astype(F32) - s.mus[0:128, :]) * inv
    tok_v[...] = s.gs[0].astype(F32) + inv * (
        d_hat
        - jnp.mean(d_hat, axis=1, keepdims=True)
        - x_hat * jnp.mean(d_hat * x_hat, axis=1, keepdims=True)
    )
    store(tok_v, tok_o)
    gm.wait()
    for n in range(8):
        gew_v[:, pl.ds(pl.multiple_of(chip_at(n) * 512, 512), 512)] = s.gm_rf[n]
    store(gew_v, gew_o)
    sm.wait()
    total = s.sm_rf[0]
    for n in range(1, 8):
        total += s.sm_rf[n]
    small_v[0:4, :] = total[0:4, :]
    source = lax.rem(2 * t + k, 8)
    bias_rows = jnp.zeros((2, 128), F32)
    for n in range(8):
        bias_rows = jnp.where(chip_at(n) == source, s.sm_rf[n, 4:6, :], bias_rows)
    small_v[4:5, :] = jnp.where(a == 0, bias_rows[0:1], bias_rows[1:2])
    small_v[5:6, :] = s.sm_f[t, 6:7, :]
    small_v[6:7, :] = s.sm_f[t, 7:8, :]
    small_v[7:8, :] = jnp.zeros((1, 128), F32)
    store(small_v, small_o)
    ga.wait()
    for n in range(8):
        for o in range(3):
            at = pl.ds(pl.multiple_of(o * 1024 + chip_at(n) * 128, 128), 128)
            gtw_v[:, at] = s.ga_rf[n, :, o * 128 : o * 128 + 128]
    store(gtw_v, gtw_o)
    for copy in stored:
        copy.wait()
    send.finish()


RESULTS = (
    ((128, 1024), BF),
    ((128, 1024), F32),
    ((8, 3072), F32),
    ((8, 4096), F32),
    ((8, 1024), F32),
    ((32, 1024), F32),
    ((16, 128), F32),
)


def block(pairs, pos, x, g, tw, ow, ew, sw, tb, eb, g1, b1, g2, b2, ob, sb):
    return pl.pallas_call(
        block_kernel,
        out_shape=tuple(jax.ShapeDtypeStruct(*result) for result in RESULTS),
        in_specs=[pl.BlockSpec(memory_space=pltpu.SMEM), VM] + [ANY] * 6 + [VM] * 8,
        out_specs=(ANY,) * 7,
        scratch_shapes=[pltpu.VMEM(shape, kind) for _, shape, kind in SCRATCH]
        + [
            pltpu.SemaphoreType.DMA((COPIES,)),
            pltpu.SemaphoreType.DMA((COPIES,)),
            pltpu.SemaphoreType.DMA((LOADS,)),
            pltpu.SMEM((32,), jnp.int32),
            pltpu.SemaphoreType.DMA((7,)),
        ]
        + [pltpu.VMEM(*result) for result in RESULTS],
        compiler_params=pltpu.CompilerParams(
            collective_id=0, has_side_effects=True, vmem_limit_bytes=62 * MIB
        ),
        name="block",
    )(pairs, pos, x, g, tw, ow, ew, sw, tb, eb, g1, b1, g2, b2, ob, sb)


def results_kernel(
    act, tok, gtw, gew, gow, gsw, small,
    act_o, tok_o, gtw_o, gew_o, gow_o, gsw_o,
    fg_o, fb_o, sg_o, sb_o, tb_o, vb_o, ob_o, eb_o, hb_o,
):
    for src, dst in (
        (act, act_o), (tok, tok_o), (gtw, gtw_o), (gew, gew_o), (gow, gow_o), (gsw, gsw_o)
    ):
        dst[...] = src[...]
    k, f = lax.rem(lax.axis_index("ctx"), 2), lax.axis_index("fsdp")
    rows = small[0:8, :]
    eights = pltpu.roll(rows, lax.rem(128 - (k * 64 + f * 8), 128), 1)
    for j, dst in enumerate((fg_o, fb_o, sg_o, sb_o)):
        dst[...] = eights[j : j + 1, 0:8]
    vb_o[...] = eights[6:7, 0:8]
    ob_o[...] = eights[5:6, 0:8]
    hb_o[...] = eights[5:6, 0:8]
    tb_o[...] = pltpu.roll(rows, lax.rem(128 - f * 16, 128), 1)[4:5, 0:16]
    wide = small[pl.ds(8 + k * 2 + lax.div(f, 4), 1), :]
    wide = jnp.broadcast_to(wide, (8, 128))
    eb_o[...] = pltpu.roll(wide, lax.rem(128 - lax.rem(f, 4) * 32, 128), 1)[0:1, 0:32]


def results(*arrays):
    vectors = (8, 8, 8, 8, 16, 8, 8, 32, 8)
    return pl.pallas_call(
        results_kernel,
        out_shape=tuple(jax.ShapeDtypeStruct(v.shape, v.dtype) for v in arrays[:6])
        + tuple(jax.ShapeDtypeStruct((1, n), F32) for n in vectors),
        compiler_params=pltpu.CompilerParams(vmem_limit_bytes=62 * MIB),
        name="results",
    )(*arrays)


def shards(
    tokens_in,
    positions,
    block_pairs,
    first_gain,
    first_bias,
    second_gain,
    second_bias,
    triple_weight,
    triple_bias,
    output_weight,
    output_bias,
    expand_weight,
    expand_bias,
    shrink_weight,
    shrink_bias,
    cotangent,
):
    x, g = tokens_in.reshape(128, 1024), cotangent.reshape(128, 1024)

    def line(v):
        return v.reshape(1, -1)

    found = block(
        block_pairs.T,
        positions,
        x,
        g,
        triple_weight,
        output_weight,
        expand_weight,
        shrink_weight,
        line(triple_bias),
        line(expand_bias),
        line(first_gain),
        line(first_bias),
        line(second_gain),
        line(second_bias),
        line(output_bias),
        line(shrink_bias),
    )
    act, tok, gtw, gew, gow, gsw, fg, fb, sg, sb, tb, vb, ob, eb, hb = results(*found)
    return (
        act.reshape(tokens_in.shape),
        tok.reshape(tokens_in.shape),
        fg.reshape(8),
        fb.reshape(8),
        sg.reshape(8),
        sb.reshape(8),
        gtw,
        tb.reshape(16),
        vb.reshape(8),
        gow,
        ob.reshape(8),
        gew,
        eb.reshape(32),
        gsw,
        hb.reshape(8),
    )


def solution(mesh):
    return jax.shard_map(
        shards,
        mesh=mesh,
        in_specs=(
            P("fsdp", "ctx", None, None, None),
            P("fsdp", None),
            P(),
            P(),
            P(),
            P(),
            P(),
            P("fsdp", None),
            P(),
            P(None, "fsdp"),
            P(),
            P("fsdp", None),
            P(),
            P(None, "fsdp"),
            P(),
            P("fsdp", "ctx", None, None, None),
        ),
        out_specs=(
            P("fsdp", "ctx", None, None, None),
            P("fsdp", "ctx", None, None, None),
            P(("ctx", "fsdp")),
            P(("ctx", "fsdp")),
            P(("ctx", "fsdp")),
            P(("ctx", "fsdp")),
            P(("ctx", "fsdp"), None),
            P(("ctx", "fsdp")),
            P(("ctx", "fsdp")),
            P(("ctx", "fsdp"), None),
            P(("ctx", "fsdp")),
            P(("ctx", "fsdp"), None),
            P(("ctx", "fsdp")),
            P(("ctx", "fsdp"), None),
            P(("ctx", "fsdp")),
        ),
        check_vma=False,
    )
```

```python
import math

import jax
import jax.numpy as jnp
import numpy as np
from jax import lax
from jax.experimental import pallas as pl
from jax.experimental.pallas import tpu as pltpu
from jax.sharding import PartitionSpec as P

MESH = pl.DeviceIdType.MESH
BF, F32 = jnp.bfloat16, jnp.float32
EPS = 1e-05
BASE = 10000.0
MIB = 1 << 20
SCALE = 0.125
TILE = 256
RATES = 1.0 / BASE ** (np.arange(0, 16, 2, dtype=np.float32) / 16)

ZL, KC, ZH = (1, 0, 0, 0, 0), (0, 0, 1, 0, 0), (0, 0, 0, 0, 1)
YS = {i: (0, i, 0, 0, 0) for i in (1, 2, 3)}
XS = {i: (0, 0, 0, i, 0) for i in (1, 2, 3)}
NEAR_FIRST = (1, 3, 2)
OFFS = ((0, 0), (0, 1), (0, 3), (0, 2), (1, 0), (1, 1), (1, 3), (1, 2))
SLOT = {off: n for n, off in enumerate(OFFS)}


def origin(da, i):
    return SLOT[(da, (4 - i) % 4)]


def chips(n):
    return (*OFFS[n], 0, 0, 0)


def coords():
    c, f = lax.axis_index("ctx"), lax.axis_index("fsdp")
    return lax.div(c, 8), lax.rem(lax.div(c, 2), 4), lax.rem(c, 2), lax.div(f, 2), lax.rem(f, 2)


def device_at(me, off):
    a, b, k, x, h = (lax.rem(p + o, n) for p, o, n in zip(me, off, (2, 4, 2, 4, 2)))
    return ((a * 4 + b) * 2 + k, x * 2 + h)


def barrier(me, offs):
    sem = pltpu.get_barrier_semaphore()
    for off in offs:
        pl.semaphore_signal(sem, inc=1, device_id=device_at(me, off), device_id_type=MESH)
    pl.semaphore_wait(sem, len(offs))


class Sender:
    def __init__(self, me, send_sems, recv_sems):
        self.me, self.send_sems, self.recv_sems, self.copies = me, send_sems, recv_sems, []

    def __call__(self, src, dst, off):
        i = len(self.copies)
        copy = pltpu.make_async_remote_copy(
            src_ref=src,
            dst_ref=dst,
            send_sem=self.send_sems.at[i],
            recv_sem=self.recv_sems.at[i],
            device_id=device_at(self.me, off),
            device_id_type=MESH,
        )
        copy.start()
        self.copies.append(copy)
        return copy

    def finish(self):
        for copy in self.copies:
            copy.wait_send()


def nt(left, right):
    return lax.dot_general(left, right, (((1,), (1,)), ((), ())), preferred_element_type=F32)


def tn(left, right):
    return lax.dot_general(left, right, (((0,), (0,)), ((), ())), preferred_element_type=F32)


def nn(left, right):
    return jnp.dot(left, right, preferred_element_type=F32)


def down(v):
    return jnp.sum(v, axis=0, keepdims=True)


def lanes(shape):
    return lax.broadcasted_iota(jnp.int32, shape, 1)


def roll(v, shift):
    return pltpu.roll(v, shift, 1)


ANY = pl.BlockSpec(memory_space=pl.ANY)
VM = pl.BlockSpec(memory_space=pltpu.VMEM)


def row_sum_scratch(name, rows):
    low = 128 - rows
    return (
        (name + "_rz", (4, rows, 1024), BF),
        (name + "_t", (4, rows, 1024), BF),
        (name + "_tr", (2, rows // 2, 1024), BF),
        (name + "_rt", (2, rows, 1024), BF),
        (name + "_yr", (2, 2, low // 2, 1024), BF),
        (name + "_u", (2, 2, low, 1024), BF),
        (name + "_ry", (2, 2, low, 1024), BF),
        (name + "_w", (low, 1024), BF),
        (name + "_rw", (low, 1024), BF),
    )


COPIES = 60 + 2 * 17 + 10 + 2 * 17 + 5 + 5 + 5 + 21
LOADS = 8
TOK = (8, 128, 1024)
SCRATCH = (
    ("xs", TOK, BF),
    ("gs", TOK, BF),
    ("first", TOK, BF),
    ("second", (1024, 1024), BF),
    ("mus", (1024, 1), F32),
    ("invs", (1024, 1), F32),
    ("was", (1024, 896), BF),
    ("wos", (128, 1024), BF),
    ("wss", (512, 1024), BF),
    ("slope", (1024, 512), F32),
    ("hidden", (1024, 512), BF),
    ("dexp", (1024, 512), BF),
    ("cst", (16, 2048), F32),
    ("cs3", (32, 16, 128), F32),
    ("pk", (32, 64, 256), BF),
    ("th", (16, 64, 256), BF),
    ("pd", (32, 64, 128), BF),
    ("td", (16, 64, 128), BF),
    ("kv", (2048, 128), BF),
    ("qz", (2048, 128), BF),
    ("kvt", (128, 2048), BF),
    ("dt", (64, 2048), BF),
    ("sc", (2048, TILE), F32),
    ("es", (36, TILE, TILE), BF),
    ("acc", (2048, 128), F32),
    ("mixs", (64, 2048), F32),
    ("rsum", (8, TILE), F32),
    ("ot", (32, 64, 128), BF),
    ("o_own", (16, 64, 128), BF),
    ("o_away", (16, 64, 128), BF),
    ("o_got", (16, 64, 128), BF),
    ("dd", (32, 64, 256), BF),
    ("d_own", (16, 64, 256), BF),
    ("d_away", (16, 64, 256), BF),
    ("d_got", (16, 64, 256), BF),
    ("attn", (1024, 128), BF),
    ("dtr", (1024, 384), BF),
    ("act", TOK, BF),
    *row_sum_scratch("act", 64),
    ("dhat", TOK, BF),
    *row_sum_scratch("dhat", 32),
    ("gsh", (512, 1024), F32),
    ("gm", (2, 8, 144, 512), BF),
    ("gm_r", (8, 144, 512), BF),
    ("gm_u", (8, 144, 512), BF),
    ("gm_ru", (3, 2, 144, 512), BF),
    ("gm_v", (2, 144, 512), BF),
    ("gm_rv", (144, 512), BF),
    ("gm_f", (8, 8, 512), F32),
    ("gm_rf", (8, 8, 512), F32),
    ("go", (128, 1024), F32),
    ("ga", (2, 8, 64, 384), BF),
    ("ga_r", (8, 64, 384), BF),
    ("ga_u", (8, 64, 384), BF),
    ("ga_ru", (3, 2, 64, 384), BF),
    ("ga_v", (2, 64, 384), BF),
    ("ga_rv", (64, 384), BF),
    ("ga_f", (8, 8, 384), F32),
    ("ga_rf", (8, 8, 384), F32),
    ("sm", (8, 1024), F32),
    ("sm_r", (8, 1024), F32),
    ("sm_u", (8, 1024), F32),
    ("sm_ru", (3, 8, 1024), F32),
    ("sm_v", (8, 1024), F32),
    ("sm_rv", (8, 1024), F32),
    ("sm_f", (8, 8, 128), F32),
    ("sm_rf", (8, 8, 128), F32),
)


class Refs:
    pass


def halves(rows):
    middle = (rows.start + rows.stop) // 2
    return {1: slice(rows.start, middle), 3: slice(middle, rows.stop)}


class TokenGather:
    def __init__(self, send, dst, rows):
        self.send, self.dst = send, dst
        self.top, self.low = slice(0, rows), slice(rows, 128)
        self.zy, self.far_y, self.far_z = [], [], []

    def first(self):
        send, d = self.send, self.dst
        self.y = {i: send(d.at[0, self.low], d.at[origin(0, i), self.low], YS[i]) for i in (1, 3)}
        self.z = send(d.at[0, self.top], d.at[4, self.top], ZL)

    def rest(self):
        send, d = self.send, self.dst
        self.own_z = send(d.at[0, self.low], d.at[4, self.low], ZL)
        self.own_y = {i: send(d.at[0, self.top], d.at[origin(0, i), self.top], YS[i]) for i in (1, 3)}

    def relay(self, i, da, rows):
        part, src, dst = halves(rows)[i], origin(da, i), SLOT[(da, 2)]
        return self.send(self.dst.at[src, part], self.dst.at[dst, part], YS[i])

    def second(self):
        send, d = self.send, self.dst
        self.far = []
        for i in (1, 3):
            self.y[i].wait_recv()
            self.far.append(self.relay(i, 0, self.low))
            self.zy.append(send(d.at[origin(0, i), self.low], d.at[origin(1, i), self.low], ZL))
        self.z.wait_recv()
        self.yz = {i: send(d.at[4, self.top], d.at[origin(1, i), self.top], YS[i]) for i in (1, 3)}

    def third(self):
        send, d = self.send, self.dst
        for copy in self.far:
            copy.wait_recv()
        self.zy.append(send(d.at[3, self.low], d.at[7, self.low], ZL))
        for i in (1, 3):
            self.own_y[i].wait_recv()
            self.far_y.append(self.relay(i, 0, self.top))

    def fourth(self):
        for i in (1, 3):
            self.yz[i].wait_recv()
            self.far_z.append(self.relay(i, 1, self.top))

    def near(self):
        for copy in self.far_y:
            copy.wait_recv()

    def beside(self):
        self.own_z.wait_recv()

    def end(self):
        for copy in self.zy + self.far_z:
            copy.wait_recv()


class RowSum:
    def __init__(self, send, src, rz, t, tr, rt, yr, u, ry, w, rw):
        self.send, self.src, self.rz, self.t, self.tr, self.rt = send, src, rz, t, tr, rt
        self.yr, self.u, self.ry, self.w, self.rw = yr, u, ry, w, rw
        self.top, self.low = slice(0, rz.shape[1]), slice(rz.shape[1], 128)
        self.z, self.far, self.on = {}, {}, []

    def start(self, n):
        self.start_z(n)
        self.start_far(n)

    def start_z(self, n):
        if n > 3:
            self.z[n - 4] = self.send(self.src.at[n, self.top], self.rz.at[n - 4], ZL)

    def start_far(self, n):
        da, db = OFFS[n]
        if db == 2:
            for i, part in halves(self.low).items():
                self.far[da, i] = self.send(self.src.at[n, part], self.yr.at[da, i // 2], YS[i])

    def along_y(self):
        split = halves(self.low)
        own = halves(slice(0, self.low.stop - self.low.start))
        for da in (1, 0):
            for i in (1, 3):
                n, j = SLOT[(da, i)], i // 2
                self.far[da, i].wait_recv()
                self.u[da, j, own[i]] = (
                    self.src[n, split[i]].astype(F32) + self.yr[da, j].astype(F32)
                ).astype(BF)
                self.u[da, j, own[4 - i]] = self.src[n, split[4 - i]]
                self.far[da, i] = self.send(self.u.at[da, j], self.ry.at[da, j], YS[i])

    def after_z(self, m):
        self.z[m].wait_recv()
        total = self.src[m, self.top].astype(F32) + self.rz[m].astype(F32)
        self.t[m] = total.astype(BF)
        if m == 3:
            self.far_t = {
                i: self.send(self.t.at[3, part], self.tr.at[i // 2], YS[i])
                for i, part in halves(self.top).items()
            }

    def after_y(self):
        for i in (1, 3):
            self.far[1, i].wait_recv()
        total = self.src[4, self.low].astype(F32)
        total += self.ry[1, 0].astype(F32) + self.ry[1, 1].astype(F32)
        self.w[...] = total.astype(BF)
        self.on.append(self.send(self.w, self.rw, ZL))

    def last_y(self):
        for i, part in halves(self.top).items():
            m, j = SLOT[(0, i)], i // 2
            self.far_t[i].wait_recv()
            self.t[m, part] = (self.t[m, part].astype(F32) + self.tr[j].astype(F32)).astype(BF)
            self.on.append(self.send(self.t.at[m], self.rt.at[j], YS[i]))

    def end(self):
        for copy in [self.far[0, 1], self.far[0, 3], *self.on]:
            copy.wait_recv()
        upper = self.t[0].astype(F32) + self.rt[0].astype(F32) + self.rt[1].astype(F32)
        lower = self.src[0, self.low].astype(F32) + self.rw[...].astype(F32)
        lower += self.ry[0, 0].astype(F32) + self.ry[0, 1].astype(F32)
        return jnp.concatenate([upper, lower], axis=0)


class WeightSum:
    def __init__(self, send, me, kind, r, u, ru, v, rv, f, rf):
        self.send, self.me, self.kind = send, me, kind
        self.r, self.u, self.ru, self.v, self.rv, self.f, self.rf = r, u, ru, v, rv, f, rf

    def core(self, src):
        self.src = src
        self.sent = [self.send(src.at[1 - self.me[2]], self.r, KC)]

    def wait(self):
        for copy in self.sent:
            copy.wait_recv()

    def along_x(self):
        x = self.me[3]
        self.core_sum()
        self.sent = []
        for j, i in enumerate(NEAR_FIRST):
            there = pl.ds(lax.rem(x + i, 4) * 2, 2)
            self.sent.append(self.send(self.u.at[there], self.ru.at[j], XS[i]))

    def along_z(self):
        x, h = self.me[3], self.me[4]
        self.wait()
        for hh in range(2):
            total = self.u[x * 2 + hh].astype(F32)
            for j in range(3):
                total += self.ru[j, hh].astype(F32)
            self.v[hh] = total.astype(self.kind)
        self.sent = [self.send(self.v.at[1 - h], self.rv, ZH)]

    def core_sum(self):
        self.wait()
        k = self.me[2]

        def one(f, _):
            self.u[f] = (self.src[k, f].astype(F32) + self.r[f].astype(F32)).astype(self.kind)
            return 0

        lax.fori_loop(0, 8, one, 0)

    def total(self):
        self.wait()
        return self.v[self.me[4]].astype(F32) + self.rv[...].astype(F32)

    def to_owners(self):
        a, b = self.me[0], self.me[1]
        self.sent = []
        for n in range(1, 8):
            da, db = OFFS[n]
            there = lax.rem(a + da, 2) * 4 + lax.rem(b + db, 4)
            self.sent.append(self.send(self.f.at[there], self.rf.at[origin(da, db)], chips(n)))
        self.rf[0] = self.f[a * 4 + b]


def block_kernel(
    pairs, pos, x, g, tw, ow, ew, sw, tb, eb, g1, b1, g2, b2, ob, sb,
    act_o, tok_o, gtw_o, gew_o, gow_o, gsw_o, small_o, *scratch,
):
    s = Refs()
    for (name, _, _), ref in zip(SCRATCH, scratch):
        setattr(s, name, ref)
    ss, rs, ls, inv_slot, os, *values = scratch[len(SCRATCH) :]
    act_v, tok_v, gtw_v, gew_v, gow_v, gsw_v, small_v = values
    me = coords()
    a, b, k, xx, h = me
    t, f = a * 4 + b, xx * 2 + h
    local = []

    def load(src, dst):
        copy = pltpu.make_async_copy(src, dst, ls.at[len(local)])
        copy.start()
        local.append(copy)

    stored = []

    def store(src, dst):
        copy = pltpu.make_async_copy(src, dst, os.at[len(stored)])
        copy.start()
        stored.append(copy)

    def cols_at(ff):
        return pl.ds(pl.multiple_of(ff * 128, 128), 128)

    def pieces(ff):
        rows = pl.ds(pl.multiple_of(ff * 128 + k * 64, 64), 64)
        return (
            s.was.at[rows, 0:384],
            s.was.at[rows, 384:896],
            s.wos.at[pl.ds(pl.multiple_of(k * 64, 64), 64), cols_at(ff)],
            s.wss.at[pl.ds(pl.multiple_of(k * 256, 256), 256), cols_at(ff)],
        )

    half = pl.ds(pl.multiple_of(k * 64, 64), 64)
    mine = pl.ds(pl.multiple_of(f * 128 + k * 64, 64), 64)
    for o in range(3):
        load(
            tw.at[half, pl.ds(pl.multiple_of(o * 1024 + t * 128, 128), 128)],
            s.was.at[mine, pl.ds(o * 128, 128)],
        )
    load(ew.at[half, pl.ds(pl.multiple_of(t * 512, 512), 512)], s.was.at[mine, pl.ds(384, 512)])
    load(ow.at[pl.ds(pl.multiple_of(t * 128 + k * 64, 64), 64)], pieces(f)[2])
    load(sw.at[pl.ds(pl.multiple_of(t * 512 + k * 256, 256), 256)], pieces(f)[3])
    load(x, s.xs.at[0])
    load(g, s.gs.at[0])
    barrier(me, [*(chips(n) for n in range(1, 8)), *XS.values(), ZH, KC])
    send = Sender(me, ss, rs)

    def wait(copies):
        for copy in copies:
            copy.wait_recv()

    for copy in local:
        copy.wait()
    ways = {0: ZH, **XS}
    weights = {0: [], 1: []}

    def weights_out(ff, part, ways):
        refs = pieces(ff)[:1] if part == 0 else pieces(ff)[1:]
        sent = {i: [send(ref, ref, way) for ref in refs] for i, way in ways.items()}
        weights[part] += [send(ref, ref, KC) for ref in refs]
        return sent

    def weights_on(came, part, hh):
        for i in NEAR_FIRST:
            wait(came[i])
            weights_out(lax.rem(xx + 4 - i, 4) * 2 + hh, part, {})

    w_own = {0: weights_out(f, 0, ways)}
    xt, gt = TokenGather(send, s.xs, 96), TokenGather(send, s.gs, 96)
    xt.first()
    xt.rest()

    def chip_at(n):
        da, db = OFFS[n]
        return lax.rem(a + da, 2) * 4 + lax.rem(b + db, 4)

    def block_of(kk, n, j):
        return pairs[j, chip_at(n) * 2 + kk]

    held = [block_of(kk, n, j) for kk in range(2) for n in range(8) for j in range(2)]

    def find(j, _):
        at = jnp.int32(0)
        for q, block in enumerate(held):
            at = jnp.where(block == j, q, at)
        inv_slot[j] = at
        return 0

    lax.fori_loop(0, 32, find, 0)
    row = lax.broadcasted_iota(jnp.int32, (8, 1), 0)
    rates = jnp.zeros((8, 1), F32)
    for j in range(8):
        rates = jnp.where(row == j, float(RATES[j]), rates)
    angles = rates * pos[...].astype(F32)
    s.cst[0:8, :] = jnp.cos(angles)
    s.cst[8:16, :] = jnp.sin(angles)
    low16 = lanes((16, 128)) < 64
    for j in range(16):
        both = s.cst[:, j * 128 : j * 128 + 128]
        turned = roll(both, 64)
        s.cs3[2 * j] = jnp.where(low16, both, turned)
        s.cs3[2 * j + 1] = jnp.where(low16, turned, both)
    s.sm[...] = jnp.zeros_like(s.sm)

    def norm(n):
        rows = slice(n * 128, n * 128 + 128)
        v = s.xs[n].astype(F32)
        mean = jnp.mean(v, axis=1, keepdims=True)
        centred = v - mean
        inv = lax.rsqrt(jnp.mean(centred * centred, axis=1, keepdims=True) + EPS)
        s.mus[rows, :] = mean
        s.invs[rows, :] = inv
        x_hat = centred * inv
        s.first[n] = (x_hat * g1[...] + b1[...]).astype(BF)
        s.second[rows, :] = (x_hat * g2[...] + b2[...]).astype(BF)

    norm(0)
    fz = xx * 2 + (1 - h)
    wait(w_own[0][0])
    w_z = {0: weights_out(fz, 0, XS)}
    w_own[1] = weights_out(f, 1, ways)
    xt.second()
    xt.third()
    norm(1)
    norm(2)
    xt.fourth()
    gt.first()
    gt.rest()
    weights_on(w_own[0], 0, h)
    weights_on(w_z[0], 0, 1 - h)
    xt.near()
    norm(3)
    wait(w_own[1][0])
    w_z[1] = weights_out(fz, 1, XS)

    low = lanes((256, 128)) < 64
    low128 = lanes((16, 128)) < 64
    early = (lanes((256, 128)) & 63) < 8
    bias_at = [tb[0:1, pl.ds(pl.multiple_of(o * 1024 + t * 128, 128), 128)] for o in range(3)]
    triple_bias = jnp.concatenate(bias_at, axis=1)
    expand_bias = eb[0:1, pl.ds(pl.multiple_of(t * 512, 512), 512)]

    def deal(tiles, own, away, to, m):
        quads = pl.ds(4 * m, 4)
        for j, (head0, head1) in enumerate(tiles):
            at = slice(j * 128, j * 128 + 128)
            keep = jnp.where(k == 0, head0, head1).astype(BF).reshape(4, 64, 128)
            give = jnp.where(k == 0, head1, head0).astype(BF).reshape(4, 64, 128)
            own[pl.ds(k * 16 + 4 * m, 4), :, at] = keep
            away[quads, :, at] = give
        return send(away.at[quads], to.at[pl.ds(k * 16 + 4 * m, 4)], KC)

    def attend_in(m):
        rows = slice(m * 256, m * 256 + 256)
        tables = []
        for n in (2 * m, 2 * m + 1):
            tables.append(
                jnp.where(low128, s.cs3[block_of(k, n, 0)], s.cs3[block_of(k, n, 1)])
            )
        cs = jnp.concatenate(tables, axis=1)
        cos, sin = cs[0:8], cs[8:16]
        one, zero = jnp.ones((48, 256), F32), jnp.zeros((48, 256), F32)
        tc = jnp.concatenate([cos, cos, one, cos, cos, one], axis=0).T
        ts = jnp.concatenate([-sin, sin, zero, -sin, sin, zero], axis=0).T

        def turn(v):
            return v * tc + jnp.where(early, roll(v, 120), roll(v, 8)) * ts

        left = s.first[2 * m : 2 * m + 2].reshape(256, 1024)
        triple = nn(left, s.was[:, 0:384]) + triple_bias
        query, key, value = turn(triple[:, 0:128]), turn(triple[:, 128:256]), triple[:, 256:384]
        query *= SCALE
        zeros = jnp.zeros_like(value)
        return deal(
            (
                (jnp.where(low, key, roll(value, 64)), jnp.where(low, roll(key, 64), value)),
                (jnp.where(low, query, zeros), jnp.where(low, roll(query, 64), zeros)),
            ),
            s.pk,
            s.th,
            s.pk,
            m,
        )

    def forward_in(m):
        rows = slice(m * 256, m * 256 + 256)
        u = nn(s.second[rows, :], s.was[:, 384:896]) + expand_bias
        cdf = 0.5 * (1.0 + lax.erf(u * math.sqrt(0.5)))
        pdf = jnp.exp(-0.5 * u * u) * (1.0 / math.sqrt(2.0 * math.pi))
        s.hidden[rows, :] = (u * cdf).astype(BF)
        s.slope[rows, :] = cdf + u * pdf

    wait(weights[0])
    heads_in = [attend_in(0), attend_in(1)]
    xt.beside()
    norm(4)
    xt.end()
    for n in (5, 6, 7):
        norm(n)
    heads_in += [attend_in(2), attend_in(3)]

    wait(heads_in)
    def place(j, _):
        at = pl.ds(pl.multiple_of(j * 64, 64), 64)
        s.kv[at, :] = s.pk[inv_slot[j], :, 0:128]
        s.qz[at, :] = s.pk[inv_slot[j], :, 128:256]
        return 0

    lax.fori_loop(0, 32, place, 0, unroll=4)
    for i in range(8):
        cols = slice(i * TILE, i * TILE + TILE)
        s.kvt[:, cols] = s.kv[cols, :].astype(F32).T.astype(BF)
    seen = lax.broadcasted_iota(jnp.int32, (TILE, TILE), 0) <= lanes((TILE, TILE))

    def folded(v, op):
        parts = [v[j * 8 : j * 8 + 8] for j in range(TILE // 8)]
        while len(parts) > 1:
            parts = [op(parts[j], parts[j + 1]) for j in range(0, len(parts), 2)]
        return parts[0]

    def tile(i, j):
        return i * (i + 1) // 2 + j

    def at_tile(i):
        return slice(i * TILE, i * TILE + TILE)

    for i in range(8):
        cols = at_tile(i)
        q_i = s.qz[cols, :]
        peak = None
        for j in range(i + 1):
            score = nt(s.kv[at_tile(j), :], q_i)
            if j == i:
                score = jnp.where(seen, score, -jnp.inf)
            s.sc[at_tile(j), :] = score
            high = folded(score, jnp.maximum)
            peak = high if peak is None else jnp.maximum(peak, high)
        peak = jnp.max(peak, axis=0, keepdims=True)
        total, mix = jnp.zeros((8, TILE), F32), jnp.zeros((64, TILE), F32)
        for j in range(i + 1):
            e = jnp.exp(s.sc[at_tile(j), :] - peak)
            total += folded(e, jnp.add)
            e_low = e.astype(BF)
            s.es[tile(i, j)] = e_low
            mix += nn(s.kvt[64:128, at_tile(j)], e_low)
        inv = 1.0 / jnp.sum(total, axis=0, keepdims=True)
        mix *= inv
        s.rsum[i : i + 1, :] = inv
        s.mixs[:, cols] = mix
        out = jnp.concatenate([mix, jnp.zeros_like(mix)], axis=0).T
        s.ot[4 * i : 4 * i + 4] = out.astype(BF).reshape(4, 64, 128)
        if i == 1:
            gt.second()
        if i == 0:
            weights_on(w_own[1], 1, h)
        if i == 5:
            gt.third()
        if i == 6:
            weights_on(w_z[1], 1, 1 - h)
    for n in range(8):
        for j in range(2):
            s.o_own[2 * n + j] = s.ot[block_of(k, n, j)]
            s.o_away[2 * n + j] = s.ot[block_of(1 - k, n, j)]
    o_sent = send(s.o_away, s.o_got, KC)
    wait(weights[1])
    for m in range(4):
        forward_in(m)
    gt.fourth()

    act = RowSum(send, s.act, *(getattr(s, n) for n, _, _ in row_sum_scratch("act", 64)))
    o_sent.wait_recv()
    for p in (1, 0):
        for m in (2 * p + 1, 2 * p):
            rows = slice(m * 256, m * 256 + 256)
            own = s.o_own[4 * m : 4 * m + 4].reshape(256, 128).astype(F32)
            got = s.o_got[4 * m : 4 * m + 4].reshape(256, 128).astype(F32)
            head0, head1 = jnp.where(k == 0, own, got), jnp.where(k == 0, got, own)
            s.attn[rows, :] = jnp.where(low, head0, roll(head1, 64)).astype(BF)
        half = slice(p * 512, p * 512 + 512)
        out = nn(s.attn[half, :], s.wos[...]) + nn(s.hidden[half, :], s.wss[...])
        s.act[4 * p : 4 * p + 4] = out.astype(BF).reshape(4, 128, 1024)
        for n in (4 * p + 3, 4 * p + 2, 4 * p + 1, 4 * p):
            act.start(n)

    def back_to_heads(p):
        dmix = nt(s.gs[4 * p : 4 * p + 4].reshape(512, 1024), s.wos[...])
        for m in (2 * p, 2 * p + 1):
            part = dmix[(m - 2 * p) * 256 : (m - 2 * p) * 256 + 256]
            grads_in.append(deal(((part, roll(part, 64)),), s.pd, s.td, s.pd, m))

    def x_hat_of(m):
        rows = slice(m * 256, m * 256 + 256)
        v = s.xs[2 * m : 2 * m + 2].reshape(256, 1024).astype(F32)
        return (v - s.mus[rows, :]) * s.invs[rows, :]

    def forward_back(p):
        half = slice(p * 512, p * 512 + 512)
        d_hidden = nt(s.gs[4 * p : 4 * p + 4].reshape(512, 1024), s.wss[...])
        s.dexp[half, :] = (d_hidden * s.slope[half, :]).astype(BF)
        d_second = nt(s.dexp[half, :], s.was[:, 384:896])
        for m in (2 * p, 2 * p + 1):
            rows = slice(m * 256, m * 256 + 256)
            part = d_second[(m - 2 * p) * 256 : (m - 2 * p) * 256 + 256]
            s.dhat[2 * m : 2 * m + 2] = (part * g2[...]).astype(BF).reshape(2, 128, 1024)
            s.sm[2:3, :] += down(part * x_hat_of(m))
            s.sm[3:4, :] += down(part)
            s.sm[4:5, :] += down(s.gs[2 * m : 2 * m + 2].reshape(256, 1024).astype(F32))
            s.sm[5:6, 384:896] += down(s.dexp[rows, :].astype(F32))

    grads_in = []
    gt.near()
    back_to_heads(0)
    forward_back(0)
    gt.beside()
    gt.end()
    back_to_heads(1)
    forward_back(1)
    act.along_y()
    act.after_z(3)

    gm = WeightSum(send, me, BF, s.gm_r, s.gm_u, s.gm_ru, s.gm_v, s.gm_rv, s.gm_f, s.gm_rf)
    ga = WeightSum(send, me, BF, s.ga_r, s.ga_u, s.ga_ru, s.ga_v, s.ga_rv, s.ga_f, s.ga_rf)
    s.slope[...] = tn(s.second[...], s.dexp[...])
    s.gsh[...] = tn(s.hidden[...], s.gs[...].reshape(1024, 1024))
    s.go[...] = tn(s.attn[...], s.gs[...].reshape(1024, 1024))
    for kk in range(2):
        for ff in range(8):
            at = [(tt * 2 + kk) * 64 + ff * 8 for tt in range(8)]
            own = slice((kk * 8 + ff) * 32, (kk * 8 + ff) * 32 + 32)
            s.gm[kk, ff, 0:64, :] = jnp.concatenate(
                [s.slope[r : r + 8, :] for r in at], axis=0
            ).astype(BF)
            s.gm[kk, ff, 64:96, :] = s.gsh[own, 0:512].astype(BF)
            s.gm[kk, ff, 96:128, :] = s.gsh[own, 512:1024].astype(BF)
            r = (kk * 8 + ff) * 8
            s.gm[kk, ff, 128:144, :] = jnp.concatenate(
                [s.go[r : r + 8, 0:512], s.go[r : r + 8, 512:1024]], axis=0
            ).astype(BF)
    gm.core(s.gm)

    wait(grads_in)

    for i in range(8):
        quad = [s.pd[inv_slot[4 * i + q]].astype(F32) for q in range(4)]
        s.dt[:, at_tile(i)] = jnp.concatenate(quad, axis=0).T[0:64].astype(BF)
    for i in range(8):
        cols = at_tile(i)
        scaled = (s.dt[:, cols].astype(F32) * s.rsum[i : i + 1, :]).astype(BF).astype(F32)
        inner = jnp.sum(s.mixs[:, cols] * scaled, axis=0, keepdims=True)
        d_i = jnp.concatenate([jnp.zeros_like(scaled), scaled], axis=0).T.astype(BF)
        right = jnp.concatenate([s.qz[cols, :], d_i], axis=0)
        dq = jnp.zeros((64, TILE), F32)
        for j in range(i + 1):
            rows = at_tile(j)
            e_low = s.es[tile(i, j)]
            ds = (e_low.astype(F32) * (nt(s.kv[rows, :], d_i) - inner)).astype(BF)
            both = nn(jnp.concatenate([ds, e_low], axis=1), right)
            s.acc[rows, :] = both if i == j else s.acc[rows, :] + both
            dq += nn(s.kvt[0:64, rows], ds)
        s.mixs[:, cols] = dq * SCALE
        if i == 3:
            gm.along_x()
        if i == 6:
            act.after_y()
            act.after_z(1)
            act.after_z(2)
            act.last_y()
            act.after_z(0)

    def turned_back(v, cols):
        cos, sin = s.cst[0:8, cols], s.cst[8:16, cols]
        f1, f2 = v[0:8], v[8:16]
        return [f1 * cos + f2 * sin, f2 * cos - f1 * sin, v[16:64]]

    for i in range(8):
        cols = at_tile(i)
        tail = s.acc[cols, :]
        both = turned_back(s.mixs[:, cols], cols) + turned_back(tail.T[0:64], cols)
        s.dd[4 * i : 4 * i + 4, :, 0:128] = (
            jnp.concatenate(both, axis=0).T.astype(BF).reshape(4, 64, 128)
        )
        s.dd[4 * i : 4 * i + 4, :, 128:256] = tail.astype(BF).reshape(4, 64, 128)
    for n in range(8):
        for j in range(2):
            s.d_own[2 * n + j] = s.dd[block_of(k, n, j)]
            s.d_away[2 * n + j] = s.dd[block_of(1 - k, n, j)]
    d_sent = send(s.d_away, s.d_got, KC)

    dhat = RowSum(send, s.dhat, *(getattr(s, n) for n, _, _ in row_sum_scratch("dhat", 32)))
    d_sent.wait_recv()
    for m in (3, 1, 2, 0):
        rows = slice(m * 256, m * 256 + 256)
        quads = slice(4 * m, 4 * m + 4)
        tiles = []
        for at in (slice(0, 128), slice(128, 256)):
            own = s.d_own[quads, :, at].reshape(256, 128).astype(F32)
            got = s.d_got[quads, :, at].reshape(256, 128).astype(F32)
            tiles.append((jnp.where(k == 0, own, got), jnp.where(k == 0, got, own)))
        (p_0, p_1), (r_0, r_1) = tiles
        turned = jnp.concatenate(
            [
                jnp.where(low, p_0, roll(p_1, 64)),
                jnp.where(low, roll(p_0, 64), p_1),
                jnp.where(low, roll(r_0, 64), r_1),
            ],
            axis=1,
        )
        turned_low = turned.astype(BF)
        s.dtr[rows, :] = turned_low
        d_first = nt(turned_low, s.was[:, 0:384])
        before = s.dhat[2 * m : 2 * m + 2].reshape(256, 1024).astype(F32)
        s.dhat[2 * m : 2 * m + 2] = (
            (before + d_first * g1[...]).astype(BF).reshape(2, 128, 1024)
        )
        dhat.start(2 * m + 1)
        dhat.start(2 * m)
        s.sm[0:1, :] += down(d_first * x_hat_of(m))
        s.sm[1:2, :] += down(d_first)
        s.sm[5:6, 0:384] += down(turned)

    sm_core = send(s.sm, s.sm_r, KC)
    s.slope[:, 0:384] = tn(s.first[...].reshape(1024, 1024), s.dtr[...])
    for kk in range(2):
        for ff in range(8):
            at = [(tt * 2 + kk) * 64 + ff * 8 for tt in range(8)]
            s.ga[kk, ff] = jnp.concatenate(
                [s.slope[q : q + 8, 0:384] for q in at], axis=0
            ).astype(BF)
    ga.core(s.ga)
    dhat.after_z(3)
    dhat.along_y()
    gm.along_z()
    sm_core.wait_recv()
    s.sm_u[...] = s.sm[...] + s.sm_r[...]
    sm_x = [send(s.sm_u, s.sm_ru.at[j], XS[i]) for j, i in enumerate(NEAR_FIRST)]
    ga.along_x()
    act_v[...] = (s.xs[0].astype(F32) + (ob[...] + sb[...]) + act.end()).astype(BF)
    store(act_v, act_o)
    dhat.after_z(1)
    dhat.after_z(2)
    dhat.last_y()
    dhat.after_y()
    total = gm.total()
    for j in range(8):
        s.gm_f[j] = total[j * 8 : j * 8 + 8, :]
    gsw_v[:, 0:512] = total[64:96, :]
    gsw_v[:, 512:1024] = total[96:128, :]
    gow_v[:, 0:512] = total[128:136, :]
    gow_v[:, 512:1024] = total[136:144, :]
    store(gsw_v, gsw_o)
    store(gow_v, gow_o)
    wait(sm_x)
    s.sm_v[...] = s.sm_u[...] + s.sm_ru[0] + s.sm_ru[1] + s.sm_ru[2]
    sm_zh = send(s.sm_v, s.sm_rv, ZH)
    ga.along_z()
    gm.to_owners()
    dhat.after_z(0)
    sm_zh.wait_recv()
    total = s.sm_v[...] + s.sm_rv[...]
    for j in range(8):
        s.sm_f[j, 0:4, :] = total[0:4, j * 128 : j * 128 + 128]
        s.sm_f[j, 4:5, :] = total[5:6, 0:128]
        s.sm_f[j, 5:6, :] = total[5:6, 128:256]
        s.sm_f[j, 6:7, :] = total[4:5, j * 128 : j * 128 + 128]
        s.sm_f[j, 7:8, :] = total[5:6, 256:384]
    small_v[8:12, :] = jnp.concatenate(
        [total[5:6, 384 + j * 128 : 512 + j * 128] for j in range(4)], axis=0
    )
    small_v[12:16, :] = jnp.zeros((4, 128), F32)
    sm = WeightSum(send, me, F32, None, None, None, None, None, s.sm_f, s.sm_rf)
    sm.to_owners()
    total = ga.total()
    for j in range(8):
        s.ga_f[j] = total[j * 8 : j * 8 + 8, :]
    ga.to_owners()
    d_hat = dhat.end()
    inv = s.invs[0:128, :]
    x_hat = (s.xs[0].astype(F32) - s.mus[0:128, :]) * inv
    tok_v[...] = s.gs[0].astype(F32) + inv * (
        d_hat
        - jnp.mean(d_hat, axis=1, keepdims=True)
        - x_hat * jnp.mean(d_hat * x_hat, axis=1, keepdims=True)
    )
    store(tok_v, tok_o)
    gm.wait()
    for n in range(8):
        gew_v[:, pl.ds(pl.multiple_of(chip_at(n) * 512, 512), 512)] = s.gm_rf[n]
    store(gew_v, gew_o)
    sm.wait()
    total = s.sm_rf[0]
    for n in range(1, 8):
        total += s.sm_rf[n]
    small_v[0:4, :] = total[0:4, :]
    source = lax.rem(2 * t + k, 8)
    bias_rows = jnp.zeros((2, 128), F32)
    for n in range(8):
        bias_rows = jnp.where(chip_at(n) == source, s.sm_rf[n, 4:6, :], bias_rows)
    small_v[4:5, :] = jnp.where(a == 0, bias_rows[0:1], bias_rows[1:2])
    small_v[5:6, :] = s.sm_f[t, 6:7, :]
    small_v[6:7, :] = s.sm_f[t, 7:8, :]
    small_v[7:8, :] = jnp.zeros((1, 128), F32)
    store(small_v, small_o)
    ga.wait()
    for n in range(8):
        for o in range(3):
            at = pl.ds(pl.multiple_of(o * 1024 + chip_at(n) * 128, 128), 128)
            gtw_v[:, at] = s.ga_rf[n, :, o * 128 : o * 128 + 128]
    store(gtw_v, gtw_o)
    for copy in stored:
        copy.wait()
    send.finish()


RESULTS = (
    ((128, 1024), BF),
    ((128, 1024), F32),
    ((8, 3072), F32),
    ((8, 4096), F32),
    ((8, 1024), F32),
    ((32, 1024), F32),
    ((16, 128), F32),
)


def block(pairs, pos, x, g, tw, ow, ew, sw, tb, eb, g1, b1, g2, b2, ob, sb):
    return pl.pallas_call(
        block_kernel,
        out_shape=tuple(jax.ShapeDtypeStruct(*result) for result in RESULTS),
        in_specs=[pl.BlockSpec(memory_space=pltpu.SMEM), VM] + [ANY] * 6 + [VM] * 8,
        out_specs=(ANY,) * 7,
        scratch_shapes=[pltpu.VMEM(shape, kind) for _, shape, kind in SCRATCH]
        + [
            pltpu.SemaphoreType.DMA((COPIES,)),
            pltpu.SemaphoreType.DMA((COPIES,)),
            pltpu.SemaphoreType.DMA((LOADS,)),
            pltpu.SMEM((32,), jnp.int32),
            pltpu.SemaphoreType.DMA((7,)),
        ]
        + [pltpu.VMEM(*result) for result in RESULTS],
        compiler_params=pltpu.CompilerParams(
            collective_id=0, has_side_effects=True, vmem_limit_bytes=62 * MIB
        ),
        name="block",
    )(pairs, pos, x, g, tw, ow, ew, sw, tb, eb, g1, b1, g2, b2, ob, sb)


def results_kernel(
    act, tok, gtw, gew, gow, gsw, small,
    act_o, tok_o, gtw_o, gew_o, gow_o, gsw_o,
    fg_o, fb_o, sg_o, sb_o, tb_o, vb_o, ob_o, eb_o, hb_o,
):
    for src, dst in (
        (act, act_o), (tok, tok_o), (gtw, gtw_o), (gew, gew_o), (gow, gow_o), (gsw, gsw_o)
    ):
        dst[...] = src[...]
    k, f = lax.rem(lax.axis_index("ctx"), 2), lax.axis_index("fsdp")
    rows = small[0:8, :]
    eights = pltpu.roll(rows, lax.rem(128 - (k * 64 + f * 8), 128), 1)
    for j, dst in enumerate((fg_o, fb_o, sg_o, sb_o)):
        dst[...] = eights[j : j + 1, 0:8]
    vb_o[...] = eights[6:7, 0:8]
    ob_o[...] = eights[5:6, 0:8]
    hb_o[...] = eights[5:6, 0:8]
    tb_o[...] = pltpu.roll(rows, lax.rem(128 - f * 16, 128), 1)[4:5, 0:16]
    wide = small[pl.ds(8 + k * 2 + lax.div(f, 4), 1), :]
    wide = jnp.broadcast_to(wide, (8, 128))
    eb_o[...] = pltpu.roll(wide, lax.rem(128 - lax.rem(f, 4) * 32, 128), 1)[0:1, 0:32]


def results(*arrays):
    vectors = (8, 8, 8, 8, 16, 8, 8, 32, 8)
    return pl.pallas_call(
        results_kernel,
        out_shape=tuple(jax.ShapeDtypeStruct(v.shape, v.dtype) for v in arrays[:6])
        + tuple(jax.ShapeDtypeStruct((1, n), F32) for n in vectors),
        compiler_params=pltpu.CompilerParams(vmem_limit_bytes=62 * MIB),
        name="results",
    )(*arrays)


def shards(
    tokens_in,
    positions,
    block_pairs,
    first_gain,
    first_bias,
    second_gain,
    second_bias,
    triple_weight,
    triple_bias,
    output_weight,
    output_bias,
    expand_weight,
    expand_bias,
    shrink_weight,
    shrink_bias,
    cotangent,
):
    x, g = tokens_in.reshape(128, 1024), cotangent.reshape(128, 1024)

    def line(v):
        return v.reshape(1, -1)

    found = block(
        block_pairs.T,
        positions,
        x,
        g,
        triple_weight,
        output_weight,
        expand_weight,
        shrink_weight,
        line(triple_bias),
        line(expand_bias),
        line(first_gain),
        line(first_bias),
        line(second_gain),
        line(second_bias),
        line(output_bias),
        line(shrink_bias),
    )
    act, tok, gtw, gew, gow, gsw, fg, fb, sg, sb, tb, vb, ob, eb, hb = results(*found)
    return (
        act.reshape(tokens_in.shape),
        tok.reshape(tokens_in.shape),
        fg.reshape(8),
        fb.reshape(8),
        sg.reshape(8),
        sb.reshape(8),
        gtw,
        tb.reshape(16),
        vb.reshape(8),
        gow,
        ob.reshape(8),
        gew,
        eb.reshape(32),
        gsw,
        hb.reshape(8),
    )


def solution(mesh):
    return jax.shard_map(
        shards,
        mesh=mesh,
        in_specs=(
            P("fsdp", "ctx", None, None, None),
            P("fsdp", None),
            P(),
            P(),
            P(),
            P(),
            P(),
            P("fsdp", None),
            P(),
            P(None, "fsdp"),
            P(),
            P("fsdp", None),
            P(),
            P(None, "fsdp"),
            P(),
            P("fsdp", "ctx", None, None, None),
        ),
        out_specs=(
            P("fsdp", "ctx", None, None, None),
            P("fsdp", "ctx", None, None, None),
            P(("ctx", "fsdp")),
            P(("ctx", "fsdp")),
            P(("ctx", "fsdp")),
            P(("ctx", "fsdp")),
            P(("ctx", "fsdp"), None),
            P(("ctx", "fsdp")),
            P(("ctx", "fsdp")),
            P(("ctx", "fsdp"), None),
            P(("ctx", "fsdp")),
            P(("ctx", "fsdp"), None),
            P(("ctx", "fsdp")),
            P(("ctx", "fsdp"), None),
            P(("ctx", "fsdp")),
        ),
        check_vma=False,
    )
```
